32 devices in a mesh: src: 4 (over z), tgt: 8 (over y, x, core).
Axes of the slice: x: 2, y: 2, z: 4, core: 2. Of those that a mesh axis runs over, the one named last changes fastest.
Arguments:
- src_points: bfloat16 [32, 256, 128], P('src', 'tgt')
- tgt_points: bfloat16 [64, 256, 128], P('tgt', 'src'), may hold values from -1.5 to 1.5
- src_mass: bfloat16 [32, 256], P('src', 'tgt'), may hold values from 0.099609375 to 10
- tgt_mass: bfloat16 [64, 256], P('tgt', 'src'), may hold values from 0.099609375 to 10
- src_potential: bfloat16 [32, 256], P('src', 'tgt'), may hold values from -452 to 452
- tgt_potential: bfloat16 [64, 256], P('tgt', 'src'), may hold values from -452 to 452
- src_counts: int32 [32], P('src'), may hold values from 16 to 256, as said below
- tgt_counts: int32 [64], P('tgt'), may hold values from 16 to 256, as said below
- keep: int32 [32, 64], P('src', 'tgt'), may hold values from 0 to 1, as said below
Outputs:
- images: float32 [32, 256, 128], P('src', 'tgt')
- src_final: float32 [32, 256], P('src', 'tgt')
- tgt_final: float32 [64, 256], P('tgt', 'src')
The draws below stay inside these ranges and needn't reach their ends.
Inputs may be any that keep to these rules, and one draw needn't show every extreme that they name: `keep`: every source block keeps at least one target block and every target block is kept by at least one source block. `src_counts`: some source block is full. `tgt_counts`: some target block is full.
All inputs are finite; a program needn't handle non-finite values.
Results may differ from the reference program's by a relative error of at most 0.0003.
Values may be sent and summed in bfloat16 or wider, within the bound.
No kernel may reach another device: no remote copies, remote signals or barrier semaphores. Data moves between devices by JAX's collectives and lax.ppermute only.
A program may use at most 64 MiB of HBM per device.

```python
import math
import jax
import jax.numpy as jnp
from jax import lax

W = 128
BLOCK = 256
ITERS = 4
NSB = 32
NTB = 64


def draw_src_points(key, part):
    values = 0.25 * jax.random.normal(key, (NSB, BLOCK, W), jnp.float32)
    return values.astype(jnp.bfloat16)


def coarse_potential(key, rows):
    rough = jnp.clip(jax.random.normal(jax.random.fold_in(key, 22), (rows, BLOCK), jnp.float32), -2.0, 2.0)
    offset = jnp.clip(150.0 * jax.random.normal(jax.random.fold_in(key, 21), (rows, BLOCK), jnp.float32), -450.0, 450.0)
    return (offset + rough).astype(jnp.bfloat16)


def draw_src_potential(key, part):
    return coarse_potential(jax.random.fold_in(key, 31), NSB)


def draw_tgt_potential(key, part):
    return coarse_potential(jax.random.fold_in(key, 37), NTB)


def live_counts(key, total):
    lowest = max(1, BLOCK // 16)
    values = jax.random.randint(key, (total,), lowest, BLOCK + 1)
    order = jax.random.permutation(jax.random.fold_in(key, 7), total)
    values = values.at[order[0]].set(BLOCK)
    values = values.at[order[1]].set(lowest)
    return values.astype(jnp.int32)


def draw_src_counts(key, part):
    return live_counts(jax.random.fold_in(key, 11), NSB)


def draw_tgt_counts(key, part):
    return live_counts(jax.random.fold_in(key, 13), NTB)


def draw_keep(key, part):
    rates = jax.random.randint(jax.random.fold_in(key, 1), (NSB, 1), 1, 9)
    rolls = jax.random.randint(jax.random.fold_in(key, 2), (NSB, NTB), 0, 24)
    shift_a = jax.random.randint(jax.random.fold_in(key, 3), (), 0, NTB)
    shift_b = jax.random.randint(jax.random.fold_in(key, 4), (), 0, NSB)
    rows = jnp.arange(NSB, dtype=jnp.int32)[:, None]
    cols = jnp.arange(NTB, dtype=jnp.int32)[None, :]
    cover_a = cols == (rows * NTB // NSB + shift_a) % NTB
    cover_b = rows == (cols * NSB // NTB + shift_b) % NSB
    return ((rolls < rates) | cover_a | cover_b).astype(jnp.int32)


def levels(rng, extent, pieces, smallest, largest):
    loudness = 1.0
    for position, shards_of in pieces:
        heights = jax.random.uniform(jax.random.fold_in(jax.random.fold_in(rng, 6), position), (shards_of,), jnp.float32, smallest / len(pieces), largest / len(pieces))
        loudness = loudness * jnp.repeat(jnp.exp(heights), extent[position] // shards_of).reshape((-1,) + (1,) * (len(extent) - 1 - position))
    return loudness


def centred(own_key, shape, scale, most, split=(), kind=jnp.bfloat16):
    array = scale * jax.random.normal(own_key, shape, jnp.float32)
    if split:
        array = array * levels(own_key, shape, split, -0.22, 0.18)
    return jnp.clip(array, -most, most).astype(kind)


def setup_inputs(seed: int = 0) -> dict:
    keys = jax.random.split(jax.random.key(seed), 10)
    src_points = draw_src_points(jax.random.fold_in(keys[9], 71), 0)
    tgt_points = centred(keys[1], (NTB, BLOCK, W), 0.25, 1.5, ((0, 8), (1, 4)))
    src_mass = jnp.clip(jnp.exp(math.log(10.0) - 4.609084 * jax.random.uniform(keys[2], (NSB, BLOCK), jnp.float32) ** levels(keys[2], (NSB, BLOCK), ((0, 4), (1, 8)), -0.2, 0.2)), 0.099609375, 10.0).astype(jnp.bfloat16)
    tgt_mass = jnp.clip(jnp.exp(math.log(10.0) - 4.609084 * jax.random.uniform(keys[3], (NTB, BLOCK), jnp.float32) ** levels(keys[3], (NTB, BLOCK), ((0, 8), (1, 4)), -0.2, 0.2)), 0.099609375, 10.0).astype(jnp.bfloat16)
    src_potential = draw_src_potential(jax.random.fold_in(keys[9], 71), 0)
    tgt_potential = draw_tgt_potential(jax.random.fold_in(keys[9], 71), 0)
    src_counts = draw_src_counts(jax.random.fold_in(keys[9], 71), 0)
    tgt_counts = draw_tgt_counts(jax.random.fold_in(keys[9], 71), 0)
    keep = draw_keep(jax.random.fold_in(keys[9], 71), 0)
    return {"src_points": src_points, "tgt_points": tgt_points, "src_mass": src_mass, "tgt_mass": tgt_mass, "src_potential": src_potential, "tgt_potential": tgt_potential, "src_counts": src_counts, "tgt_counts": tgt_counts, "keep": keep}


EPSILON = 0.1
FLOOR = -1.0e30


def reference(src_points, tgt_points, src_mass, tgt_mass, src_potential, tgt_potential, src_counts, tgt_counts, keep):
    nsb, blk, width = src_points.shape
    ntb = tgt_points.shape[0]
    xs = src_points.astype(jnp.float32)
    ys = tgt_points.astype(jnp.float32).reshape(ntb * blk, width)
    y_half = 0.5 * jnp.sum(ys * ys, axis=1)
    slots = jnp.arange(blk, dtype=jnp.int32)
    src_live = slots[None, :] < src_counts[:, None]
    tgt_live = (slots[None, :] < tgt_counts[:, None]).reshape(-1)
    log_a = jnp.log(src_mass.astype(jnp.float32))
    log_b = jnp.log(tgt_mass.astype(jnp.float32)).reshape(-1)
    kept = jnp.repeat(keep > 0, blk, axis=1)

    def tile(x):
        x_half = 0.5 * jnp.sum(x * x, axis=1)
        return x_half[:, None] + y_half[None, :] - jnp.dot(x, ys.T, precision=lax.Precision.HIGHEST)

    def sweep(f_now, g_now):
        def visit(carry, item):
            colmax, colsum = carry
            x, live, lga, fpart, pair = item
            cost = tile(x)
            row_ok = pair[None, :] & tgt_live[None, :]
            col_ok = pair[None, :] & live[:, None]
            scored = jnp.where(row_ok, log_b[None, :] + (g_now[None, :] - cost) / EPSILON, FLOOR)
            rmax = jnp.max(scored, axis=1)
            rsum = jnp.sum(jnp.where(row_ok, jnp.exp(scored - rmax[:, None]), 0.0), axis=1)
            colterm = jnp.where(col_ok, lga[:, None] + (fpart[:, None] - cost) / EPSILON, FLOOR)
            peak = jnp.maximum(colmax, jnp.max(colterm, axis=0))
            colsum = colsum * jnp.exp(colmax - peak) + jnp.sum(jnp.where(col_ok, jnp.exp(colterm - peak[None, :]), 0.0), axis=0)
            return (peak, colsum), -EPSILON * (rmax + jnp.log(rsum))

        start = (jnp.full((ntb * blk,), FLOOR, jnp.float32), jnp.zeros((ntb * blk,), jnp.float32))
        (colmax, colsum), f_new = lax.scan(visit, start, (xs, src_live, log_a, f_now, kept))
        return f_new, -EPSILON * (colmax + jnp.log(colsum))

    f_cur = src_potential.astype(jnp.float32)
    g_cur = tgt_potential.astype(jnp.float32).reshape(-1)
    for step in range(ITERS):
        f_new, g_new = sweep(f_cur, g_cur)
        f_cur = 0.5 * (f_cur + f_new)
        g_cur = 0.5 * (g_cur + g_new)

    def project(carry, item):
        x, pair = item
        cost = tile(x)
        row_ok = pair[None, :] & tgt_live[None, :]
        scored = jnp.where(row_ok, log_b[None, :] + (g_cur[None, :] - cost) / EPSILON, FLOOR)
        rmax = jnp.max(scored, axis=1)
        weights = jnp.where(row_ok, jnp.exp(scored - rmax[:, None]), 0.0)
        total = jnp.sum(weights, axis=1)
        moved = jnp.dot(weights, ys, precision=lax.Precision.HIGHEST) / total[:, None]
        return carry, moved

    unused, images = lax.scan(project, jnp.zeros((), jnp.float32), (xs, kept))
    return images, f_cur, g_cur.reshape(ntb, blk)
```

```python
import functools
import math

import jax
import jax.numpy as jnp
from jax import lax
from jax.experimental import pallas as pl
from jax.experimental.pallas import tpu as pltpu
from jax.sharding import PartitionSpec as P

ITERS = 4
EPSILON = 0.1
UNIT = 1.0 / (EPSILON * math.log(2.0))
FLOOR = -1e30


def whole_block(ref, k):
    piece = ref[:, k]
    return piece.reshape(piece.shape[0] * piece.shape[1], piece.shape[2])


def spread_columns(vec, col_ref):
    turned = vec.T
    for k in range(vec.shape[0]):
        col_ref[k] = jnp.broadcast_to(turned[:, k : k + 1], col_ref.shape[1:])


def reduce_pass(lane_ref, lane_blocks, stream_ref, stream_blocks, col_ref, kept, peak_ref, sum_ref):
    peak_ref[...] = jnp.full(peak_ref.shape, FLOOR, jnp.float32)
    sum_ref[...] = jnp.zeros(sum_ref.shape, jnp.float32)

    @pl.loop(0, lane_blocks)
    def _(p):
        @pl.loop(0, stream_blocks)
        def _(q):
            @pl.when(kept(p, q))
            def _():
                dots = lax.dot_general(
                    whole_block(stream_ref, q),
                    whole_block(lane_ref, p),
                    (((1,), (1,)), ((), ())),
                    preferred_element_type=jnp.float32,
                )
                n, lanes = dots.shape
                col = col_ref[q]
                col = jnp.concatenate([col] * (lanes // 128), axis=1)
                score = (dots * UNIT + col).reshape(n // 8, 8, lanes)
                old = peak_ref[p]
                new = jnp.maximum(old, jnp.max(score, axis=0))
                sum_ref[p] = sum_ref[p] * jnp.exp2(old - new) + jnp.sum(jnp.exp2(score - new[None]), axis=0)
                peak_ref[p] = new

    peak = peak_ref[...]
    top = jnp.max(peak, axis=1, keepdims=True)
    total = jnp.sum(sum_ref[...] * jnp.exp2(peak - top), axis=1)
    return top[:, 0] + jnp.log2(total)


def sweep_kernel(keep_ref, x_ref, y_ref, u_ref, h_ref, rows_ref, cols_ref, col_ref, peak_ref, sum_ref):
    sb, tb = x_ref.shape[1], y_ref.shape[1]
    spread_columns(h_ref[...], col_ref)
    rows_ref[...] = reduce_pass(
        x_ref, sb, y_ref, tb, col_ref, lambda p, q: keep_ref[p, q] > 0, peak_ref, sum_ref
    )
    spread_columns(u_ref[...], col_ref)
    cols_ref[...] = reduce_pass(
        y_ref, tb, x_ref, sb, col_ref, lambda q, p: keep_ref[p, q] > 0, peak_ref, sum_ref
    )


def project_kernel(keep_ref, x_ref, y_ref, h_ref, image_ref, lse_ref, acc_ref, peak_ref):
    sb, tb = x_ref.shape[1], y_ref.shape[1]
    width = x_ref.shape[3]

    @pl.loop(0, sb)
    def _(p):
        acc_ref[...] = jnp.zeros(acc_ref.shape, jnp.float32)
        peak_ref[...] = jnp.full(peak_ref.shape, FLOOR, jnp.float32)

        @pl.loop(0, tb)
        def _(q):
            @pl.when(keep_ref[p, q] > 0)
            def _():
                ys = whole_block(y_ref, q)
                dots = lax.dot_general(
                    whole_block(x_ref, p), ys, (((1,), (1,)), ((), ())), preferred_element_type=jnp.float32
                )
                score = dots * UNIT + h_ref[pl.ds(q, 1), :]
                old = peak_ref[...]
                new = jnp.maximum(old, jnp.max(score, axis=1, keepdims=True))
                weights = jnp.exp2(score - new[:, :1])
                high = weights.astype(jnp.bfloat16)
                low = (weights - high.astype(jnp.float32)).astype(jnp.bfloat16)
                full = jnp.concatenate([ys, jnp.ones(ys.shape, ys.dtype)], axis=1)
                moved = jnp.dot(high, full, preferred_element_type=jnp.float32) + jnp.dot(
                    low, full, preferred_element_type=jnp.float32
                )
                acc_ref[...] = acc_ref[...] * jnp.exp2(old - new)[:, :1] + moved
                peak_ref[...] = new

        total = acc_ref[:, width:]
        safe = jnp.where(total > 0.0, total, 1.0)
        image_ref[p] = acc_ref[:, :width] / safe
        lse = peak_ref[...] + jnp.log2(safe)
        lse_ref[pl.ds(p, 1), :] = lse.T[:1]


def merge_lse(parts):
    top = functools.reduce(jnp.maximum, parts)
    return top + jnp.log2(sum(jnp.exp2(part - top) for part in parts))


def all_lse(part, axis):
    got = lax.all_gather(part, axis)
    return merge_lse([got[k] for k in range(got.shape[0])])


def on_device(
    src_points, tgt_points, src_mass, tgt_mass, src_potential, tgt_potential, src_counts, tgt_counts, keep
):
    ntgt = lax.axis_size("tgt")
    nsrc = lax.axis_size("src")
    sb, src_piece, width = src_points.shape
    tb, tgt_piece, _ = tgt_points.shape
    blk = src_piece * ntgt

    x = lax.all_gather(src_points, "tgt")
    y = lax.all_gather(tgt_points, "src")

    def vectors(mass, potential, points, counts, axis):
        pair = lax.all_gather(jnp.stack([mass, potential]), axis).astype(jnp.float32)
        pair = jnp.transpose(pair, (1, 2, 0, 3)).reshape(2, mass.shape[0], blk)
        wide = points.astype(jnp.float32)
        half = jnp.transpose((0.5 * UNIT) * jnp.sum(wide * wide, axis=3), (1, 0, 2)).reshape(mass.shape[0], blk)
        live = jnp.arange(blk, dtype=jnp.int32)[None, :] < counts[:, None]
        return pair[1] * UNIT, half, jnp.log2(pair[0]) - half, live

    f, x_half, x_base, src_live = vectors(src_mass, src_potential, x, src_counts, "tgt")
    g, y_half, y_base, tgt_live = vectors(tgt_mass, tgt_potential, y, tgt_counts, "src")

    smem = pl.BlockSpec(memory_space=pltpu.SMEM)
    vmem = pl.BlockSpec(memory_space=pltpu.VMEM)
    most = max(sb, tb)
    params = pltpu.CompilerParams(vmem_limit_bytes=40 * 1024 * 1024)
    sweep = pl.pallas_call(
        sweep_kernel,
        out_shape=(jax.ShapeDtypeStruct((sb, blk), jnp.float32), jax.ShapeDtypeStruct((tb, blk), jnp.float32)),
        in_specs=[smem] + [vmem] * 4,
        out_specs=(vmem, vmem),
        scratch_shapes=[
            pltpu.VMEM((most, blk, 128), jnp.float32),
            pltpu.VMEM((most, 8, blk), jnp.float32),
            pltpu.VMEM((most, 8, blk), jnp.float32),
        ],
        compiler_params=params,
        name="sweep",
    )
    project = pl.pallas_call(
        project_kernel,
        out_shape=(
            jax.ShapeDtypeStruct((sb, blk, width), jnp.float32),
            jax.ShapeDtypeStruct((sb, blk), jnp.float32),
        ),
        in_specs=[smem] + [vmem] * 3,
        out_specs=(vmem, vmem),
        scratch_shapes=[pltpu.VMEM((blk, 2 * width), jnp.float32), pltpu.VMEM((blk, 128), jnp.float32)],
        compiler_params=params,
        name="project",
    )

    for step in range(ITERS):
        u = jnp.where(src_live, f + x_base, FLOOR)
        h = jnp.where(tgt_live, g + y_base, FLOOR)
        rows, cols = sweep(keep, x, y, u, h)
        rows = all_lse(rows, "tgt")
        cols = all_lse(cols, "src")
        f = 0.5 * (f + (x_half - rows))
        g = 0.5 * (g + (y_half - cols))

    h = jnp.where(tgt_live, g + y_base, FLOOR)
    image, lse = project(keep, x, y, h)
    whole = all_lse(lse, "tgt")
    image = image * jnp.exp2(lse - whole)[:, :, None]
    pieces = lax.all_to_all(image.reshape(sb, ntgt, src_piece, width), "tgt", 1, 0)
    images = jnp.sum(pieces, axis=0)
    src_start = lax.axis_index("tgt") * src_piece
    tgt_start = lax.axis_index("src") * tgt_piece
    src_final = lax.dynamic_slice_in_dim(f * (1.0 / UNIT), src_start, src_piece, 1)
    tgt_final = lax.dynamic_slice_in_dim(g * (1.0 / UNIT), tgt_start, tgt_piece, 1)
    return images, src_final, tgt_final


def solution(mesh):
    return jax.shard_map(
        on_device,
        mesh=mesh,
        in_specs=(
            P("src", "tgt", None),
            P("tgt", "src", None),
            P("src", "tgt"),
            P("tgt", "src"),
            P("src", "tgt"),
            P("tgt", "src"),
            P("src"),
            P("tgt"),
            P("src", "tgt"),
        ),
        out_specs=(P("src", "tgt", None), P("src", "tgt"), P("tgt", "src")),
        check_vma=False,
    )
```

```python
import functools
import math

import jax
import jax.numpy as jnp
from jax import lax
from jax.experimental import pallas as pl
from jax.experimental.pallas import tpu as pltpu
from jax.sharding import PartitionSpec as P

ITERS = 4
EPSILON = 0.1
UNIT = 1.0 / (EPSILON * math.log(2.0))
FLOOR = -1e30
LANES = 128
GROUP = 4

SMEM = pl.BlockSpec(memory_space=pltpu.SMEM)
VMEM = pl.BlockSpec(memory_space=pltpu.VMEM)
PARAMS = pltpu.CompilerParams(vmem_limit_bytes=40 * 1024 * 1024)


def f32(*shape):
    return jax.ShapeDtypeStruct(shape, jnp.float32)


def swap(part, axis, mask):
    return lax.ppermute(part, axis, [(i, i ^ mask) for i in range(lax.axis_size(axis))])


def near_count(axis):
    return lax.axis_size(axis) // 4


def merge_lse(parts):
    top = functools.reduce(jnp.maximum, parts)
    return top + jnp.log2(sum(jnp.exp2(part - top) for part in parts))


def exchange_lse(part, axis):
    near = near_count(axis)
    if near > 1:
        part = merge_lse([part] + [swap(part, axis, d) for d in range(1, near)])
    return [part] + [swap(part, axis, near * k) for k in range(1, 4)]


def gather_pieces(piece, axis):
    near = near_count(axis)
    four = jnp.stack([piece] + [swap(piece, axis, near * k) for k in range(1, 4)])
    return [four] + [swap(four, axis, d) for d in range(1, near)]


def whole_block(ref, k):
    piece = ref[:, k]
    return piece.reshape(piece.shape[0] * piece.shape[1], piece.shape[2])


def spread_columns(vec, col_ref):
    turned = vec.T
    for k in range(vec.shape[0]):
        col_ref[k] = jnp.broadcast_to(turned[:, k : k + 1], col_ref.shape[1:])


def pair_dots(lhs_ref, p, rhs_ref, q):
    return lax.dot_general(
        whole_block(lhs_ref, p),
        whole_block(rhs_ref, q),
        (((1,), (1,)), ((), ())),
        preferred_element_type=jnp.float32,
    )


def column_lse(dots, col):
    score = dots * UNIT + jnp.concatenate([col] * (dots.shape[1] // LANES), axis=1)
    peak = jnp.max(score, axis=0, keepdims=True)
    return peak, jnp.sum(jnp.exp2(score - peak), axis=0, keepdims=True)


def clear(peak_ref, sum_ref):
    peak_ref[...] = jnp.full(peak_ref.shape, FLOOR, jnp.float32)
    sum_ref[...] = jnp.zeros(sum_ref.shape, jnp.float32)


def merge_slots(peak_ref, sum_ref, count):
    shape = (count, peak_ref.shape[0] // count, peak_ref.shape[1])
    peak = peak_ref[...].reshape(shape)
    top = jnp.max(peak, axis=1, keepdims=True)
    total = jnp.sum(sum_ref[...].reshape(shape) * jnp.exp2(peak - top), axis=1)
    return top[:, 0] + jnp.log2(jnp.maximum(total, 1.0))


def visit_pairs(count_ref, list_ref, tb, work):
    @pl.loop(0, pl.cdiv(count_ref[0], GROUP))
    def _(step):
        codes = [list_ref[step * GROUP + k] for k in range(GROUP)]
        work([(code // tb, lax.rem(code, tb)) for code in codes])


def sweep(count_ref, list_ref, x_ref, y_ref, u, h, rows_ref, cols_ref, scratch):
    ucol_ref, hcol_ref, rpeak_ref, rsum_ref, cpeak_ref, csum_ref = scratch
    sb, tb = x_ref.shape[1], y_ref.shape[1]
    spread_columns(u, ucol_ref)
    spread_columns(h, hcol_ref)
    clear(rpeak_ref, rsum_ref)
    clear(cpeak_ref, csum_ref)

    def work(pairs):
        found = []
        for p, q in pairs:
            row = column_lse(pair_dots(y_ref, q, x_ref, p), hcol_ref[q])
            col = column_lse(pair_dots(x_ref, p, y_ref, q), ucol_ref[p])
            found.append((p, q, row, col))
        for p, q, row, col in found:
            rpeak_ref[pl.ds(p * tb + q, 1), :], rsum_ref[pl.ds(p * tb + q, 1), :] = row
            cpeak_ref[pl.ds(q * sb + p, 1), :], csum_ref[pl.ds(q * sb + p, 1), :] = col

    visit_pairs(count_ref, list_ref, tb, work)
    rows_ref[...] = merge_slots(rpeak_ref, rsum_ref, sb)
    cols_ref[...] = merge_slots(cpeak_ref, csum_ref, tb)


def sweep_scratch(sb, tb, blk):
    return [
        pltpu.VMEM((sb, blk, LANES), jnp.float32),
        pltpu.VMEM((tb, blk, LANES), jnp.float32),
        pltpu.VMEM((sb * tb, blk), jnp.float32),
        pltpu.VMEM((sb * tb, blk), jnp.float32),
        pltpu.VMEM((sb * tb, blk), jnp.float32),
        pltpu.VMEM((sb * tb, blk), jnp.float32),
    ]


def list_kernel(keep_ref, count_ref, list_ref):
    sb, tb = keep_ref.shape

    def add(code, state):
        n, last = state
        kept = keep_ref[code // tb, lax.rem(code, tb)] > 0
        list_ref[n] = code
        return n + kept.astype(jnp.int32), jnp.where(kept, code, last)

    n, last = lax.fori_loop(0, sb * tb, add, (jnp.int32(0), jnp.int32(0)))
    for k in range(GROUP):
        list_ref[n + k] = last
    count_ref[0] = n


def assemble(place, counts_ref, four_refs, points_ref, vec_ref):
    n, blocks, piece, width = points_ref.shape
    blk = n * piece
    vec_ref[...] = jnp.zeros(vec_ref.shape, jnp.float32)
    for d, four_ref in enumerate(four_refs):
        for k in range(4):
            owner = jnp.bitwise_xor(place, len(four_refs) * k + d)
            points_ref[owner] = four_ref[k, : blocks * piece].reshape(blocks, piece, width)
            tile = owner * piece // LANES
            for v in range(2):
                start = blocks * piece + v * blocks
                vec_ref[v, tile] += four_ref[k, start : start + blocks].astype(jnp.float32)
    mass = jnp.concatenate([vec_ref[0, t] for t in range(blk // LANES)], axis=1)
    potential = jnp.concatenate([vec_ref[1, t] for t in range(blk // LANES)], axis=1) * UNIT
    block_of = lax.broadcasted_iota(jnp.int32, (blocks, blk), 0)
    slot_of = lax.broadcasted_iota(jnp.int32, (blocks, blk), 1)
    half = jnp.zeros((blocks, blk), jnp.float32)
    count = jnp.zeros((blocks, blk), jnp.int32)
    ones = jnp.ones((blocks, width), jnp.bfloat16)
    for k in range(blocks):
        wide = whole_block(points_ref, k).astype(jnp.float32)
        square = wide * wide
        high = square.astype(jnp.bfloat16)
        low = (square - high.astype(jnp.float32)).astype(jnp.bfloat16)
        norm = sum(
            lax.dot_general(ones, part, (((1,), (1,)), ((), ())), preferred_element_type=jnp.float32)
            for part in (high, low)
        )
        half = jnp.where(block_of == k, norm * (0.5 * UNIT), half)
        count = jnp.where(block_of == k, counts_ref[k], count)
    base = jnp.where(slot_of < count, jnp.log2(mass) - half, FLOOR)
    return potential, half, base


def first_kernel(nx, ny, place_ref, src_counts_ref, tgt_counts_ref, count_ref, list_ref, *refs):
    x_fours, y_fours, refs = refs[:nx], refs[nx : nx + ny], refs[nx + ny :]
    x_ref, y_ref, fixed_ref, f_ref, g_ref, rows_ref, cols_ref, xvec_ref, yvec_ref = refs[:9]
    f, x_half, x_base = assemble(place_ref[1], src_counts_ref, x_fours, x_ref, xvec_ref)
    g, y_half, y_base = assemble(place_ref[0], tgt_counts_ref, y_fours, y_ref, yvec_ref)
    f_ref[...] = f
    g_ref[...] = g
    for k, vec in enumerate((x_half, x_base, y_half, y_base)):
        fixed_ref[k] = vec
    sweep(count_ref, list_ref, x_ref, y_ref, f + x_base, g + y_base, rows_ref, cols_ref, refs[9:])


def updated(old, half, part_refs):
    return 0.5 * (old + (half - merge_lse([ref[...] for ref in part_refs])))


def step_kernel(count_ref, list_ref, x_ref, y_ref, fixed_ref, f_in_ref, g_in_ref, *refs):
    row_refs, col_refs, refs = refs[:4], refs[4:8], refs[8:]
    f_ref, g_ref, rows_ref, cols_ref = refs[:4]
    f = updated(f_in_ref[...], fixed_ref[0], row_refs)
    g = updated(g_in_ref[...], fixed_ref[2], col_refs)
    f_ref[...] = f
    g_ref[...] = g
    sweep(count_ref, list_ref, x_ref, y_ref, f + fixed_ref[1], g + fixed_ref[3], rows_ref, cols_ref, refs[4:])


def project_kernel(near, place_ref, count_ref, list_ref, x_ref, y_ref, fixed_ref, g_in_ref, *refs):
    col_refs, g_ref, out_refs = refs[:4], refs[4], refs[5 : 5 + near]
    h_ref, col_ref, peak_ref, sum_ref, acc_ref = refs[5 + near :]
    n, sb, piece, width = x_ref.shape
    tb = y_ref.shape[1]
    blk = n * piece
    g = updated(g_in_ref[...], fixed_ref[2], col_refs)
    g_ref[...] = g
    h = g + fixed_ref[3]
    h_ref[...] = h
    spread_columns(h, col_ref)
    clear(peak_ref, sum_ref)

    def measure(pairs):
        found = [(p * tb + q, column_lse(pair_dots(y_ref, q, x_ref, p), col_ref[q])) for p, q in pairs]
        for slot, row in found:
            peak_ref[pl.ds(slot, 1), :], sum_ref[pl.ds(slot, 1), :] = row

    visit_pairs(count_ref, list_ref, tb, measure)
    lse = merge_slots(peak_ref, sum_ref, sb)
    spread_columns(lse, col_ref)
    acc_ref[...] = jnp.zeros(acc_ref.shape, jnp.float32)

    def move(pairs):
        moves = []
        for p, q in pairs:
            ys = whole_block(y_ref, q)
            col = jnp.concatenate([col_ref[p]] * (blk // LANES), axis=1)
            weights = jnp.exp2(pair_dots(x_ref, p, y_ref, q) * UNIT + (h_ref[pl.ds(q, 1), :] - col))
            high = weights.astype(jnp.bfloat16)
            low = (weights - high.astype(jnp.float32)).astype(jnp.bfloat16)
            full = jnp.concatenate([ys, jnp.ones(ys.shape, ys.dtype)], axis=1)
            moves.append(
                jnp.dot(high, full, preferred_element_type=jnp.float32)
                + jnp.dot(low, full, preferred_element_type=jnp.float32)
            )
        return moves

    def move_all(pairs):
        for (p, _), moved in zip(pairs, move(pairs)):
            acc_ref[p] += moved

    @pl.loop(0, count_ref[0])
    def _(k):
        code = list_ref[k]
        move_all([(code // tb, lax.rem(code, tb))])

    me = lax.rem(place_ref[1], near)
    for p in range(sb):
        total = acc_ref[p, :, width:]
        image = acc_ref[p, :, :width] / jnp.where(total > 0.0, total, 1.0)
        acc_ref[p, :, :width] = image
    for e, out_ref in enumerate(out_refs):
        for far in range(4):
            owner = far * near + jnp.bitwise_xor(me, e)
            for p in range(sb):
                out_ref[far, p * piece : (p + 1) * piece] = acc_ref[p, pl.ds(owner * piece, piece), :width]
            left = lse[:, :LANES]
            for t in range(1, blk // LANES):
                left = jnp.where(owner * piece // LANES == t, lse[:, t * LANES : (t + 1) * LANES], left)
            out_ref[far, sb * piece :] = left


def merge_images(parts, offset, sb, piece, turn_ref):
    whole = merge_lse([lse for _, lse in parts])
    weights = []
    for k, (_, lse) in enumerate(parts):
        turn_ref[k] = jnp.exp2(lse - whole).T
        weights.append(turn_ref[k, pl.ds(offset, piece), :])
    images = []
    for p in range(sb):
        images.append(
            sum(
                image[p * piece : (p + 1) * piece] * weight[:, p : p + 1]
                for (image, _), weight in zip(parts, weights)
            )
        )
    return images, whole


def near_kernel(near, sb, piece, place_ref, *refs):
    in_refs, out_refs, turn_ref = refs[:near], refs[near : near + 4], refs[near + 4]
    me = lax.rem(place_ref[1], near)
    mine = place_ref[1] // near
    rows = sb * piece
    for d, out_ref in enumerate(out_refs):
        far = jnp.bitwise_xor(mine, d)
        offset = lax.rem((far * near + me) * piece, LANES)
        parts = [(ref[far, :rows], ref[far, rows:]) for ref in in_refs]
        images, whole = merge_images(parts, pl.multiple_of(offset, piece), sb, piece, turn_ref)
        for p in range(sb):
            out_ref[p * piece : (p + 1) * piece] = images[p]
        out_ref[rows:] = whole


def far_kernel(sb, piece, place_ref, *refs):
    in_refs, out_ref, turn_ref = refs[:4], refs[4], refs[5]
    rows = sb * piece
    offset = lax.rem(place_ref[1] * piece, LANES)
    parts = [(ref[:rows], ref[rows:]) for ref in in_refs]
    images, _ = merge_images(parts, pl.multiple_of(offset, piece), sb, piece, turn_ref)
    for p in range(sb):
        out_ref[p] = images[p]


def packed(points, mass, potential, axis):
    blocks, piece, width = points.shape
    here = lax.axis_index(axis) * piece % LANES
    lane = jnp.arange(LANES, dtype=jnp.int32)[None, :]
    inside = (lane >= here) & (lane < here + piece)

    def placed(vec):
        return jnp.where(inside, jnp.tile(vec, (1, LANES // piece)), 0)

    return jnp.concatenate([points.reshape(blocks * piece, width), placed(mass), placed(potential)])


def on_device(
    src_points, tgt_points, src_mass, tgt_mass, src_potential, tgt_potential, src_counts, tgt_counts, keep
):
    ntgt, nsrc = lax.axis_size("tgt"), lax.axis_size("src")
    near = near_count("tgt")
    sb, src_piece, width = src_points.shape
    tb, tgt_piece, _ = tgt_points.shape
    blk = src_piece * ntgt
    place = jnp.stack([lax.axis_index("src"), lax.axis_index("tgt")]).astype(jnp.int32)

    count, pairs = pl.pallas_call(
        list_kernel,
        out_shape=(
            jax.ShapeDtypeStruct((1,), jnp.int32),
            jax.ShapeDtypeStruct((sb * tb + GROUP,), jnp.int32),
        ),
        in_specs=[SMEM],
        out_specs=(SMEM, SMEM),
        name="kept_pairs",
    )(keep)

    y_fours = gather_pieces(packed(tgt_points, tgt_mass, tgt_potential, "src"), "src")
    x_fours = gather_pieces(packed(src_points, src_mass, src_potential, "tgt"), "tgt")

    vectors = (f32(sb, blk), f32(tb, blk), f32(sb, blk), f32(tb, blk))
    x, y, fixed, f, g, rows, cols = pl.pallas_call(
        functools.partial(first_kernel, len(x_fours), len(y_fours)),
        out_shape=(
            jax.ShapeDtypeStruct((ntgt, sb, src_piece, width), jnp.bfloat16),
            jax.ShapeDtypeStruct((nsrc, tb, tgt_piece, width), jnp.bfloat16),
            f32(4, sb, blk),
        )
        + vectors,
        in_specs=[SMEM] * 5 + [VMEM] * (len(x_fours) + len(y_fours)),
        out_specs=(VMEM,) * 7,
        scratch_shapes=[
            pltpu.VMEM((2, blk // LANES, sb, LANES), jnp.float32),
            pltpu.VMEM((2, blk // LANES, tb, LANES), jnp.float32),
        ]
        + sweep_scratch(sb, tb, blk),
        compiler_params=PARAMS,
        name="first_sweep",
    )(place, src_counts, tgt_counts, count, pairs, *x_fours, *y_fours)

    step = pl.pallas_call(
        step_kernel,
        out_shape=vectors,
        in_specs=[SMEM] * 2 + [VMEM] * 13,
        out_specs=(VMEM,) * 4,
        scratch_shapes=sweep_scratch(sb, tb, blk),
        compiler_params=PARAMS,
        name="sweep",
    )
    for _ in range(ITERS - 1):
        row_parts = exchange_lse(rows, "tgt")
        col_parts = exchange_lse(cols, "src")
        f, g, rows, cols = step(count, pairs, x, y, fixed, f, g, *row_parts, *col_parts)

    col_parts = exchange_lse(cols, "src")
    row_parts = exchange_lse(rows, "tgt")
    tile = sb * src_piece + sb
    g, *near_parts = pl.pallas_call(
        functools.partial(project_kernel, near),
        out_shape=(f32(tb, blk),) + (f32(4, tile, width),) * near,
        in_specs=[SMEM] * 3 + [VMEM] * 8,
        out_specs=(VMEM,) * (1 + near),
        scratch_shapes=[
            pltpu.VMEM((tb, blk), jnp.float32),
            pltpu.VMEM((max(sb, tb), blk, LANES), jnp.float32),
            pltpu.VMEM((sb * tb, blk), jnp.float32),
            pltpu.VMEM((sb * tb, blk), jnp.float32),
            pltpu.VMEM((sb, blk, 2 * width), jnp.float32),
        ],
        compiler_params=PARAMS,
        name="project",
    )(place, count, pairs, x, y, fixed, g, *col_parts)
    if near > 1:
        near_parts = near_parts[:1] + [swap(near_parts[d], "tgt", d) for d in range(1, near)]
    far_parts = pl.pallas_call(
        functools.partial(near_kernel, near, sb, src_piece),
        out_shape=(f32(tile, width),) * 4,
        in_specs=[SMEM] + [VMEM] * near,
        out_specs=(VMEM,) * 4,
        scratch_shapes=[pltpu.VMEM((near, LANES, sb), jnp.float32)],
        compiler_params=PARAMS,
        name="merge_near",
    )(place, *near_parts)
    far_parts = [far_parts[0]] + [swap(far_parts[k], "tgt", near * k) for k in range(1, 4)]
    images = pl.pallas_call(
        functools.partial(far_kernel, sb, src_piece),
        out_shape=f32(sb, src_piece, width),
        in_specs=[SMEM] + [VMEM] * 4,
        out_specs=VMEM,
        scratch_shapes=[pltpu.VMEM((4, LANES, sb), jnp.float32)],
        compiler_params=PARAMS,
        name="merge_far",
    )(place, *far_parts)

    f = 0.5 * (f + (fixed[0] - merge_lse(row_parts)))
    src_final = lax.dynamic_slice_in_dim(f * (1.0 / UNIT), place[1] * src_piece, src_piece, 1)
    tgt_final = lax.dynamic_slice_in_dim(g * (1.0 / UNIT), place[0] * tgt_piece, tgt_piece, 1)
    return images, src_final, tgt_final


def solution(mesh):
    return jax.shard_map(
        on_device,
        mesh=mesh,
        in_specs=(
            P("src", "tgt", None),
            P("tgt", "src", None),
            P("src", "tgt"),
            P("tgt", "src"),
            P("src", "tgt"),
            P("tgt", "src"),
            P("src"),
            P("tgt"),
            P("src", "tgt"),
        ),
        out_specs=(P("src", "tgt", None), P("src", "tgt"), P("tgt", "src")),
        check_vma=False,
    )
```

```python
import functools
import math

import jax
import jax.numpy as jnp
from jax import lax
from jax.experimental import pallas as pl
from jax.experimental.pallas import tpu as pltpu
from jax.sharding import PartitionSpec as P

ITERS = 4
EPSILON = 0.1
UNIT = 1.0 / (EPSILON * math.log(2.0))
FLOOR = -1e30
LANES = 128
GROUP = 8
MOVE_GROUP = 4

SMEM = pl.BlockSpec(memory_space=pltpu.SMEM)
VMEM = pl.BlockSpec(memory_space=pltpu.VMEM)
PARAMS = pltpu.CompilerParams(vmem_limit_bytes=40 * 1024 * 1024)


def f32(*shape):
    return jax.ShapeDtypeStruct(shape, jnp.float32)


def swap(part, axis, mask):
    return lax.ppermute(part, axis, [(i, i ^ mask) for i in range(lax.axis_size(axis))])


def near_count(axis):
    return lax.axis_size(axis) // 4


def merge_lse(parts):
    top = functools.reduce(jnp.maximum, parts)
    return top + jnp.log2(sum(jnp.exp2(part - top) for part in parts))


def exchange_lse(part, axis):
    near = near_count(axis)
    if near > 1:
        part = merge_lse([part] + [swap(part, axis, d) for d in range(1, near)])
    return [part] + [swap(part, axis, near * k) for k in range(1, 4)]


def gather_points(x_piece, y_piece, y_rows):
    nx, ny = near_count("tgt"), near_count("src")
    y_one, y_three = swap(y_piece, "src", ny), swap(y_piece, "src", 3 * ny)
    x_far = [swap(x_piece, "tgt", nx * k) for k in range(1, 4)]
    y_one, y_three, *x_far = lax.optimization_barrier((y_one, y_three, *x_far))
    half = y_rows // 2
    y_found = [
        (0, 0, y_piece),
        (ny, 0, y_one),
        (3 * ny, 0, y_three),
        (2 * ny, 0, swap(y_three[:half], "src", ny)),
        (2 * ny, half, swap(y_one[half:], "src", 3 * ny)),
    ]
    x_found = [(0, 0, x_piece)] + [(nx * k, 0, x_far[k - 1]) for k in range(1, 4)]
    return spread_near(x_found, "tgt"), spread_near(y_found, "src")


def spread_near(found, axis):
    near = near_count(axis)
    arrays = [array for _, _, array in found]
    parts = [(mask, first, k, 0, array.shape[0]) for k, (mask, first, array) in enumerate(found)]
    if near > 1:
        whole = jnp.concatenate(arrays)
        starts = [sum(a.shape[0] for a in arrays[:k]) for k in range(len(arrays))]
        arrays = [whole] + [swap(whole, axis, d) for d in range(1, near)]
        parts = [
            (mask ^ d, first, d, start, count)
            for d in range(near)
            for (mask, first, _, _, count), start in zip(parts, starts)
        ]
    return arrays, parts


def whole_block(ref, k):
    piece = ref[:, k]
    return piece.reshape(piece.shape[0] * piece.shape[1], piece.shape[2])


def split_columns(vec, split_ref):
    blocks, slots = vec.shape
    vec = vec * (1.0 / UNIT)
    parts = []
    for _ in range(3):
        part = vec.astype(jnp.bfloat16).astype(jnp.float32)
        parts.append(part)
        vec = vec - part
    parts.append(jnp.zeros((LANES - 3 * blocks, slots), jnp.float32))
    split_ref[...] = jnp.concatenate(parts, axis=0).T.astype(jnp.bfloat16)


def column_scores(stream_ref, q, split_ref, lane_ref, p):
    blocks = stream_ref.shape[1]
    lane = lax.broadcasted_iota(jnp.int32, split_ref.shape, 1)
    pick = jnp.where((lane < 3 * blocks) & (lax.rem(lane, blocks) == q), 1.0, 0.0).astype(jnp.bfloat16)
    score = lax.dot_general(
        jnp.concatenate([whole_block(stream_ref, q), split_ref[...]], axis=1),
        jnp.concatenate([whole_block(lane_ref, p), pick], axis=1),
        (((1,), (1,)), ((), ())),
        preferred_element_type=jnp.float32,
    )
    return score, jnp.max(score, axis=0, keepdims=True)


def column_lse(*operands):
    score, peak = column_scores(*operands)
    return peak * UNIT, jnp.sum(jnp.exp2((score - peak) * UNIT), axis=0, keepdims=True)


def clear(peak_ref, sum_ref):
    peak_ref[...] = jnp.full(peak_ref.shape, FLOOR, jnp.float32)
    sum_ref[...] = jnp.zeros(sum_ref.shape, jnp.float32)


def merge_slots(peak_ref, sum_ref, count):
    shape = (count, peak_ref.shape[0] // count, peak_ref.shape[1])
    peak = peak_ref[...].reshape(shape)
    top = jnp.max(peak, axis=1, keepdims=True)
    total = jnp.sum(sum_ref[...].reshape(shape) * jnp.exp2(peak - top), axis=1)
    return top[:, 0] + jnp.log2(jnp.maximum(total, 1.0))


def visit_pairs(count_ref, list_ref, tb, group, work):
    count = count_ref[0]

    @pl.loop(0, pl.cdiv(count, group))
    def _(step):
        places = [step * group + k for k in range(group)]
        codes = [list_ref[place] for place in places]
        work([(code // tb, lax.rem(code, tb), place < count) for place, code in zip(places, codes)])


def sweep(count_ref, list_ref, x_ref, y_ref, u, h, rows_ref, cols_ref, scratch):
    u_split_ref, h_split_ref, rpeak_ref, rsum_ref, cpeak_ref, csum_ref = scratch
    sb, tb = x_ref.shape[1], y_ref.shape[1]
    split_columns(u, u_split_ref)
    split_columns(h, h_split_ref)
    clear(rpeak_ref, rsum_ref)
    clear(cpeak_ref, csum_ref)

    def work(pairs):
        found = []
        for p, q, _ in pairs:
            row = column_lse(y_ref, q, h_split_ref, x_ref, p)
            col = column_lse(x_ref, p, u_split_ref, y_ref, q)
            found.append((p, q, row, col))
        for p, q, row, col in found:
            rpeak_ref[pl.ds(p * tb + q, 1), :], rsum_ref[pl.ds(p * tb + q, 1), :] = row
            cpeak_ref[pl.ds(q * sb + p, 1), :], csum_ref[pl.ds(q * sb + p, 1), :] = col

    visit_pairs(count_ref, list_ref, tb, GROUP, work)
    rows_ref[...] = merge_slots(rpeak_ref, rsum_ref, sb)
    cols_ref[...] = merge_slots(cpeak_ref, csum_ref, tb)


def sweep_scratch(sb, tb, blk):
    return [
        pltpu.VMEM((blk, LANES), jnp.bfloat16),
        pltpu.VMEM((blk, LANES), jnp.bfloat16),
        pltpu.VMEM((sb * tb, blk), jnp.float32),
        pltpu.VMEM((sb * tb, blk), jnp.float32),
        pltpu.VMEM((sb * tb, blk), jnp.float32),
        pltpu.VMEM((sb * tb, blk), jnp.float32),
    ]


def project_scratch(sb, tb, blk, width):
    return [
        pltpu.VMEM((blk, LANES), jnp.bfloat16),
        pltpu.VMEM((tb, width, blk), jnp.bfloat16),
        pltpu.VMEM((sb + 1, 1, blk), jnp.float32),
        pltpu.VMEM((sb + 1, 1, blk), jnp.float32),
        pltpu.VMEM((sb + 1, width, blk), jnp.float32),
        pltpu.VMEM((sb, blk, width), jnp.float32),
    ]


def list_kernel(keep_ref, count_ref, list_ref):
    sb, tb = keep_ref.shape

    n, last = jnp.int32(0), jnp.int32(0)
    for code in range(sb * tb):
        kept = keep_ref[code // tb, code % tb] > 0
        list_ref[n] = code
        n = n + kept.astype(jnp.int32)
        last = jnp.where(kept, code, last)
    for k in range(GROUP):
        list_ref[n + k] = last
    count_ref[0] = n


def assemble(place, counts_ref, parts, part_refs, points_ref, vec_ref):
    n, blocks, piece, width = points_ref.shape
    blk = n * piece
    vec_ref[...] = jnp.zeros(vec_ref.shape, jnp.float32)
    for mask, first, k, start, count in parts:
        owner = jnp.bitwise_xor(place, mask)
        rows = min(count, blocks * piece - first)
        points_ref[owner, first // piece : (first + rows) // piece] = part_refs[k][start : start + rows].reshape(
            rows // piece, piece, width
        )
        if rows < count:
            vecs = part_refs[k][start + rows : start + count].astype(jnp.float32)
            tile = owner * piece // LANES
            vec_ref[0, tile] += vecs[:blocks]
            vec_ref[1, tile] += vecs[blocks:]
    mass = jnp.concatenate([vec_ref[0, t] for t in range(blk // LANES)], axis=1)
    potential = jnp.concatenate([vec_ref[1, t] for t in range(blk // LANES)], axis=1) * UNIT
    block_of = lax.broadcasted_iota(jnp.int32, (blocks, blk), 0)
    slot_of = lax.broadcasted_iota(jnp.int32, (blocks, blk), 1)
    half = jnp.zeros((blocks, blk), jnp.float32)
    count = jnp.zeros((blocks, blk), jnp.int32)
    ones = jnp.ones((blocks, width), jnp.bfloat16)
    for k in range(blocks):
        wide = whole_block(points_ref, k).astype(jnp.float32)
        square = wide * wide
        high = square.astype(jnp.bfloat16)
        low = (square - high.astype(jnp.float32)).astype(jnp.bfloat16)
        norm = sum(
            lax.dot_general(ones, part, (((1,), (1,)), ((), ())), preferred_element_type=jnp.float32)
            for part in (high, low)
        )
        half = jnp.where(block_of == k, norm * (0.5 * UNIT), half)
        count = jnp.where(block_of == k, counts_ref[k], count)
    base = jnp.where(slot_of < count, jnp.log2(mass) - half, FLOOR)
    return potential, half, base


def first_kernel(x_parts, y_parts, src_counts_ref, tgt_counts_ref, count_ref, list_ref, *refs):
    nx = 1 + max(part[2] for part in x_parts)
    ny = 1 + max(part[2] for part in y_parts)
    x_in, y_in, refs = refs[:nx], refs[nx : nx + ny], refs[nx + ny :]
    x_ref, y_ref, fixed_ref, f_ref, g_ref, rows_ref, cols_ref, xvec_ref, yvec_ref = refs[:9]
    f, x_half, x_base = assemble(lax.axis_index("tgt"), src_counts_ref, x_parts, x_in, x_ref, xvec_ref)
    g, y_half, y_base = assemble(lax.axis_index("src"), tgt_counts_ref, y_parts, y_in, y_ref, yvec_ref)
    f_ref[...] = f
    g_ref[...] = g
    for k, vec in enumerate((x_half, x_base, y_half, y_base)):
        fixed_ref[k] = vec
    sweep(count_ref, list_ref, x_ref, y_ref, f + x_base, g + y_base, rows_ref, cols_ref, refs[9:])


def updated(old, half, part_refs):
    return 0.5 * (old + (half - merge_lse([ref[...] for ref in part_refs])))


def step_kernel(count_ref, list_ref, x_ref, y_ref, fixed_ref, f_in_ref, g_in_ref, *refs):
    row_refs, col_refs, refs = refs[:4], refs[4:8], refs[8:]
    f_ref, g_ref, rows_ref, cols_ref = refs[:4]
    f = updated(f_in_ref[...], fixed_ref[0], row_refs)
    g = updated(g_in_ref[...], fixed_ref[2], col_refs)
    f_ref[...] = f
    g_ref[...] = g
    sweep(count_ref, list_ref, x_ref, y_ref, f + fixed_ref[1], g + fixed_ref[3], rows_ref, cols_ref, refs[4:])


def project_kernel(near, count_ref, list_ref, x_ref, y_ref, fixed_ref, g_in_ref, *refs):
    col_refs, g_ref, out_refs = refs[:4], refs[4], refs[5 : 5 + near]
    split_ref, turned_ref, peak_ref, sum_ref, acc_ref, image_ref = refs[5 + near :]
    n, sb, piece, width = x_ref.shape
    tb = y_ref.shape[1]
    blk = n * piece
    g = updated(g_in_ref[...], fixed_ref[2], col_refs)
    g_ref[...] = g
    split_columns(g + fixed_ref[3], split_ref)
    for q in range(tb):
        turned_ref[q] = whole_block(y_ref, q).T
    clear(peak_ref, sum_ref)
    acc_ref[...] = jnp.zeros(acc_ref.shape, jnp.float32)

    def move(pairs):
        found = []
        for p, q, real in pairs:
            score, peak = column_scores(y_ref, q, split_ref, x_ref, p)
            weights = jnp.exp2((score - peak) * UNIT)
            high = weights.astype(jnp.bfloat16)
            low = (weights - high.astype(jnp.float32)).astype(jnp.bfloat16)
            ys = turned_ref[q]
            moved = jnp.dot(ys, high, preferred_element_type=jnp.float32) + jnp.dot(
                ys, low, preferred_element_type=jnp.float32
            )
            found.append((jnp.where(real, p, sb), peak * UNIT, jnp.sum(weights, axis=0, keepdims=True), moved))
        for p, peak, total, moved in found:
            old = peak_ref[p]
            new = jnp.maximum(old, peak)
            before, here = jnp.exp2(old - new), jnp.exp2(peak - new)
            peak_ref[p] = new
            sum_ref[p] = sum_ref[p] * before + total * here
            acc_ref[p] = acc_ref[p] * before + moved * here

    visit_pairs(count_ref, list_ref, tb, MOVE_GROUP, move)
    rows = []
    for p in range(sb):
        total = jnp.maximum(sum_ref[p], 1.0)
        image_ref[p] = (acc_ref[p] / total).T
        rows.append(peak_ref[p] + jnp.log2(total))
    lse = jnp.concatenate(rows, axis=0)

    me = lax.rem(lax.axis_index("tgt"), near)
    for e, out_ref in enumerate(out_refs):
        for far in range(4):
            owner = far * near + jnp.bitwise_xor(me, e)
            for p in range(sb):
                out_ref[far, p * piece : (p + 1) * piece] = image_ref[p, pl.ds(pl.multiple_of(owner * piece, piece), piece)]
            left = lse[:, :LANES]
            for t in range(1, blk // LANES):
                left = jnp.where(owner * piece // LANES == t, lse[:, t * LANES : (t + 1) * LANES], left)
            out_ref[far, sb * piece :] = left


def merge_images(parts, offset, sb, piece, turn_ref):
    whole = merge_lse([lse for _, lse in parts])
    weights = []
    for k, (_, lse) in enumerate(parts):
        turn_ref[k] = jnp.exp2(lse - whole).T
        weights.append(turn_ref[k, pl.ds(offset, piece), :])
    images = []
    for p in range(sb):
        images.append(
            sum(
                image[p * piece : (p + 1) * piece] * weight[:, p : p + 1]
                for (image, _), weight in zip(parts, weights)
            )
        )
    return images, whole


def near_kernel(near, sb, piece, *refs):
    in_refs, out_refs, turn_ref = refs[:near], refs[near : near + 4], refs[near + 4]
    place = lax.axis_index("tgt")
    me, mine = lax.rem(place, near), place // near
    rows = sb * piece
    for d, out_ref in enumerate(out_refs):
        far = jnp.bitwise_xor(mine, d)
        offset = lax.rem((far * near + me) * piece, LANES)
        parts = [(ref[far, :rows], ref[far, rows:]) for ref in in_refs]
        images, whole = merge_images(parts, pl.multiple_of(offset, piece), sb, piece, turn_ref)
        for p in range(sb):
            out_ref[p * piece : (p + 1) * piece] = images[p]
        out_ref[rows:] = whole


def far_kernel(sb, piece, *refs):
    in_refs, out_ref, turn_ref = refs[:4], refs[4], refs[5]
    rows = sb * piece
    offset = lax.rem(lax.axis_index("tgt") * piece, LANES)
    parts = [(ref[:rows], ref[rows:]) for ref in in_refs]
    images, _ = merge_images(parts, pl.multiple_of(offset, piece), sb, piece, turn_ref)
    for p in range(sb):
        out_ref[p] = images[p]


def pack_kernel(*refs):
    for k, axis in enumerate(("tgt", "src")):
        points_ref, mass_ref, potential_ref = refs[3 * k : 3 * k + 3]
        out_ref = refs[6 + k]
        blocks, piece, width = points_ref.shape
        here = lax.rem(lax.axis_index(axis) * piece, LANES)
        slot = lax.broadcasted_iota(jnp.int32, (piece, LANES), 0)
        lane = lax.broadcasted_iota(jnp.int32, (piece, LANES), 1)
        put = jnp.where(lane == slot + here, 1.0, 0.0).astype(jnp.bfloat16)
        vecs = [jnp.dot(ref[...], put, preferred_element_type=jnp.float32) for ref in (mass_ref, potential_ref)]
        out_ref[: blocks * piece] = points_ref[...].reshape(blocks * piece, width)
        out_ref[blocks * piece :] = jnp.concatenate(vecs, axis=0).astype(jnp.bfloat16)


def on_device(
    src_points, tgt_points, src_mass, tgt_mass, src_potential, tgt_potential, src_counts, tgt_counts, keep
):
    ntgt, nsrc = lax.axis_size("tgt"), lax.axis_size("src")
    near = near_count("tgt")
    sb, src_piece, width = src_points.shape
    tb, tgt_piece, _ = tgt_points.shape
    blk = src_piece * ntgt
    count, pairs = pl.pallas_call(
        list_kernel,
        out_shape=(
            jax.ShapeDtypeStruct((1,), jnp.int32),
            jax.ShapeDtypeStruct((sb * tb + GROUP,), jnp.int32),
        ),
        in_specs=[SMEM],
        out_specs=(SMEM, SMEM),
        name="kept_pairs",
    )(keep)

    x_rows, y_rows = sb * src_piece, tb * tgt_piece
    x_packed, y_packed = pl.pallas_call(
        pack_kernel,
        out_shape=(
            jax.ShapeDtypeStruct((x_rows + 2 * sb, width), jnp.bfloat16),
            jax.ShapeDtypeStruct((y_rows + 2 * tb, width), jnp.bfloat16),
        ),
        in_specs=[VMEM] * 6,
        out_specs=(VMEM, VMEM),
        name="pack",
    )(src_points, src_mass, src_potential, tgt_points, tgt_mass, tgt_potential)
    (x_in, x_parts), (y_in, y_parts) = gather_points(x_packed, y_packed, y_rows)

    vectors = (f32(sb, blk), f32(tb, blk), f32(sb, blk), f32(tb, blk))
    x, y, fixed, f, g, rows, cols = pl.pallas_call(
        functools.partial(first_kernel, x_parts, y_parts),
        out_shape=(
            jax.ShapeDtypeStruct((ntgt, sb, src_piece, width), jnp.bfloat16),
            jax.ShapeDtypeStruct((nsrc, tb, tgt_piece, width), jnp.bfloat16),
            f32(4, sb, blk),
        )
        + vectors,
        in_specs=[SMEM] * 4 + [VMEM] * (len(x_in) + len(y_in)),
        out_specs=(VMEM,) * 7,
        scratch_shapes=[
            pltpu.VMEM((2, blk // LANES, sb, LANES), jnp.float32),
            pltpu.VMEM((2, blk // LANES, tb, LANES), jnp.float32),
        ]
        + sweep_scratch(sb, tb, blk),
        compiler_params=PARAMS,
        name="first_sweep",
    )(src_counts, tgt_counts, count, pairs, *x_in, *y_in)

    step = pl.pallas_call(
        step_kernel,
        out_shape=vectors,
        in_specs=[SMEM] * 2 + [VMEM] * 13,
        out_specs=(VMEM,) * 4,
        scratch_shapes=sweep_scratch(sb, tb, blk),
        compiler_params=PARAMS,
        name="sweep",
    )
    for _ in range(ITERS - 1):
        row_parts = exchange_lse(rows, "tgt")
        col_parts = exchange_lse(cols, "src")
        f, g, rows, cols = step(count, pairs, x, y, fixed, f, g, *row_parts, *col_parts)

    col_parts = exchange_lse(cols, "src")
    row_parts = exchange_lse(rows, "tgt")
    tile = sb * src_piece + sb
    g, *near_parts = pl.pallas_call(
        functools.partial(project_kernel, near),
        out_shape=(f32(tb, blk),) + (f32(4, tile, width),) * near,
        in_specs=[SMEM] * 2 + [VMEM] * 8,
        out_specs=(VMEM,) * (1 + near),
        scratch_shapes=project_scratch(sb, tb, blk, width),
        compiler_params=PARAMS,
        name="project",
    )(count, pairs, x, y, fixed, g, *col_parts)
    if near > 1:
        near_parts = near_parts[:1] + [swap(near_parts[d], "tgt", d) for d in range(1, near)]
    far_parts = pl.pallas_call(
        functools.partial(near_kernel, near, sb, src_piece),
        out_shape=(f32(tile, width),) * 4,
        in_specs=[VMEM] * near,
        out_specs=(VMEM,) * 4,
        scratch_shapes=[pltpu.VMEM((near, LANES, sb), jnp.float32)],
        compiler_params=PARAMS,
        name="merge_near",
    )(*near_parts)
    far_parts = [far_parts[0]] + [swap(far_parts[k], "tgt", near * k) for k in range(1, 4)]
    images = pl.pallas_call(
        functools.partial(far_kernel, sb, src_piece),
        out_shape=f32(sb, src_piece, width),
        in_specs=[VMEM] * 4,
        out_specs=VMEM,
        scratch_shapes=[pltpu.VMEM((4, LANES, sb), jnp.float32)],
        compiler_params=PARAMS,
        name="merge_far",
    )(*far_parts)

    f = 0.5 * (f + (fixed[0] - merge_lse(row_parts)))
    src_final = lax.dynamic_slice_in_dim(f * (1.0 / UNIT), lax.axis_index("tgt") * src_piece, src_piece, 1)
    tgt_final = lax.dynamic_slice_in_dim(g * (1.0 / UNIT), lax.axis_index("src") * tgt_piece, tgt_piece, 1)
    return images, src_final, tgt_final


def solution(mesh):
    return jax.shard_map(
        on_device,
        mesh=mesh,
        in_specs=(
            P("src", "tgt", None),
            P("tgt", "src", None),
            P("src", "tgt"),
            P("tgt", "src"),
            P("src", "tgt"),
            P("tgt", "src"),
            P("src"),
            P("tgt"),
            P("src", "tgt"),
        ),
        out_specs=(P("src", "tgt", None), P("src", "tgt"), P("tgt", "src")),
        check_vma=False,
    )
```

```python
import functools
import math

import jax
import jax.numpy as jnp
from jax import lax
from jax.experimental import pallas as pl
from jax.experimental.pallas import tpu as pltpu
from jax.sharding import PartitionSpec as P

ITERS = 4
EPSILON = 0.1
UNIT = 1.0 / (EPSILON * math.log(2.0))
FLOOR = -1e30
LANES = 128
GROUP = 8
MOVE_GROUP = 4

SMEM = pl.BlockSpec(memory_space=pltpu.SMEM)
VMEM = pl.BlockSpec(memory_space=pltpu.VMEM)
PARAMS = pltpu.CompilerParams(vmem_limit_bytes=40 * 1024 * 1024)


def f32(*shape):
    return jax.ShapeDtypeStruct(shape, jnp.float32)


def swap(part, axis, mask):
    return lax.ppermute(part, axis, [(i, i ^ mask) for i in range(lax.axis_size(axis))])


def near_count(axis):
    return lax.axis_size(axis) // 4


def merge_lse(parts):
    top = functools.reduce(jnp.maximum, parts)
    return top + jnp.log2(sum(jnp.exp2(part - top) for part in parts))


def exchange_lse(part, axis):
    near = near_count(axis)
    if near > 1:
        part = merge_lse([part] + [swap(part, axis, d) for d in range(1, near)])
    return merge_lse([part] + [swap(part, axis, near * k) for k in range(1, 4)])


def exchange_both(both):
    if near_count("tgt") != 2 or near_count("src") != 1:
        whole = jnp.stack([exchange_lse(both[0], "tgt"), exchange_lse(both[1], "src")])
        return whole, whole
    odd = lax.rem(lax.axis_index("tgt"), 2) == 1
    other = swap(both, "tgt", 1)
    rows = merge_lse([both[0], other[0]])
    part = jnp.where(odd, jnp.stack([rows, rows]), jnp.stack([both[1], other[1]]))
    ntgt, nsrc = lax.axis_size("tgt"), lax.axis_size("src")

    def swap_far(k):
        pairs = [
            (s * ntgt + t, s * ntgt + (t ^ (2 * k)) if t % 2 else (s ^ k) * ntgt + t)
            for s in range(nsrc)
            for t in range(ntgt)
        ]
        return lax.ppermute(part, ("src", "tgt"), pairs)

    whole = merge_lse([part] + [swap_far(k) for k in range(1, 4)])
    return whole, swap(whole, "tgt", 1)


def gather_points(x_piece, y_piece, y_rows):
    nx, ny = near_count("tgt"), near_count("src")
    y_one, y_three = swap(y_piece, "src", ny), swap(y_piece, "src", 3 * ny)
    x_far = [swap(x_piece, "tgt", nx * k) for k in range(1, 4)]
    y_one, y_three, *x_far = lax.optimization_barrier((y_one, y_three, *x_far))
    half = y_rows // 2
    y_found = [
        (0, 0, y_piece),
        (ny, 0, y_one),
        (3 * ny, 0, y_three),
        (2 * ny, 0, swap(y_three[:half], "src", ny)),
        (2 * ny, half, swap(y_one[half:], "src", 3 * ny)),
    ]
    x_found = [(0, 0, x_piece)] + [(nx * k, 0, x_far[k - 1]) for k in range(1, 4)]
    return spread_near(x_found, "tgt"), spread_near(y_found, "src")


def spread_near(found, axis):
    near = near_count(axis)
    arrays, parts = [], []
    for d in range(near):
        for mask, first, array in found:
            parts.append((mask ^ d, first, len(arrays), array.shape[0]))
            arrays.append(swap(array, axis, d) if d else array)
    return arrays, parts


def whole_block(ref, k):
    piece = ref[:, k]
    return piece.reshape(piece.shape[0] * piece.shape[1], piece.shape[2])


def split_columns(vec, split_ref):
    blocks, slots = vec.shape
    vec = vec * (1.0 / UNIT)
    parts = []
    for _ in range(3):
        part = vec.astype(jnp.bfloat16).astype(jnp.float32)
        parts.append(part)
        vec = vec - part
    parts.append(jnp.zeros((LANES - 3 * blocks, slots), jnp.float32))
    split_ref[...] = jnp.concatenate(parts, axis=0).T.astype(jnp.bfloat16)


def column_scores(stream_ref, q, split_ref, lane_ref, p):
    blocks = stream_ref.shape[1]
    lane = lax.broadcasted_iota(jnp.int32, (16, LANES), 1)
    pick = jnp.where((lane < 3 * blocks) & (lax.rem(lane, blocks) == q), 1.0, 0.0).astype(jnp.bfloat16)
    pick = jnp.concatenate([pick] * (split_ref.shape[0] // 16), axis=0)
    score = lax.dot_general(
        jnp.concatenate([whole_block(stream_ref, q), split_ref[...]], axis=1),
        jnp.concatenate([whole_block(lane_ref, p), pick], axis=1),
        (((1,), (1,)), ((), ())),
        preferred_element_type=jnp.float32,
    )
    return score, jnp.max(score, axis=0, keepdims=True)


def column_lse(*operands):
    score, peak = column_scores(*operands)
    return peak * UNIT, jnp.sum(jnp.exp2((score - peak) * UNIT), axis=0, keepdims=True)


def clear(peak_ref, sum_ref):
    peak_ref[...] = jnp.full(peak_ref.shape, FLOOR, jnp.float32)
    sum_ref[...] = jnp.zeros(sum_ref.shape, jnp.float32)


def merge_slots(peak_ref, sum_ref, count):
    shape = (count, peak_ref.shape[0] // count, peak_ref.shape[1])
    peak = peak_ref[...].reshape(shape)
    top = jnp.max(peak, axis=1, keepdims=True)
    total = jnp.sum(sum_ref[...].reshape(shape) * jnp.exp2(peak - top), axis=1)
    return top[:, 0] + jnp.log2(jnp.maximum(total, 1.0))


def visit_pairs(list_ref, tb, group, work):
    count = list_ref[0]

    @pl.loop(0, pl.cdiv(count, group))
    def _(step):
        places = [step * group + k for k in range(group)]
        codes = [list_ref[1 + place] for place in places]
        work([(code // tb, lax.rem(code, tb), place < count) for place, code in zip(places, codes)])


def sweep(list_ref, x_ref, y_ref, u, h, both_ref, scratch):
    u_split_ref, h_split_ref, rpeak_ref, rsum_ref, cpeak_ref, csum_ref = scratch
    sb, tb = x_ref.shape[1], y_ref.shape[1]
    split_columns(u, u_split_ref)
    split_columns(h, h_split_ref)
    clear(rpeak_ref, rsum_ref)
    clear(cpeak_ref, csum_ref)

    def work(pairs):
        found = []
        for p, q, _ in pairs:
            row = column_lse(y_ref, q, h_split_ref, x_ref, p)
            col = column_lse(x_ref, p, u_split_ref, y_ref, q)
            found.append((p, q, row, col))
        for p, q, row, col in found:
            rpeak_ref[pl.ds(p * tb + q, 1), :], rsum_ref[pl.ds(p * tb + q, 1), :] = row
            cpeak_ref[pl.ds(q * sb + p, 1), :], csum_ref[pl.ds(q * sb + p, 1), :] = col

    visit_pairs(list_ref, tb, GROUP, work)
    both_ref[0] = merge_slots(rpeak_ref, rsum_ref, sb)
    both_ref[1] = merge_slots(cpeak_ref, csum_ref, tb)


def sweep_scratch(sb, tb, blk):
    return [
        pltpu.VMEM((blk, LANES), jnp.bfloat16),
        pltpu.VMEM((blk, LANES), jnp.bfloat16),
        pltpu.VMEM((sb * tb, blk), jnp.float32),
        pltpu.VMEM((sb * tb, blk), jnp.float32),
        pltpu.VMEM((sb * tb, blk), jnp.float32),
        pltpu.VMEM((sb * tb, blk), jnp.float32),
    ]


def project_scratch(sb, tb, blk, width):
    return [
        pltpu.VMEM((blk, LANES), jnp.bfloat16),
        pltpu.VMEM((tb, width, blk), jnp.bfloat16),
        pltpu.VMEM((sb + 1, 1, blk), jnp.float32),
        pltpu.VMEM((sb + 1, 1, blk), jnp.float32),
        pltpu.VMEM((sb + 1, width, blk), jnp.float32),
        pltpu.VMEM((sb, blk, width), jnp.float32),
    ]


def list_kernel(keep_ref, list_ref):
    sb, tb = keep_ref.shape
    n, last = jnp.int32(1), jnp.int32(0)
    for code in range(sb * tb):
        kept = keep_ref[code // tb, code % tb] > 0
        list_ref[n] = code
        n = n + kept.astype(jnp.int32)
        last = jnp.where(kept, code, last)
    for k in range(GROUP):
        list_ref[n + k] = last
    list_ref[0] = n - 1


def assemble(place, counts_ref, parts, part_refs, points_ref, vec_ref):
    n, blocks, piece, width = points_ref.shape
    blk = n * piece
    vec_ref[...] = jnp.zeros(vec_ref.shape, jnp.float32)
    for mask, first, k, count in parts:
        owner = jnp.bitwise_xor(place, mask)
        rows = min(count, blocks * piece - first)
        points_ref[owner, first // piece : (first + rows) // piece] = part_refs[k][:rows].reshape(
            rows // piece, piece, width
        )
        if rows < count:
            vecs = part_refs[k][rows:count].astype(jnp.float32)
            tile = owner * piece // LANES
            vec_ref[0, tile] += vecs[:blocks]
            vec_ref[1, tile] += vecs[blocks:]
    mass = jnp.concatenate([vec_ref[0, t] for t in range(blk // LANES)], axis=1)
    potential = jnp.concatenate([vec_ref[1, t] for t in range(blk // LANES)], axis=1) * UNIT
    block_of = lax.broadcasted_iota(jnp.int32, (blocks, blk), 0)
    slot_of = lax.broadcasted_iota(jnp.int32, (blocks, blk), 1)
    half = jnp.zeros((blocks, blk), jnp.float32)
    count = jnp.zeros((blocks, blk), jnp.int32)
    ones = jnp.ones((blocks, width), jnp.bfloat16)
    for k in range(blocks):
        wide = whole_block(points_ref, k).astype(jnp.float32)
        square = wide * wide
        high = square.astype(jnp.bfloat16)
        low = (square - high.astype(jnp.float32)).astype(jnp.bfloat16)
        norm = sum(
            lax.dot_general(ones, part, (((1,), (1,)), ((), ())), preferred_element_type=jnp.float32)
            for part in (high, low)
        )
        half = jnp.where(block_of == k, norm * (0.5 * UNIT), half)
        count = jnp.where(block_of == k, counts_ref[k], count)
    base = jnp.where(slot_of < count, jnp.log2(mass) - half, FLOOR)
    return potential, half, base


def first_kernel(x_parts, y_parts, src_counts_ref, tgt_counts_ref, list_ref, *refs):
    nx = 1 + max(part[2] for part in x_parts)
    ny = 1 + max(part[2] for part in y_parts)
    x_in, y_in, refs = refs[:nx], refs[nx : nx + ny], refs[nx + ny :]
    x_ref, y_ref, fixed_ref, f_ref, g_ref, both_ref, xvec_ref, yvec_ref = refs[:8]
    f, x_half, x_base = assemble(lax.axis_index("tgt"), src_counts_ref, x_parts, x_in, x_ref, xvec_ref)
    g, y_half, y_base = assemble(lax.axis_index("src"), tgt_counts_ref, y_parts, y_in, y_ref, yvec_ref)
    f_ref[...] = f
    g_ref[...] = g
    for k, vec in enumerate((x_half, x_base, y_half, y_base)):
        fixed_ref[k] = vec
    sweep(list_ref, x_ref, y_ref, f + x_base, g + y_base, both_ref, refs[8:])


def chosen(whole_ref, other_ref, paired):
    if not paired:
        return whole_ref[0], whole_ref[1]
    odd = lax.rem(lax.axis_index("tgt"), 2) == 1
    return jnp.where(odd, whole_ref[0], other_ref[0]), jnp.where(odd, other_ref[1], whole_ref[0])


def updated(f, g, fixed_ref, whole_ref, other_ref, paired):
    rows, cols = chosen(whole_ref, other_ref, paired)
    return 0.5 * (f + (fixed_ref[0] - rows)), 0.5 * (g + (fixed_ref[2] - cols))


def step_kernel(paired, list_ref, x_ref, y_ref, fixed_ref, f_in_ref, g_in_ref, whole_ref, other_ref, *refs):
    f_ref, g_ref, both_ref = refs[:3]
    f, g = updated(f_in_ref[...], g_in_ref[...], fixed_ref, whole_ref, other_ref, paired)
    f_ref[...] = f
    g_ref[...] = g
    sweep(list_ref, x_ref, y_ref, f + fixed_ref[1], g + fixed_ref[3], both_ref, refs[3:])


def project_kernel(
    near, paired, list_ref, x_ref, y_ref, fixed_ref, f_in_ref, g_in_ref, whole_ref, other_ref, *refs
):
    f_ref, g_ref, out_refs = refs[0], refs[1], refs[2 : 2 + near]
    split_ref, turned_ref, peak_ref, sum_ref, acc_ref, image_ref = refs[2 + near :]
    n, sb, piece, width = x_ref.shape
    tb = y_ref.shape[1]
    blk = n * piece
    f, g = updated(f_in_ref[...], g_in_ref[...], fixed_ref, whole_ref, other_ref, paired)
    f_ref[...] = f * (1.0 / UNIT)
    g_ref[...] = g * (1.0 / UNIT)
    split_columns(g + fixed_ref[3], split_ref)
    for q in range(tb):
        turned_ref[q] = whole_block(y_ref, q).T
    clear(peak_ref, sum_ref)
    acc_ref[...] = jnp.zeros(acc_ref.shape, jnp.float32)

    def move(pairs):
        found = []
        for p, q, real in pairs:
            score, peak = column_scores(y_ref, q, split_ref, x_ref, p)
            weights = jnp.exp2((score - peak) * UNIT)
            high = weights.astype(jnp.bfloat16)
            low = (weights - high.astype(jnp.float32)).astype(jnp.bfloat16)
            ys = turned_ref[q]
            moved = jnp.dot(ys, high, preferred_element_type=jnp.float32) + jnp.dot(
                ys, low, preferred_element_type=jnp.float32
            )
            found.append((jnp.where(real, p, sb), peak * UNIT, jnp.sum(weights, axis=0, keepdims=True), moved))
        for p, peak, total, moved in found:
            old = peak_ref[p]
            new = jnp.maximum(old, peak)
            before, here = jnp.exp2(old - new), jnp.exp2(peak - new)
            peak_ref[p] = new
            sum_ref[p] = sum_ref[p] * before + total * here
            acc_ref[p] = acc_ref[p] * before + moved * here

    visit_pairs(list_ref, tb, MOVE_GROUP, move)
    rows = []
    for p in range(sb):
        total = jnp.maximum(sum_ref[p], 1.0)
        image_ref[p] = (acc_ref[p] / total).T
        rows.append(peak_ref[p] + jnp.log2(total))
    lse = jnp.concatenate(rows, axis=0)

    me = lax.rem(lax.axis_index("tgt"), near)
    for e, out_ref in enumerate(out_refs):
        for far in range(4):
            owner = far * near + jnp.bitwise_xor(me, e)
            for p in range(sb):
                out_ref[far, p * piece : (p + 1) * piece] = image_ref[p, pl.ds(pl.multiple_of(owner * piece, piece), piece)]
            left = lse[:, :LANES]
            for t in range(1, blk // LANES):
                left = jnp.where(owner * piece // LANES == t, lse[:, t * LANES : (t + 1) * LANES], left)
            out_ref[far, sb * piece :] = left


def merge_images(parts, offset, sb, piece, turn_ref):
    whole = merge_lse([lse for _, lse in parts])
    weights = []
    for k, (_, lse) in enumerate(parts):
        turn_ref[k] = jnp.exp2(lse - whole).T
        weights.append(turn_ref[k, pl.ds(offset, piece), :])
    images = []
    for p in range(sb):
        images.append(
            sum(
                image[p * piece : (p + 1) * piece] * weight[:, p : p + 1]
                for (image, _), weight in zip(parts, weights)
            )
        )
    return images, whole


def near_kernel(near, sb, piece, *refs):
    in_refs, out_refs, turn_ref = refs[:near], refs[near : near + 4], refs[near + 4]
    place = lax.axis_index("tgt")
    me, mine = lax.rem(place, near), place // near
    rows = sb * piece
    for d, out_ref in enumerate(out_refs):
        far = jnp.bitwise_xor(mine, d)
        offset = lax.rem((far * near + me) * piece, LANES)
        parts = [(ref[far, :rows], ref[far, rows:]) for ref in in_refs]
        images, whole = merge_images(parts, pl.multiple_of(offset, piece), sb, piece, turn_ref)
        for p in range(sb):
            out_ref[p * piece : (p + 1) * piece] = images[p]
        out_ref[rows:] = whole


def far_kernel(sb, piece, *refs):
    in_refs, out_ref, turn_ref = refs[:4], refs[4], refs[5]
    rows = sb * piece
    offset = lax.rem(lax.axis_index("tgt") * piece, LANES)
    parts = [(ref[:rows], ref[rows:]) for ref in in_refs]
    images, _ = merge_images(parts, pl.multiple_of(offset, piece), sb, piece, turn_ref)
    for p in range(sb):
        out_ref[p] = images[p]


def pack_kernel(*refs):
    for k, axis in enumerate(("tgt", "src")):
        points_ref, mass_ref, potential_ref = refs[3 * k : 3 * k + 3]
        out_ref = refs[6 + k]
        blocks, piece, width = points_ref.shape
        here = lax.rem(lax.axis_index(axis) * piece, LANES)
        slot = lax.broadcasted_iota(jnp.int32, (piece, LANES), 0)
        lane = lax.broadcasted_iota(jnp.int32, (piece, LANES), 1)
        put = jnp.where(lane == slot + here, 1.0, 0.0).astype(jnp.bfloat16)
        vecs = [jnp.dot(ref[...], put, preferred_element_type=jnp.float32) for ref in (mass_ref, potential_ref)]
        out_ref[: blocks * piece] = points_ref[...].reshape(blocks * piece, width)
        out_ref[blocks * piece :] = jnp.concatenate(vecs, axis=0).astype(jnp.bfloat16)


def on_device(
    src_points, tgt_points, src_mass, tgt_mass, src_potential, tgt_potential, src_counts, tgt_counts, keep
):
    ntgt, nsrc = lax.axis_size("tgt"), lax.axis_size("src")
    near = near_count("tgt")
    sb, src_piece, width = src_points.shape
    tb, tgt_piece, _ = tgt_points.shape
    blk = src_piece * ntgt
    pairs = pl.pallas_call(
        list_kernel,
        out_shape=jax.ShapeDtypeStruct((1 + sb * tb + GROUP,), jnp.int32),
        in_specs=[SMEM],
        out_specs=SMEM,
        compiler_params=PARAMS,
        name="kept_pairs",
    )(keep)

    x_rows, y_rows = sb * src_piece, tb * tgt_piece
    x_packed, y_packed = pl.pallas_call(
        pack_kernel,
        out_shape=(
            jax.ShapeDtypeStruct((x_rows + 2 * sb, width), jnp.bfloat16),
            jax.ShapeDtypeStruct((y_rows + 2 * tb, width), jnp.bfloat16),
        ),
        in_specs=[VMEM] * 6,
        out_specs=(VMEM, VMEM),
        name="pack",
    )(src_points, src_mass, src_potential, tgt_points, tgt_mass, tgt_potential)
    (x_in, x_parts), (y_in, y_parts) = gather_points(x_packed, y_packed, y_rows)

    paired = near == 2 and near_count("src") == 1
    vectors = (f32(sb, blk), f32(tb, blk), f32(2, sb, blk))
    x, y, fixed, f, g, both = pl.pallas_call(
        functools.partial(first_kernel, x_parts, y_parts),
        out_shape=(
            jax.ShapeDtypeStruct((ntgt, sb, src_piece, width), jnp.bfloat16),
            jax.ShapeDtypeStruct((nsrc, tb, tgt_piece, width), jnp.bfloat16),
            f32(4, sb, blk),
        )
        + vectors,
        in_specs=[SMEM] * 3 + [VMEM] * (len(x_in) + len(y_in)),
        out_specs=(VMEM,) * 6,
        scratch_shapes=[
            pltpu.VMEM((2, blk // LANES, sb, LANES), jnp.float32),
            pltpu.VMEM((2, blk // LANES, tb, LANES), jnp.float32),
        ]
        + sweep_scratch(sb, tb, blk),
        compiler_params=PARAMS,
        name="first_sweep",
    )(src_counts, tgt_counts, pairs, *x_in, *y_in)

    step = pl.pallas_call(
        functools.partial(step_kernel, paired),
        out_shape=vectors,
        in_specs=[SMEM] + [VMEM] * 7,
        out_specs=(VMEM,) * 3,
        scratch_shapes=sweep_scratch(sb, tb, blk),
        compiler_params=PARAMS,
        name="sweep",
    )
    for _ in range(ITERS - 1):
        f, g, both = step(pairs, x, y, fixed, f, g, *exchange_both(both))
    tile = sb * src_piece + sb
    f, g, *near_parts = pl.pallas_call(
        functools.partial(project_kernel, near, paired),
        out_shape=(f32(sb, blk), f32(tb, blk)) + (f32(4, tile, width),) * near,
        in_specs=[SMEM] + [VMEM] * 7,
        out_specs=(VMEM,) * (2 + near),
        scratch_shapes=project_scratch(sb, tb, blk, width),
        compiler_params=PARAMS,
        name="project",
    )(pairs, x, y, fixed, f, g, *exchange_both(both))
    if near > 1:
        near_parts = near_parts[:1] + [swap(near_parts[d], "tgt", d) for d in range(1, near)]
    far_parts = pl.pallas_call(
        functools.partial(near_kernel, near, sb, src_piece),
        out_shape=(f32(tile, width),) * 4,
        in_specs=[VMEM] * near,
        out_specs=(VMEM,) * 4,
        scratch_shapes=[pltpu.VMEM((near, LANES, sb), jnp.float32)],
        compiler_params=PARAMS,
        name="merge_near",
    )(*near_parts)
    far_parts = [far_parts[0]] + [swap(far_parts[k], "tgt", near * k) for k in range(1, 4)]
    images = pl.pallas_call(
        functools.partial(far_kernel, sb, src_piece),
        out_shape=f32(sb, src_piece, width),
        in_specs=[VMEM] * 4,
        out_specs=VMEM,
        scratch_shapes=[pltpu.VMEM((4, LANES, sb), jnp.float32)],
        compiler_params=PARAMS,
        name="merge_far",
    )(*far_parts)

    src_final = lax.dynamic_slice_in_dim(f, lax.axis_index("tgt") * src_piece, src_piece, 1)
    tgt_final = lax.dynamic_slice_in_dim(g, lax.axis_index("src") * tgt_piece, tgt_piece, 1)
    return images, src_final, tgt_final


def solution(mesh):
    return jax.shard_map(
        on_device,
        mesh=mesh,
        in_specs=(
            P("src", "tgt", None),
            P("tgt", "src", None),
            P("src", "tgt"),
            P("tgt", "src"),
            P("src", "tgt"),
            P("tgt", "src"),
            P("src"),
            P("tgt"),
            P("src", "tgt"),
        ),
        out_specs=(P("src", "tgt", None), P("src", "tgt"), P("tgt", "src")),
        check_vma=False,
    )
```

```python
import functools
import math

import jax
import jax.numpy as jnp
from jax import lax
from jax.experimental import pallas as pl
from jax.experimental.pallas import tpu as pltpu
from jax.sharding import PartitionSpec as P

ITERS = 4
EPSILON = 0.1
UNIT = 1.0 / (EPSILON * math.log(2.0))
FLOOR = -1e30
LANES = 128
GROUP = 8
MOVE_GROUP = 4

SMEM = pl.BlockSpec(memory_space=pltpu.SMEM)
VMEM = pl.BlockSpec(memory_space=pltpu.VMEM)
PARAMS = pltpu.CompilerParams(vmem_limit_bytes=40 * 1024 * 1024)


def f32(*shape):
    return jax.ShapeDtypeStruct(shape, jnp.float32)


def swap(part, axis, mask):
    return lax.ppermute(part, axis, [(i, i ^ mask) for i in range(lax.axis_size(axis))])


def near_count(axis):
    return lax.axis_size(axis) // 4


def merge_lse(parts):
    top = functools.reduce(jnp.maximum, parts)
    return top + jnp.log2(sum(jnp.exp2(part - top) for part in parts))


def exchange_lse(part, axis):
    near = near_count(axis)
    if near > 1:
        part = merge_lse([part] + [swap(part, axis, d) for d in range(1, near)])
    return [part] + [swap(part, axis, near * k) for k in range(1, 4)]


def exchange_both(both):
    if near_count("tgt") != 2 or near_count("src") != 1:
        whole = jnp.stack([merge_lse(exchange_lse(both[0], "tgt")), merge_lse(exchange_lse(both[1], "src"))])
        return whole, whole
    odd = lax.rem(lax.axis_index("tgt"), 2) == 1
    other = swap(both, "tgt", 1)
    rows = merge_lse([both[0], other[0]])
    part = jnp.where(odd, jnp.stack([rows, rows]), jnp.stack([both[1], other[1]]))
    ntgt, nsrc = lax.axis_size("tgt"), lax.axis_size("src")

    def swap_far(k):
        pairs = [
            (s * ntgt + t, s * ntgt + (t ^ (2 * k)) if t % 2 else (s ^ k) * ntgt + t)
            for s in range(nsrc)
            for t in range(ntgt)
        ]
        return lax.ppermute(part, ("src", "tgt"), pairs)

    whole = merge_lse([part] + [swap_far(k) for k in range(1, 4)])
    return whole, swap(whole, "tgt", 1)


def gather_points(x_piece, y_piece, y_rows):
    nx, ny = near_count("tgt"), near_count("src")
    y_two = swap(y_piece, "src", 2 * ny)
    y_one, y_three = swap(y_piece, "src", ny), swap(y_piece, "src", 3 * ny)
    x_far = [swap(x_piece, "tgt", nx * k) for k in range(1, 4)]
    y_one, y_three, *x_far = lax.optimization_barrier((y_one, y_three, *x_far))
    y_found = [(0, 0, y_piece), (ny, 0, y_one), (2 * ny, 0, y_two), (3 * ny, 0, y_three)]
    x_found = [(0, 0, x_piece)] + [(nx * k, 0, x_far[k - 1]) for k in range(1, 4)]
    return spread_near(x_found, "tgt"), spread_near(y_found, "src")


def spread_near(found, axis):
    near = near_count(axis)
    arrays, parts = [], []
    for d in range(near):
        for mask, first, array in found:
            parts.append((mask ^ d, first, len(arrays), array.shape[0]))
            arrays.append(swap(array, axis, d) if d else array)
    return arrays, parts


def whole_block(ref, k):
    piece = ref[:, k]
    return piece.reshape(piece.shape[0] * piece.shape[1], piece.shape[2])


def split_columns(vec, split_ref):
    blocks, slots = vec.shape
    vec = vec * (1.0 / UNIT)
    parts = []
    for _ in range(3):
        part = vec.astype(jnp.bfloat16).astype(jnp.float32)
        parts.append(part)
        vec = vec - part
    parts.append(jnp.zeros((LANES - 3 * blocks, slots), jnp.float32))
    split_ref[...] = jnp.concatenate(parts, axis=0).T.astype(jnp.bfloat16)


def column_scores(stream_ref, q, split_ref, lane_ref, p):
    blocks = stream_ref.shape[1]
    lane = lax.broadcasted_iota(jnp.int32, (16, LANES), 1)
    pick = jnp.where((lane < 3 * blocks) & (lax.rem(lane, blocks) == q), 1.0, 0.0).astype(jnp.bfloat16)
    pick = jnp.concatenate([pick] * (split_ref.shape[0] // 16), axis=0)
    score = lax.dot_general(
        jnp.concatenate([whole_block(stream_ref, q), split_ref[...]], axis=1),
        jnp.concatenate([whole_block(lane_ref, p), pick], axis=1),
        (((1,), (1,)), ((), ())),
        preferred_element_type=jnp.float32,
    )
    return score, jnp.max(score, axis=0, keepdims=True)


def column_lse(*operands):
    score, peak = column_scores(*operands)
    return peak * UNIT, jnp.sum(jnp.exp2((score - peak) * UNIT), axis=0, keepdims=True)


def slots_of(tile, vec):
    found = vec[:, :LANES]
    for t in range(1, vec.shape[1] // LANES):
        found = jnp.where(tile == t, vec[:, t * LANES : (t + 1) * LANES], found)
    return found


def clear(peak_ref, sum_ref):
    peak_ref[...] = jnp.full(peak_ref.shape, FLOOR, jnp.float32)
    sum_ref[...] = jnp.zeros(sum_ref.shape, jnp.float32)


def merge_slots(peak_ref, sum_ref, count):
    shape = (count, peak_ref.shape[0] // count, peak_ref.shape[1])
    peak = peak_ref[...].reshape(shape)
    top = jnp.max(peak, axis=1, keepdims=True)
    total = jnp.sum(sum_ref[...].reshape(shape) * jnp.exp2(peak - top), axis=1)
    return top[:, 0] + jnp.log2(jnp.maximum(total, 1.0))


def visit_pairs(list_ref, tb, group, work):
    count = list_ref[0]

    @pl.loop(0, pl.cdiv(count, group))
    def _(step):
        places = [step * group + k for k in range(group)]
        codes = [list_ref[1 + place] for place in places]
        work([(code // tb, lax.rem(code, tb), place < count) for place, code in zip(places, codes)])


def sweep(list_ref, x_ref, y_ref, u, h, both_ref, scratch):
    u_split_ref, h_split_ref, rpeak_ref, rsum_ref, cpeak_ref, csum_ref = scratch
    sb, tb = x_ref.shape[1], y_ref.shape[1]
    split_columns(u, u_split_ref)
    split_columns(h, h_split_ref)
    clear(rpeak_ref, rsum_ref)
    clear(cpeak_ref, csum_ref)

    def work(pairs):
        found = []
        for p, q, _ in pairs:
            row = column_lse(y_ref, q, h_split_ref, x_ref, p)
            col = column_lse(x_ref, p, u_split_ref, y_ref, q)
            found.append((p, q, row, col))
        for p, q, row, col in found:
            rpeak_ref[pl.ds(p * tb + q, 1), :], rsum_ref[pl.ds(p * tb + q, 1), :] = row
            cpeak_ref[pl.ds(q * sb + p, 1), :], csum_ref[pl.ds(q * sb + p, 1), :] = col

    visit_pairs(list_ref, tb, GROUP, work)
    both_ref[0] = merge_slots(rpeak_ref, rsum_ref, sb)
    both_ref[1] = merge_slots(cpeak_ref, csum_ref, tb)


def half_sweep(list_ref, rows, x_ref, y_ref, vec, out_ref, scratch):
    split_ref, peak_ref, sum_ref = scratch
    sb, tb = x_ref.shape[1], y_ref.shape[1]
    split_columns(vec, split_ref)
    clear(peak_ref, sum_ref)

    def work(pairs):
        found = []
        for p, q, _ in pairs:
            if rows:
                found.append((p * tb + q, column_lse(y_ref, q, split_ref, x_ref, p)))
            else:
                found.append((q * sb + p, column_lse(x_ref, p, split_ref, y_ref, q)))
        for slot, pair in found:
            peak_ref[pl.ds(slot, 1), :], sum_ref[pl.ds(slot, 1), :] = pair

    visit_pairs(list_ref, tb, GROUP, work)
    out_ref[...] = merge_slots(peak_ref, sum_ref, sb if rows else tb)


def half_scratch(sb, tb, blk):
    return [
        pltpu.VMEM((blk, LANES), jnp.bfloat16),
        pltpu.VMEM((sb * tb, blk), jnp.float32),
        pltpu.VMEM((sb * tb, blk), jnp.float32),
    ]


def sweep_scratch(sb, tb, blk):
    return [
        pltpu.VMEM((blk, LANES), jnp.bfloat16),
        pltpu.VMEM((blk, LANES), jnp.bfloat16),
        pltpu.VMEM((sb * tb, blk), jnp.float32),
        pltpu.VMEM((sb * tb, blk), jnp.float32),
        pltpu.VMEM((sb * tb, blk), jnp.float32),
        pltpu.VMEM((sb * tb, blk), jnp.float32),
    ]


def project_scratch(sb, tb, blk, width):
    return [
        pltpu.VMEM((blk, LANES), jnp.bfloat16),
        pltpu.VMEM((tb, width, blk), jnp.bfloat16),
        pltpu.VMEM((sb + 1, 1, blk), jnp.float32),
        pltpu.VMEM((sb + 1, 1, blk), jnp.float32),
        pltpu.VMEM((sb + 1, width, blk), jnp.float32),
        pltpu.VMEM((sb, blk, width), jnp.float32),
    ]


def list_kernel(keep_ref, src_counts_ref, tgt_counts_ref, x_in_ref, y_in_ref, list_ref, x_ref, y_ref):
    sb, tb = keep_ref.shape
    x_ref[...] = x_in_ref[...]
    y_ref[...] = y_in_ref[...]
    n, last = jnp.int32(1), jnp.int32(0)
    for code in range(sb * tb):
        kept = keep_ref[code // tb, code % tb] > 0
        list_ref[n] = code
        n = n + kept.astype(jnp.int32)
        last = jnp.where(kept, code, last)
    for k in range(GROUP):
        list_ref[n + k] = last
    list_ref[0] = n - 1
    for k in range(sb):
        list_ref[1 + sb * tb + GROUP + k] = src_counts_ref[k]
    for k in range(tb):
        list_ref[1 + sb * tb + GROUP + sb + k] = tgt_counts_ref[k]


def assemble(place, list_ref, counts_at, parts, part_refs, points_ref, vec_ref):
    n, blocks, piece, width = points_ref.shape
    blk = n * piece
    vec_ref[...] = jnp.zeros(vec_ref.shape, jnp.float32)
    for mask, first, k, count in parts:
        owner = jnp.bitwise_xor(place, mask)
        rows = min(count, blocks * piece - first)
        points_ref[owner, first // piece : (first + rows) // piece] = part_refs[k][:rows].reshape(
            rows // piece, piece, width
        )
        if rows < count:
            vecs = part_refs[k][rows:count].astype(jnp.float32)
            tile = owner * piece // LANES
            vec_ref[0, tile] += vecs[:blocks]
            vec_ref[1, tile] += vecs[blocks:]
    mass = jnp.concatenate([vec_ref[0, t] for t in range(blk // LANES)], axis=1)
    potential = jnp.concatenate([vec_ref[1, t] for t in range(blk // LANES)], axis=1) * UNIT
    block_of = lax.broadcasted_iota(jnp.int32, (blocks, blk), 0)
    slot_of = lax.broadcasted_iota(jnp.int32, (blocks, blk), 1)
    half = jnp.zeros((blocks, blk), jnp.float32)
    count = jnp.zeros((blocks, blk), jnp.int32)
    ones = jnp.ones((blocks, width), jnp.bfloat16)
    for k in range(blocks):
        wide = whole_block(points_ref, k).astype(jnp.float32)
        square = wide * wide
        high = square.astype(jnp.bfloat16)
        low = (square - high.astype(jnp.float32)).astype(jnp.bfloat16)
        norm = sum(
            lax.dot_general(ones, part, (((1,), (1,)), ((), ())), preferred_element_type=jnp.float32)
            for part in (high, low)
        )
        half = jnp.where(block_of == k, norm * (0.5 * UNIT), half)
        count = jnp.where(block_of == k, list_ref[counts_at + k], count)
    base = jnp.where(slot_of < count, jnp.log2(mass) - half, FLOOR)
    return potential, half, base


def first_kernel(x_parts, y_parts, list_ref, *refs):
    nx = 1 + max(part[2] for part in x_parts)
    ny = 1 + max(part[2] for part in y_parts)
    x_in, y_in, refs = refs[:nx], refs[nx : nx + ny], refs[nx + ny :]
    x_ref, y_ref, fixed_ref, f_ref, g_ref, both_ref, xvec_ref, yvec_ref = refs[:8]
    sb, tb = x_ref.shape[1], y_ref.shape[1]
    counts_at = 1 + sb * tb + GROUP
    f, x_half, x_base = assemble(lax.axis_index("tgt"), list_ref, counts_at, x_parts, x_in, x_ref, xvec_ref)
    g, y_half, y_base = assemble(lax.axis_index("src"), list_ref, counts_at + sb, y_parts, y_in, y_ref, yvec_ref)
    f_ref[...] = f
    g_ref[...] = g
    for k, vec in enumerate((x_half, x_base, y_half, y_base)):
        fixed_ref[k] = vec
    sweep(list_ref, x_ref, y_ref, f + x_base, g + y_base, both_ref, refs[8:])


def chosen(whole_ref, other_ref, paired):
    if not paired:
        return whole_ref[0], whole_ref[1]
    odd = lax.rem(lax.axis_index("tgt"), 2) == 1
    return jnp.where(odd, whole_ref[0], other_ref[0]), jnp.where(odd, other_ref[1], whole_ref[0])


def updated(f, g, fixed_ref, whole_ref, other_ref, paired):
    rows, cols = chosen(whole_ref, other_ref, paired)
    return 0.5 * (f + (fixed_ref[0] - rows)), 0.5 * (g + (fixed_ref[2] - cols))


def step_kernel(paired, list_ref, x_ref, y_ref, fixed_ref, f_in_ref, g_in_ref, whole_ref, other_ref, *refs):
    f_ref, g_ref, both_ref = refs[:3]
    f, g = updated(f_in_ref[...], g_in_ref[...], fixed_ref, whole_ref, other_ref, paired)
    f_ref[...] = f
    g_ref[...] = g
    sweep(list_ref, x_ref, y_ref, f + fixed_ref[1], g + fixed_ref[3], both_ref, refs[3:])


def last_cols_kernel(
    paired, list_ref, x_ref, y_ref, fixed_ref, f_in_ref, g_in_ref, whole_ref, other_ref, f_ref, g_ref, cols_ref, *refs
):
    f, g = updated(f_in_ref[...], g_in_ref[...], fixed_ref, whole_ref, other_ref, paired)
    f_ref[...] = f
    g_ref[...] = g
    half_sweep(list_ref, False, x_ref, y_ref, f + fixed_ref[1], cols_ref, refs)


def last_rows_kernel(list_ref, x_ref, y_ref, fixed_ref, g_ref, rows_ref, *refs):
    half_sweep(list_ref, True, x_ref, y_ref, g_ref[...] + fixed_ref[3], rows_ref, refs)


def project_kernel(near, list_ref, x_ref, y_ref, fixed_ref, g_in_ref, rows_ref, *refs):
    col_refs, g_ref, out_refs = refs[:4], refs[4], refs[5 : 5 + near]
    split_ref, turned_ref, peak_ref, sum_ref, acc_ref, image_ref = refs[5 + near :]
    n, sb, piece, width = x_ref.shape
    tb = y_ref.shape[1]
    blk = n * piece
    g = 0.5 * (g_in_ref[...] + (fixed_ref[2] - merge_lse([ref[...] for ref in col_refs])))
    g_ref[...] = g * (1.0 / UNIT)
    split_columns(g + fixed_ref[3], split_ref)
    for q in range(tb):
        turned_ref[q] = whole_block(y_ref, q).T
    clear(peak_ref, sum_ref)
    acc_ref[...] = jnp.zeros(acc_ref.shape, jnp.float32)

    def move(pairs):
        found = []
        for p, q, real in pairs:
            score, peak = column_scores(y_ref, q, split_ref, x_ref, p)
            weights = jnp.exp2((score - peak) * UNIT)
            high = weights.astype(jnp.bfloat16)
            low = (weights - high.astype(jnp.float32)).astype(jnp.bfloat16)
            ys = turned_ref[q]
            moved = jnp.dot(ys, high, preferred_element_type=jnp.float32) + jnp.dot(
                ys, low, preferred_element_type=jnp.float32
            )
            found.append((jnp.where(real, p, sb), peak * UNIT, jnp.sum(weights, axis=0, keepdims=True), moved))
        for p, peak, total, moved in found:
            old = peak_ref[p]
            new = jnp.maximum(old, peak)
            before, here = jnp.exp2(old - new), jnp.exp2(peak - new)
            peak_ref[p] = new
            sum_ref[p] = sum_ref[p] * before + total * here
            acc_ref[p] = acc_ref[p] * before + moved * here

    visit_pairs(list_ref, tb, MOVE_GROUP, move)
    rows = []
    for p in range(sb):
        total = jnp.maximum(sum_ref[p], 1.0)
        image_ref[p] = (acc_ref[p] / total).T
        rows.append(peak_ref[p] + jnp.log2(total))
    lse = jnp.concatenate(rows, axis=0)

    me = lax.rem(lax.axis_index("tgt"), near)
    for e, out_ref in enumerate(out_refs):
        for far in range(4):
            owner = far * near + jnp.bitwise_xor(me, e)
            for p in range(sb):
                out_ref[far, p * piece : (p + 1) * piece] = image_ref[p, pl.ds(pl.multiple_of(owner * piece, piece), piece)]
            tile = owner * piece // LANES
            out_ref[far, sb * piece : sb * (piece + 1)] = slots_of(tile, lse)
            out_ref[far, sb * (piece + 1) :] = slots_of(tile, rows_ref[...])


def merge_images(parts, offset, sb, piece, turn_ref):
    whole = merge_lse([lse for _, lse in parts])
    weights = []
    for k, (_, lse) in enumerate(parts):
        turn_ref[k] = jnp.exp2(lse - whole).T
        weights.append(turn_ref[k, pl.ds(offset, piece), :])
    images = []
    for p in range(sb):
        images.append(
            sum(
                image[p * piece : (p + 1) * piece] * weight[:, p : p + 1]
                for (image, _), weight in zip(parts, weights)
            )
        )
    return images, whole


def near_kernel(near, sb, piece, *refs):
    in_refs, out_refs, turn_ref = refs[:near], refs[near : near + 4], refs[near + 4]
    place = lax.axis_index("tgt")
    me, mine = lax.rem(place, near), place // near
    rows = sb * piece
    for d, out_ref in enumerate(out_refs):
        far = jnp.bitwise_xor(mine, d)
        offset = lax.rem((far * near + me) * piece, LANES)
        parts = [(ref[far, :rows], ref[far, rows : rows + sb]) for ref in in_refs]
        images, whole = merge_images(parts, pl.multiple_of(offset, piece), sb, piece, turn_ref)
        for p in range(sb):
            out_ref[p * piece : (p + 1) * piece] = images[p]
        out_ref[rows : rows + sb] = whole
        out_ref[rows + sb :] = merge_lse([ref[far, rows + sb :] for ref in in_refs])


def far_kernel(sb, piece, fixed_ref, f_in_ref, *refs):
    in_refs, out_ref, f_ref, turn_ref = refs[:4], refs[4], refs[5], refs[6]
    rows = sb * piece
    start = lax.axis_index("tgt") * piece
    offset = lax.rem(start, LANES)
    parts = [(ref[:rows], ref[rows : rows + sb]) for ref in in_refs]
    images, _ = merge_images(parts, pl.multiple_of(offset, piece), sb, piece, turn_ref)
    for p in range(sb):
        out_ref[p] = images[p]
    tile = start // LANES
    lse = merge_lse([ref[rows + sb :] for ref in in_refs])
    f = 0.5 * (slots_of(tile, f_in_ref[...]) + (slots_of(tile, fixed_ref[0]) - lse))
    f_ref[...] = pltpu.roll(f * (1.0 / UNIT), lax.rem(LANES - offset, LANES), 1)[:, :piece]


def pack_kernel(*refs):
    for k, axis in enumerate(("tgt", "src")):
        points_ref, mass_ref, potential_ref = refs[3 * k : 3 * k + 3]
        out_ref = refs[6 + k]
        blocks, piece, width = points_ref.shape
        here = lax.rem(lax.axis_index(axis) * piece, LANES)
        slot = lax.broadcasted_iota(jnp.int32, (piece, LANES), 0)
        lane = lax.broadcasted_iota(jnp.int32, (piece, LANES), 1)
        put = jnp.where(lane == slot + here, 1.0, 0.0).astype(jnp.bfloat16)
        vecs = [jnp.dot(ref[...], put, preferred_element_type=jnp.float32) for ref in (mass_ref, potential_ref)]
        out_ref[: blocks * piece] = points_ref[...].reshape(blocks * piece, width)
        out_ref[blocks * piece :] = jnp.concatenate(vecs, axis=0).astype(jnp.bfloat16)


def on_device(
    src_points, tgt_points, src_mass, tgt_mass, src_potential, tgt_potential, src_counts, tgt_counts, keep
):
    ntgt, nsrc = lax.axis_size("tgt"), lax.axis_size("src")
    near = near_count("tgt")
    sb, src_piece, width = src_points.shape
    tb, tgt_piece, _ = tgt_points.shape
    blk = src_piece * ntgt
    x_rows, y_rows = sb * src_piece, tb * tgt_piece
    x_packed, y_packed = pl.pallas_call(
        pack_kernel,
        out_shape=(
            jax.ShapeDtypeStruct((x_rows + 2 * sb, width), jnp.bfloat16),
            jax.ShapeDtypeStruct((y_rows + 2 * tb, width), jnp.bfloat16),
        ),
        in_specs=[VMEM] * 6,
        out_specs=(VMEM, VMEM),
        name="pack",
    )(src_points, src_mass, src_potential, tgt_points, tgt_mass, tgt_potential)
    (x_in, x_parts), (y_in, y_parts) = gather_points(x_packed, y_packed, y_rows)
    pairs, x_own, y_own = pl.pallas_call(
        list_kernel,
        out_shape=(
            jax.ShapeDtypeStruct((1 + sb * tb + GROUP + sb + tb,), jnp.int32),
            jax.ShapeDtypeStruct(x_packed.shape, x_packed.dtype),
            jax.ShapeDtypeStruct(y_packed.shape, y_packed.dtype),
        ),
        in_specs=[SMEM] * 3 + [VMEM] * 2,
        out_specs=(SMEM, VMEM, VMEM),
        compiler_params=PARAMS,
        name="kept_pairs",
    )(keep, src_counts, tgt_counts, x_packed, y_packed)
    x_in[0], y_in[0] = x_own, y_own

    paired = near == 2 and near_count("src") == 1
    vectors = (f32(sb, blk), f32(tb, blk), f32(2, sb, blk))
    x, y, fixed, f, g, both = pl.pallas_call(
        functools.partial(first_kernel, x_parts, y_parts),
        out_shape=(
            jax.ShapeDtypeStruct((ntgt, sb, src_piece, width), jnp.bfloat16),
            jax.ShapeDtypeStruct((nsrc, tb, tgt_piece, width), jnp.bfloat16),
            f32(4, sb, blk),
        )
        + vectors,
        in_specs=[SMEM] + [VMEM] * (len(x_in) + len(y_in)),
        out_specs=(VMEM,) * 6,
        scratch_shapes=[
            pltpu.VMEM((2, blk // LANES, sb, LANES), jnp.float32),
            pltpu.VMEM((2, blk // LANES, tb, LANES), jnp.float32),
        ]
        + sweep_scratch(sb, tb, blk),
        compiler_params=PARAMS,
        name="first_sweep",
    )(pairs, *x_in, *y_in)

    step = pl.pallas_call(
        functools.partial(step_kernel, paired),
        out_shape=vectors,
        in_specs=[SMEM] + [VMEM] * 7,
        out_specs=(VMEM,) * 3,
        scratch_shapes=sweep_scratch(sb, tb, blk),
        compiler_params=PARAMS,
        name="sweep",
    )
    for _ in range(ITERS - 2):
        f, g, both = step(pairs, x, y, fixed, f, g, *exchange_both(both))

    f, g, cols = pl.pallas_call(
        functools.partial(last_cols_kernel, paired),
        out_shape=(f32(sb, blk), f32(tb, blk), f32(tb, blk)),
        in_specs=[SMEM] + [VMEM] * 7,
        out_specs=(VMEM,) * 3,
        scratch_shapes=half_scratch(sb, tb, blk),
        compiler_params=PARAMS,
        name="last_cols",
    )(pairs, x, y, fixed, f, g, *exchange_both(both))
    col_parts = exchange_lse(cols, "src")
    rows = pl.pallas_call(
        last_rows_kernel,
        out_shape=f32(sb, blk),
        in_specs=[SMEM] + [VMEM] * 4,
        out_specs=VMEM,
        scratch_shapes=half_scratch(sb, tb, blk),
        compiler_params=PARAMS,
        name="last_rows",
    )(pairs, x, y, fixed, g)
    rows, *col_parts = lax.optimization_barrier((rows, *col_parts))
    tile = sb * (src_piece + 2)
    g, *near_parts = pl.pallas_call(
        functools.partial(project_kernel, near),
        out_shape=(f32(tb, blk),) + (f32(4, tile, width),) * near,
        in_specs=[SMEM] + [VMEM] * 9,
        out_specs=(VMEM,) * (1 + near),
        scratch_shapes=project_scratch(sb, tb, blk, width),
        compiler_params=PARAMS,
        name="project",
    )(pairs, x, y, fixed, g, rows, *col_parts)
    if near > 1:
        near_parts = near_parts[:1] + [swap(near_parts[d], "tgt", d) for d in range(1, near)]
    far_parts = pl.pallas_call(
        functools.partial(near_kernel, near, sb, src_piece),
        out_shape=(f32(tile, width),) * 4,
        in_specs=[VMEM] * near,
        out_specs=(VMEM,) * 4,
        scratch_shapes=[pltpu.VMEM((near, LANES, sb), jnp.float32)],
        compiler_params=PARAMS,
        name="merge_near",
    )(*near_parts)
    far_parts = [far_parts[0]] + [swap(far_parts[k], "tgt", near * k) for k in range(1, 4)]
    images, src_final = pl.pallas_call(
        functools.partial(far_kernel, sb, src_piece),
        out_shape=(f32(sb, src_piece, width), f32(sb, src_piece)),
        in_specs=[VMEM] * 6,
        out_specs=(VMEM, VMEM),
        scratch_shapes=[pltpu.VMEM((4, LANES, sb), jnp.float32)],
        compiler_params=PARAMS,
        name="merge_far",
    )(fixed, f, *far_parts)

    tgt_final = lax.dynamic_slice_in_dim(g, lax.axis_index("src") * tgt_piece, tgt_piece, 1)
    return images, src_final, tgt_final


def solution(mesh):
    return jax.shard_map(
        on_device,
        mesh=mesh,
        in_specs=(
            P("src", "tgt", None),
            P("tgt", "src", None),
            P("src", "tgt"),
            P("tgt", "src"),
            P("src", "tgt"),
            P("tgt", "src"),
            P("src"),
            P("tgt"),
            P("src", "tgt"),
        ),
        out_specs=(P("src", "tgt", None), P("src", "tgt"), P("tgt", "src")),
        check_vma=False,
    )
```

```python
import functools
import math

import jax
import jax.numpy as jnp
from jax import lax
from jax.experimental import pallas as pl
from jax.experimental.pallas import tpu as pltpu
from jax.sharding import PartitionSpec as P

ITERS = 4
EPSILON = 0.1
UNIT = 1.0 / (EPSILON * math.log(2.0))
FLOOR = -1e30
LANES = 128
GROUP = 16
MOVE_GROUP = 4

SMEM = pl.BlockSpec(memory_space=pltpu.SMEM)
VMEM = pl.BlockSpec(memory_space=pltpu.VMEM)
PARAMS = pltpu.CompilerParams(vmem_limit_bytes=40 * 1024 * 1024)


def f32(*shape):
    return jax.ShapeDtypeStruct(shape, jnp.float32)


def swap(part, axis, mask):
    return lax.ppermute(part, axis, [(i, i ^ mask) for i in range(lax.axis_size(axis))])


def near_count(axis):
    return lax.axis_size(axis) // 4


def merge_lse(parts):
    top = functools.reduce(jnp.maximum, parts)
    return top + jnp.log2(sum(jnp.exp2(part - top) for part in parts))


def exchange_lse(part, axis):
    near = near_count(axis)
    if near > 1:
        part = merge_lse([part] + [swap(part, axis, d) for d in range(1, near)])
    return [part] + [swap(part, axis, near * k) for k in range(1, 4)]


def shared_rows():
    return near_count("tgt") == 2 and near_count("src") == 1


def is_odd():
    return lax.rem(lax.axis_index("tgt"), 2) == 1


def exchange_plain(part, sb):
    return jnp.concatenate([merge_lse(exchange_lse(part[:sb], "tgt")), merge_lse(exchange_lse(part[sb:], "src"))])


def exchange_first(part, sb):
    other = swap(part, "tgt", 1)
    rows = merge_lse([part[:sb], other[:sb]])
    return exchange_shared(jnp.where(is_odd(), padded(rows, part), jnp.concatenate([part[sb:], other[sb:]])))


def padded(rows, part):
    return jnp.concatenate([rows] * (part.shape[0] // rows.shape[0]))


def exchange_shared(part):
    ntgt, nsrc = lax.axis_size("tgt"), lax.axis_size("src")

    def swap_far(k):
        pairs = [
            (s * ntgt + t, s * ntgt + (t ^ (2 * k)) if t % 2 else (s ^ k) * ntgt + t)
            for s in range(nsrc)
            for t in range(ntgt)
        ]
        return lax.ppermute(part, ("src", "tgt"), pairs)

    whole = merge_lse([part] + [swap_far(k) for k in range(1, 4)])
    return whole, swap(whole, "tgt", 1)


def gather_points(x_piece, y_piece, y_rows):
    nx, ny = near_count("tgt"), near_count("src")
    y_two = swap(y_piece, "src", 2 * ny)
    y_one, y_three = swap(y_piece, "src", ny), swap(y_piece, "src", 3 * ny)
    x_far = [swap(x_piece, "tgt", nx * k) for k in range(1, 4)]
    y_one, y_three, *x_far = lax.optimization_barrier((y_one, y_three, *x_far))
    y_found = [(0, 0, y_piece), (ny, 0, y_one), (2 * ny, 0, y_two), (3 * ny, 0, y_three)]
    x_found = [(0, 0, x_piece)] + [(nx * k, 0, x_far[k - 1]) for k in range(1, 4)]
    return spread_near(x_found, "tgt"), spread_near(y_found, "src")


def spread_near(found, axis):
    near = near_count(axis)
    arrays, parts = [], []
    for d in range(near):
        for mask, first, array in found:
            parts.append((mask ^ d, first, len(arrays), array.shape[0]))
            arrays.append(swap(array, axis, d) if d else array)
    return arrays, parts


def whole_block(ref, k):
    piece = ref[:, k]
    return piece.reshape(piece.shape[0] * piece.shape[1], piece.shape[2])


def split_columns(vec, split_ref):
    blocks, slots = vec.shape
    vec = vec * (1.0 / UNIT)
    parts = []
    for _ in range(3):
        part = vec.astype(jnp.bfloat16).astype(jnp.float32)
        parts.append(part)
        vec = vec - part
    parts.append(jnp.zeros((LANES - 3 * blocks, slots), jnp.float32))
    split_ref[...] = jnp.concatenate(parts, axis=0).T.astype(jnp.bfloat16)


def column_scores(stream_ref, q, split_ref, blocks, k, lane_ref, p):
    lane = lax.broadcasted_iota(jnp.int32, (16, LANES), 1)
    pick = jnp.where((lane < 3 * blocks) & (lax.rem(lane, blocks) == k), 1.0, 0.0).astype(jnp.bfloat16)
    pick = jnp.concatenate([pick] * (split_ref.shape[0] // 16), axis=0)
    score = lax.dot_general(
        jnp.concatenate([whole_block(stream_ref, q), split_ref[...]], axis=1),
        jnp.concatenate([whole_block(lane_ref, p), pick], axis=1),
        (((1,), (1,)), ((), ())),
        preferred_element_type=jnp.float32,
    )
    return score, jnp.max(score, axis=0, keepdims=True)


def column_lse(*operands):
    score, peak = column_scores(*operands)
    return peak * UNIT, jnp.sum(jnp.exp2((score - peak) * UNIT), axis=0, keepdims=True)


def slots_of(tile, vec):
    found = vec[:, :LANES]
    for t in range(1, vec.shape[1] // LANES):
        found = jnp.where(tile == t, vec[:, t * LANES : (t + 1) * LANES], found)
    return found


def clear(peak_ref, sum_ref):
    peak_ref[...] = jnp.full(peak_ref.shape, FLOOR, jnp.float32)
    sum_ref[...] = jnp.zeros(sum_ref.shape, jnp.float32)


def merge_slots(peak, total, count):
    shape = (count, peak.shape[0] // count, peak.shape[1])
    peak = peak.reshape(shape)
    top = jnp.max(peak, axis=1, keepdims=True)
    total = jnp.sum(total.reshape(shape) * jnp.exp2(peak - top), axis=1)
    return top[:, 0] + jnp.log2(jnp.maximum(total, 1.0))


def pair_list(tb, list_ref, other_ref=None):
    own = list_ref[0]
    count = own if other_ref is None else own + other_ref[0]

    def pair(place):
        place = jnp.minimum(place, count - 1)
        if other_ref is None:
            code, shift = list_ref[1 + place], 0
        else:
            mine = place < own
            here, there = list_ref[1 + jnp.where(mine, place, 0)], other_ref[1 + jnp.where(mine, 0, place - own)]
            code = jnp.where(mine, here, there)
            shift = jnp.where(mine, 0, tb)
        return code // tb, lax.rem(code, tb) + shift

    return count, pair


def visit_pairs(pairs, first, last, group, work):
    count, pair = pairs

    @pl.loop(0, pl.cdiv(last - first, group))
    def _(step):
        places = [first + step * group + k for k in range(group)]
        work([pair(place) + (place < count,) for place in places])


def half_sweep(pairs, rows, x_ref, y_ref, tb, vec, scratch):
    split_ref, peak_ref, sum_ref = scratch
    sb = x_ref.shape[1]
    used = sb * tb
    split_columns(vec, split_ref)
    clear(peak_ref, sum_ref)

    def work(group):
        found = []
        for p, q, _ in group:
            if rows:
                found.append((p * tb + q, column_lse(y_ref, q, split_ref, tb, q, x_ref, p)))
            else:
                found.append((q * sb + p, column_lse(x_ref, p, split_ref, sb, p, y_ref, q)))
        for slot, pair in found:
            peak_ref[pl.ds(slot, 1), :], sum_ref[pl.ds(slot, 1), :] = pair

    count = pairs[0]
    rest = lax.rem(count, GROUP)
    large = jnp.where(rest > GROUP // 2, count, count - rest)
    visit_pairs(pairs, 0, large, GROUP, work)
    visit_pairs(pairs, large, count, GROUP // 4, work)
    return merge_slots(peak_ref[:used], sum_ref[:used], sb if rows else tb)


def half_scratch(sb, tb, blk):
    return [
        pltpu.VMEM((blk, LANES), jnp.bfloat16),
        pltpu.VMEM((sb * tb, blk), jnp.float32),
        pltpu.VMEM((sb * tb, blk), jnp.float32),
    ]


def sweep_own(pairs, x_ref, y_ref, u, h, part_ref, scratch):
    sb, tb = u.shape[0], h.shape[0]
    part_ref[:sb] = half_sweep(pairs, True, x_ref, y_ref, tb, h, scratch)
    part_ref[sb:] = half_sweep(pairs, False, x_ref, y_ref, tb, u, scratch)


def sweep_shared(pairs, x_ref, y_ref, u, h, part_ref, scratch):
    sb, tb = u.shape[0], h.shape[0]
    odd = is_odd()

    @pl.when(odd)
    def _():
        part_ref[...] = padded(half_sweep(pairs, True, x_ref, y_ref, tb, h, scratch), part_ref)

    @pl.when(jnp.logical_not(odd))
    def _():
        part_ref[...] = half_sweep(pairs, False, x_ref, y_ref, tb, u, scratch)


def project_scratch(sb, tb, blk, width):
    return [
        pltpu.VMEM((blk, LANES), jnp.bfloat16),
        pltpu.VMEM((tb, width, blk), jnp.bfloat16),
        pltpu.VMEM((sb + 1, 1, blk), jnp.float32),
        pltpu.VMEM((sb + 1, 1, blk), jnp.float32),
        pltpu.VMEM((sb + 1, width, blk), jnp.float32),
        pltpu.VMEM((sb, blk, width), jnp.float32),
    ]


def list_kernel(keep_ref, src_counts_ref, tgt_counts_ref, x_in_ref, y_in_ref, list_ref, x_ref, y_ref):
    sb, tb = keep_ref.shape
    x_ref[...] = x_in_ref[...]
    y_ref[...] = y_in_ref[...]
    counts_at = 1 + sb * tb
    n = jnp.int32(0)
    for code in range(sb * tb):
        list_ref[1 + n] = code
        n = n + (keep_ref[code // tb, code % tb] > 0).astype(jnp.int32)
    list_ref[0] = n
    for k in range(sb):
        list_ref[counts_at + k] = src_counts_ref[k]
    for k in range(tb):
        list_ref[counts_at + sb + k] = tgt_counts_ref[k]


def assemble(place, list_ref, counts_at, parts, part_refs, points_ref, vec_ref):
    n, blocks, piece, width = points_ref.shape
    blk = n * piece
    vec_ref[...] = jnp.zeros(vec_ref.shape, jnp.float32)
    for mask, first, k, count in parts:
        owner = jnp.bitwise_xor(place, mask)
        rows = min(count, blocks * piece - first)
        points_ref[owner, first // piece : (first + rows) // piece] = part_refs[k][:rows].reshape(
            rows // piece, piece, width
        )
        if rows < count:
            vecs = part_refs[k][rows:count].astype(jnp.float32)
            tile = owner * piece // LANES
            vec_ref[0, tile] += vecs[:blocks]
            vec_ref[1, tile] += vecs[blocks:]
    mass = jnp.concatenate([vec_ref[0, t] for t in range(blk // LANES)], axis=1)
    potential = jnp.concatenate([vec_ref[1, t] for t in range(blk // LANES)], axis=1) * UNIT
    block_of = lax.broadcasted_iota(jnp.int32, (blocks, blk), 0)
    slot_of = lax.broadcasted_iota(jnp.int32, (blocks, blk), 1)
    half = jnp.zeros((blocks, blk), jnp.float32)
    count = jnp.zeros((blocks, blk), jnp.int32)
    ones = jnp.ones((blocks, width), jnp.bfloat16)
    for k in range(blocks):
        wide = whole_block(points_ref, k).astype(jnp.float32)
        square = wide * wide
        high = square.astype(jnp.bfloat16)
        low = (square - high.astype(jnp.float32)).astype(jnp.bfloat16)
        norm = sum(
            lax.dot_general(ones, part, (((1,), (1,)), ((), ())), preferred_element_type=jnp.float32)
            for part in (high, low)
        )
        half = jnp.where(block_of == k, norm * (0.5 * UNIT), half)
        count = jnp.where(block_of == k, list_ref[counts_at + k], count)
    base = jnp.where(slot_of < count, jnp.log2(mass) - half, FLOOR)
    return potential, half, base


def first_kernel(x_parts, y_parts, list_ref, *refs):
    nx = 1 + max(part[2] for part in x_parts)
    ny = 1 + max(part[2] for part in y_parts)
    x_in, y_in, refs = refs[:nx], refs[nx : nx + ny], refs[nx + ny :]
    x_ref, y_ref, xfixed_ref, yfixed_ref, f_ref, part_ref, xvec_ref, yvec_ref = refs[:8]
    sb, tb = x_ref.shape[1], y_ref.shape[1]
    counts_at = 1 + sb * tb
    f, x_half, x_base = assemble(lax.axis_index("tgt"), list_ref, counts_at, x_parts, x_in, x_ref, xvec_ref)
    g, y_half, y_base = assemble(lax.axis_index("src"), list_ref, counts_at + sb, y_parts, y_in, y_ref, yvec_ref)
    f_ref[...] = f
    xfixed_ref[0], xfixed_ref[1] = x_half, x_base
    yfixed_ref[0], yfixed_ref[1], yfixed_ref[2] = y_half, y_base, g
    sweep_own(pair_list(tb, list_ref), x_ref, y_ref, f + x_base, g + y_base, part_ref, refs[8:])


def updated(old, half, lse):
    return 0.5 * (old + (half - lse))


def chosen(sb, tb, whole_ref, other_ref):
    odd = is_odd()
    cols = jnp.concatenate([other_ref[tb:], other_ref[:tb]])
    return jnp.where(odd, whole_ref[:sb], other_ref[:sb]), jnp.where(odd, cols, whole_ref[...])


def second_kernel(list_ref, list2_ref, x_ref, y1_ref, y2_ref, xfixed_ref, yfixed1_ref, yfixed2_ref, f_in_ref, *refs):
    whole_ref, other_ref, y_ref, yfixed_ref, f_ref, part_ref = refs[:6]
    sb, tb = x_ref.shape[1], y1_ref.shape[1]
    y_ref[:, :tb] = y1_ref[...]
    y_ref[:, tb:] = y2_ref[...]
    rows, cols = chosen(sb, tb, whole_ref, other_ref)
    f = updated(f_in_ref[...], xfixed_ref[0], rows)
    half, base, g = [jnp.concatenate([yfixed1_ref[k], yfixed2_ref[k]]) for k in range(3)]
    g = updated(g, half, cols)
    f_ref[...] = f
    yfixed_ref[0], yfixed_ref[1], yfixed_ref[2] = half, base, g
    sweep_shared(pair_list(tb, list_ref, list2_ref), x_ref, y_ref, f + xfixed_ref[1], g + base, part_ref, refs[6:])


def step_kernel(shared, *refs):
    lists, refs = refs[: 1 + shared], refs[1 + shared :]
    x_ref, y_ref, xfixed_ref, yfixed_in_ref, f_in_ref = refs[:5]
    sums, refs = refs[5 : 6 + shared], refs[6 + shared :]
    yfixed_ref, f_ref, part_ref = refs[:3]
    sb, held = x_ref.shape[1], y_ref.shape[1]
    tb = held // (1 + shared)
    rows, cols = chosen(sb, tb, *sums) if shared else (sums[0][:sb], sums[0][sb:])
    f = updated(f_in_ref[...], xfixed_ref[0], rows)
    half, base, g = [yfixed_in_ref[k] for k in range(3)]
    g = updated(g, half, cols)
    f_ref[...] = f
    yfixed_ref[0], yfixed_ref[1], yfixed_ref[2] = half, base, g
    sweep = sweep_shared if shared else sweep_own
    sweep(pair_list(tb, *lists), x_ref, y_ref, f + xfixed_ref[1], g + base, part_ref, refs[3:])


def last_cols_kernel(shared, list_ref, x_ref, y_ref, xfixed_ref, yfixed_in_ref, f_in_ref, *refs):
    sums, refs = refs[: 1 + shared], refs[1 + shared :]
    yfixed_ref, f_ref, cols_ref = refs[:3]
    sb, tb = x_ref.shape[1], cols_ref.shape[0]
    rows, cols = chosen(sb, tb, *sums) if shared else (sums[0][:sb], sums[0][sb:])
    f = updated(f_in_ref[...], xfixed_ref[0], rows)
    half, base, g = [yfixed_in_ref[k, :tb] for k in range(3)]
    f_ref[...] = f
    yfixed_ref[0], yfixed_ref[1], yfixed_ref[2] = half, base, updated(g, half, cols[:tb])
    cols_ref[...] = half_sweep(pair_list(tb, list_ref), False, x_ref, y_ref, tb, f + xfixed_ref[1], refs[3:])


def last_rows_kernel(list_ref, x_ref, y_ref, yfixed_ref, rows_ref, *scratch):
    tb = yfixed_ref.shape[1]
    vec = yfixed_ref[2] + yfixed_ref[1]
    rows_ref[...] = half_sweep(pair_list(tb, list_ref), True, x_ref, y_ref, tb, vec, scratch)


def project_kernel(near, list_ref, x_ref, y_ref, yfixed_ref, rows_ref, *refs):
    col_refs, g_ref, out_refs = refs[:4], refs[4], refs[5 : 5 + near]
    split_ref, turned_ref, peak_ref, sum_ref, acc_ref, image_ref = refs[5 + near :]
    n, sb, piece, width = x_ref.shape
    tb = g_ref.shape[0]
    blk = n * piece
    g = updated(yfixed_ref[2], yfixed_ref[0], merge_lse([ref[...] for ref in col_refs]))
    g_ref[...] = g * (1.0 / UNIT)
    split_columns(g + yfixed_ref[1], split_ref)
    for q in range(tb):
        turned_ref[q] = whole_block(y_ref, q).T
    clear(peak_ref, sum_ref)
    acc_ref[...] = jnp.zeros(acc_ref.shape, jnp.float32)

    def move(group):
        found = []
        for p, q, real in group:
            score, peak = column_scores(y_ref, q, split_ref, tb, q, x_ref, p)
            weights = jnp.exp2((score - peak) * UNIT)
            high = weights.astype(jnp.bfloat16)
            low = (weights - high.astype(jnp.float32)).astype(jnp.bfloat16)
            ys = turned_ref[q]
            moved = jnp.dot(ys, high, preferred_element_type=jnp.float32) + jnp.dot(
                ys, low, preferred_element_type=jnp.float32
            )
            found.append((jnp.where(real, p, sb), peak * UNIT, jnp.sum(weights, axis=0, keepdims=True), moved))
        for p, peak, total, moved in found:
            old = peak_ref[p]
            new = jnp.maximum(old, peak)
            before, here = jnp.exp2(old - new), jnp.exp2(peak - new)
            peak_ref[p] = new
            sum_ref[p] = sum_ref[p] * before + total * here
            acc_ref[p] = acc_ref[p] * before + moved * here

    pairs = pair_list(tb, list_ref)
    visit_pairs(pairs, 0, pairs[0], MOVE_GROUP, move)
    rows = []
    for p in range(sb):
        total = jnp.maximum(sum_ref[p], 1.0)
        image_ref[p] = (acc_ref[p] / total).T
        rows.append(peak_ref[p] + jnp.log2(total))
    lse = jnp.concatenate(rows, axis=0)

    me = lax.rem(lax.axis_index("tgt"), near)
    for e, out_ref in enumerate(out_refs):
        for far in range(4):
            owner = far * near + jnp.bitwise_xor(me, e)
            for p in range(sb):
                out_ref[far, p * piece : (p + 1) * piece] = image_ref[p, pl.ds(pl.multiple_of(owner * piece, piece), piece)]
            tile = owner * piece // LANES
            out_ref[far, sb * piece : sb * (piece + 1)] = slots_of(tile, lse)
            out_ref[far, sb * (piece + 1) :] = slots_of(tile, rows_ref[...])


def merge_images(parts, offset, sb, piece, turn_ref):
    whole = merge_lse([lse for _, lse in parts])
    weights = []
    for k, (_, lse) in enumerate(parts):
        turn_ref[k] = jnp.exp2(lse - whole).T
        weights.append(turn_ref[k, pl.ds(offset, piece), :])
    images = []
    for p in range(sb):
        images.append(
            sum(
                image[p * piece : (p + 1) * piece] * weight[:, p : p + 1]
                for (image, _), weight in zip(parts, weights)
            )
        )
    return images, whole


def near_kernel(near, sb, piece, *refs):
    in_refs, out_refs, turn_ref = refs[:near], refs[near : near + 4], refs[near + 4]
    place = lax.axis_index("tgt")
    me, mine = lax.rem(place, near), place // near
    rows = sb * piece
    for d, out_ref in enumerate(out_refs):
        far = jnp.bitwise_xor(mine, d)
        offset = lax.rem((far * near + me) * piece, LANES)
        parts = [(ref[far, :rows], ref[far, rows : rows + sb]) for ref in in_refs]
        images, whole = merge_images(parts, pl.multiple_of(offset, piece), sb, piece, turn_ref)
        for p in range(sb):
            out_ref[p * piece : (p + 1) * piece] = images[p]
        out_ref[rows : rows + sb] = whole
        out_ref[rows + sb :] = merge_lse([ref[far, rows + sb :] for ref in in_refs])


def far_kernel(sb, piece, xfixed_ref, f_in_ref, *refs):
    in_refs, out_ref, f_ref, turn_ref = refs[:4], refs[4], refs[5], refs[6]
    rows = sb * piece
    start = lax.axis_index("tgt") * piece
    offset = lax.rem(start, LANES)
    parts = [(ref[:rows], ref[rows : rows + sb]) for ref in in_refs]
    images, _ = merge_images(parts, pl.multiple_of(offset, piece), sb, piece, turn_ref)
    for p in range(sb):
        out_ref[p] = images[p]
    tile = start // LANES
    lse = merge_lse([ref[rows + sb :] for ref in in_refs])
    f = updated(slots_of(tile, f_in_ref[...]), slots_of(tile, xfixed_ref[0]), lse)
    f_ref[...] = pltpu.roll(f * (1.0 / UNIT), lax.rem(LANES - offset, LANES), 1)[:, :piece]


def pack_kernel(*refs):
    for k, axis in enumerate(("tgt", "src")):
        points_ref, mass_ref, potential_ref = refs[3 * k : 3 * k + 3]
        out_ref = refs[6 + k]
        blocks, piece, width = points_ref.shape
        here = lax.rem(lax.axis_index(axis) * piece, LANES)
        slot = lax.broadcasted_iota(jnp.int32, (piece, LANES), 0)
        lane = lax.broadcasted_iota(jnp.int32, (piece, LANES), 1)
        put = jnp.where(lane == slot + here, 1.0, 0.0).astype(jnp.bfloat16)
        vecs = [jnp.dot(ref[...], put, preferred_element_type=jnp.float32) for ref in (mass_ref, potential_ref)]
        out_ref[: blocks * piece] = points_ref[...].reshape(blocks * piece, width)
        out_ref[blocks * piece :] = jnp.concatenate(vecs, axis=0).astype(jnp.bfloat16)


def on_device(
    src_points, tgt_points, src_mass, tgt_mass, src_potential, tgt_potential, src_counts, tgt_counts, keep
):
    ntgt, nsrc = lax.axis_size("tgt"), lax.axis_size("src")
    near = near_count("tgt")
    sb, src_piece, width = src_points.shape
    tb, tgt_piece, _ = tgt_points.shape
    blk = src_piece * ntgt
    x_rows, y_rows = sb * src_piece, tb * tgt_piece
    x_packed, y_packed = pl.pallas_call(
        pack_kernel,
        out_shape=(
            jax.ShapeDtypeStruct((x_rows + 2 * sb, width), jnp.bfloat16),
            jax.ShapeDtypeStruct((y_rows + 2 * tb, width), jnp.bfloat16),
        ),
        in_specs=[VMEM] * 6,
        out_specs=(VMEM, VMEM),
        name="pack",
    )(src_points, src_mass, src_potential, tgt_points, tgt_mass, tgt_potential)
    (x_in, x_parts), (y_in, y_parts) = gather_points(x_packed, y_packed, y_rows)
    pairs, x_own, y_own = pl.pallas_call(
        list_kernel,
        out_shape=(
            jax.ShapeDtypeStruct((1 + sb * tb + sb + tb,), jnp.int32),
            jax.ShapeDtypeStruct(x_packed.shape, x_packed.dtype),
            jax.ShapeDtypeStruct(y_packed.shape, y_packed.dtype),
        ),
        in_specs=[SMEM] * 3 + [VMEM] * 2,
        out_specs=(SMEM, VMEM, VMEM),
        compiler_params=PARAMS,
        name="kept_pairs",
    )(keep, src_counts, tgt_counts, x_packed, y_packed)
    x_in[0], y_in[0] = x_own, y_own

    def half_room(targets):
        return dict(scratch_shapes=half_scratch(sb, targets, blk), compiler_params=PARAMS)

    shared = shared_rows()
    x, y, xfixed, yfixed, f, part = pl.pallas_call(
        functools.partial(first_kernel, x_parts, y_parts),
        out_shape=(
            jax.ShapeDtypeStruct((ntgt, sb, src_piece, width), jnp.bfloat16),
            jax.ShapeDtypeStruct((nsrc, tb, tgt_piece, width), jnp.bfloat16),
            f32(2, sb, blk),
            f32(3, tb, blk),
            f32(sb, blk),
            f32(sb + tb, blk),
        ),
        in_specs=[SMEM] + [VMEM] * (len(x_in) + len(y_in)),
        out_specs=(VMEM,) * 6,
        scratch_shapes=[
            pltpu.VMEM((2, blk // LANES, sb, LANES), jnp.float32),
            pltpu.VMEM((2, blk // LANES, tb, LANES), jnp.float32),
        ]
        + half_scratch(sb, tb, blk),
        compiler_params=PARAMS,
        name="first_sweep",
    )(pairs, *x_in, *y_in)

    if shared:
        pairs_two, y_two, yfixed_two = [swap(array, "tgt", 1) for array in (pairs, y, yfixed)]
        sums = exchange_first(part, sb)
        y, yfixed, f, part = pl.pallas_call(
            second_kernel,
            out_shape=(
                jax.ShapeDtypeStruct((nsrc, 2 * tb, tgt_piece, width), jnp.bfloat16),
                f32(3, 2 * tb, blk),
                f32(sb, blk),
                f32(2 * tb, blk),
            ),
            in_specs=[SMEM] * 2 + [VMEM] * 9,
            out_specs=(VMEM,) * 4,
            name="second_sweep",
            **half_room(2 * tb),
        )(pairs, pairs_two, x, y, y_two, xfixed, yfixed, yfixed_two, f, *sums)
        lists = (pairs, pairs_two)
    else:
        lists = (pairs,)
    held = yfixed.shape[1]
    step = pl.pallas_call(
        functools.partial(step_kernel, shared),
        out_shape=(f32(3, held, blk), f32(sb, blk), f32(*part.shape)),
        in_specs=[SMEM] * len(lists) + [VMEM] * (6 + shared),
        out_specs=(VMEM,) * 3,
        name="sweep",
        **half_room(held),
    )

    def exchange():
        return exchange_shared(part) if shared else (exchange_plain(part, sb),)

    for _ in range(ITERS - 2 - shared):
        yfixed, f, part = step(*lists, x, y, xfixed, yfixed, f, *exchange())

    yfixed, f, cols = pl.pallas_call(
        functools.partial(last_cols_kernel, shared),
        out_shape=(f32(3, tb, blk), f32(sb, blk), f32(tb, blk)),
        in_specs=[SMEM] + [VMEM] * (6 + shared),
        out_specs=(VMEM,) * 3,
        name="last_cols",
        **half_room(tb),
    )(pairs, x, y, xfixed, yfixed, f, *exchange())
    col_parts = exchange_lse(cols, "src")
    rows = pl.pallas_call(
        last_rows_kernel,
        out_shape=f32(sb, blk),
        in_specs=[SMEM] + [VMEM] * 3,
        out_specs=VMEM,
        name="last_rows",
        **half_room(tb),
    )(pairs, x, y, yfixed)
    rows, *col_parts = lax.optimization_barrier((rows, *col_parts))
    tile = sb * (src_piece + 2)
    g, *near_parts = pl.pallas_call(
        functools.partial(project_kernel, near),
        out_shape=(f32(tb, blk),) + (f32(4, tile, width),) * near,
        in_specs=[SMEM] + [VMEM] * 8,
        out_specs=(VMEM,) * (1 + near),
        scratch_shapes=project_scratch(sb, tb, blk, width),
        compiler_params=PARAMS,
        name="project",
    )(pairs, x, y, yfixed, rows, *col_parts)
    if near > 1:
        near_parts = near_parts[:1] + [swap(near_parts[d], "tgt", d) for d in range(1, near)]
    far_parts = pl.pallas_call(
        functools.partial(near_kernel, near, sb, src_piece),
        out_shape=(f32(tile, width),) * 4,
        in_specs=[VMEM] * near,
        out_specs=(VMEM,) * 4,
        scratch_shapes=[pltpu.VMEM((near, LANES, sb), jnp.float32)],
        compiler_params=PARAMS,
        name="merge_near",
    )(*near_parts)
    far_parts = [far_parts[0]] + [swap(far_parts[k], "tgt", near * k) for k in range(1, 4)]
    images, src_final = pl.pallas_call(
        functools.partial(far_kernel, sb, src_piece),
        out_shape=(f32(sb, src_piece, width), f32(sb, src_piece)),
        in_specs=[VMEM] * 6,
        out_specs=(VMEM, VMEM),
        scratch_shapes=[pltpu.VMEM((4, LANES, sb), jnp.float32)],
        compiler_params=PARAMS,
        name="merge_far",
    )(xfixed, f, *far_parts)

    tgt_final = lax.dynamic_slice_in_dim(g, lax.axis_index("src") * tgt_piece, tgt_piece, 1)
    return images, src_final, tgt_final


def solution(mesh):
    return jax.shard_map(
        on_device,
        mesh=mesh,
        in_specs=(
            P("src", "tgt", None),
            P("tgt", "src", None),
            P("src", "tgt"),
            P("tgt", "src"),
            P("src", "tgt"),
            P("tgt", "src"),
            P("src"),
            P("tgt"),
            P("src", "tgt"),
        ),
        out_specs=(P("src", "tgt", None), P("src", "tgt"), P("tgt", "src")),
        check_vma=False,
    )
```

```python
import functools
import math

import jax
import jax.numpy as jnp
from jax import lax
from jax.experimental import pallas as pl
from jax.experimental.pallas import tpu as pltpu
from jax.sharding import PartitionSpec as P

ITERS = 4
EPSILON = 0.1
UNIT = 1.0 / (EPSILON * math.log(2.0))
FLOOR = -1e30
LANES = 128
GROUP = 16
MOVE_GROUP = 6

SMEM = pl.BlockSpec(memory_space=pltpu.SMEM)
VMEM = pl.BlockSpec(memory_space=pltpu.VMEM)
PARAMS = pltpu.CompilerParams(vmem_limit_bytes=40 * 1024 * 1024)


def f32(*shape):
    return jax.ShapeDtypeStruct(shape, jnp.float32)


def swap(part, axis, mask):
    return lax.ppermute(part, axis, [(i, i ^ mask) for i in range(lax.axis_size(axis))])


def near_count(axis):
    return lax.axis_size(axis) // 4


def merge_lse(parts):
    top = functools.reduce(jnp.maximum, parts)
    return top + jnp.log2(sum(jnp.exp2(part - top) for part in parts))


def exchange_lse(part, axis):
    near = near_count(axis)
    if near > 1:
        part = merge_lse([part] + [swap(part, axis, d) for d in range(1, near)])
    return [part] + [swap(part, axis, near * k) for k in range(1, 4)]


def shared_rows():
    return near_count("tgt") == 2 and near_count("src") == 1


def is_odd():
    return lax.rem(lax.axis_index("tgt"), 2) == 1


def exchange_plain(part, sb):
    return jnp.concatenate([merge_lse(exchange_lse(part[:sb], "tgt")), merge_lse(exchange_lse(part[sb:], "src"))])


def exchange_first(part, sb):
    other = swap(part, "tgt", 1)
    rows = merge_lse([part[:sb], other[:sb]])
    part = jnp.where(is_odd(), padded(rows, part), jnp.concatenate([part[sb:], other[sb:]]))
    return exchange_shared(part, 1)


def padded(rows, part):
    return jnp.concatenate([rows] * (part.shape[0] // rows.shape[0]))


def exchange_shared(part, row_side):
    ntgt, nsrc = lax.axis_size("tgt"), lax.axis_size("src")

    def swap_far(k):
        pairs = [
            (s * ntgt + t, s * ntgt + (t ^ (2 * k)) if t % 2 == row_side else (s ^ k) * ntgt + t)
            for s in range(nsrc)
            for t in range(ntgt)
        ]
        return lax.ppermute(part, ("src", "tgt"), pairs)

    return merge_lse([part] + [swap_far(k) for k in range(1, 4)])


def gather_points(x_piece, y_piece, y_rows):
    nx, ny = near_count("tgt"), near_count("src")
    y_two = swap(y_piece, "src", 2 * ny)
    y_one, y_three = swap(y_piece, "src", ny), swap(y_piece, "src", 3 * ny)
    x_far = [swap(x_piece, "tgt", nx * k) for k in range(1, 4)]
    y_one, y_three, *x_far = lax.optimization_barrier((y_one, y_three, *x_far))
    y_found = [(0, 0, y_piece), (ny, 0, y_one), (2 * ny, 0, y_two), (3 * ny, 0, y_three)]
    x_found = [(0, 0, x_piece)] + [(nx * k, 0, x_far[k - 1]) for k in range(1, 4)]
    return spread_near(x_found, "tgt"), spread_near(y_found, "src")


def spread_near(found, axis):
    near = near_count(axis)
    arrays, parts = [], []
    for d in range(near):
        for mask, first, array in found:
            parts.append((mask ^ d, first, len(arrays), array.shape[0]))
            arrays.append(swap(array, axis, d) if d else array)
    return arrays, parts


def whole_block(ref, k):
    piece = ref[:, k]
    return piece.reshape(piece.shape[0] * piece.shape[1], piece.shape[2])


def split_columns(vec, split_ref):
    blocks, slots = vec.shape
    vec = vec * (1.0 / UNIT)
    parts = []
    for _ in range(3):
        part = vec.astype(jnp.bfloat16).astype(jnp.float32)
        parts.append(part)
        vec = vec - part
    parts.append(jnp.zeros((LANES - 3 * blocks, slots), jnp.float32))
    split_ref[...] = jnp.concatenate(parts, axis=0).T.astype(jnp.bfloat16)


def column_scores(stream_ref, q, split_ref, blocks, k, lane_ref, p):
    lane = lax.broadcasted_iota(jnp.int32, (16, LANES), 1)
    pick = jnp.where((lane < 3 * blocks) & (lax.rem(lane, blocks) == k), 1.0, 0.0).astype(jnp.bfloat16)
    pick = jnp.concatenate([pick] * (split_ref.shape[0] // 16), axis=0)
    score = lax.dot_general(
        jnp.concatenate([whole_block(stream_ref, q), split_ref[...]], axis=1),
        jnp.concatenate([whole_block(lane_ref, p), pick], axis=1),
        (((1,), (1,)), ((), ())),
        preferred_element_type=jnp.float32,
    )
    return score, jnp.max(score, axis=0, keepdims=True)


def column_lse(*operands):
    score, peak = column_scores(*operands)
    return peak * UNIT, jnp.sum(jnp.exp2((score - peak) * UNIT), axis=0, keepdims=True)


def slots_of(tile, vec):
    found = vec[:, :LANES]
    for t in range(1, vec.shape[1] // LANES):
        found = jnp.where(tile == t, vec[:, t * LANES : (t + 1) * LANES], found)
    return found


def clear(peak_ref, sum_ref):
    peak_ref[...] = jnp.full(peak_ref.shape, FLOOR, jnp.float32)
    sum_ref[...] = jnp.zeros(sum_ref.shape, jnp.float32)


def merge_slots(peak, total, count):
    shape = (count, peak.shape[0] // count, peak.shape[1])
    peak = peak.reshape(shape)
    top = jnp.max(peak, axis=1, keepdims=True)
    total = jnp.sum(total.reshape(shape) * jnp.exp2(peak - top), axis=1)
    return top[:, 0] + jnp.log2(jnp.maximum(total, 1.0))


def pair_list(tb, list_ref, other_ref=None):
    own = list_ref[0]
    count = own if other_ref is None else own + other_ref[0]

    def pair(place):
        place = jnp.minimum(place, count - 1)
        if other_ref is None:
            code, shift = list_ref[1 + place], 0
        else:
            mine = place < own
            here, there = list_ref[1 + jnp.where(mine, place, 0)], other_ref[1 + jnp.where(mine, 0, place - own)]
            code = jnp.where(mine, here, there)
            shift = jnp.where(mine, 0, tb)
        return code // tb, lax.rem(code, tb) + shift

    return count, pair


def visit_pairs(pairs, first, last, group, work):
    count, pair = pairs

    @pl.loop(0, pl.cdiv(last - first, group))
    def _(step):
        places = [first + step * group + k for k in range(group)]
        work([pair(place) + (place < count,) for place in places])


def half_sweep(pairs, rows, x_ref, y_ref, tb, vec, scratch):
    split_ref, peak_ref, sum_ref = scratch
    sb = x_ref.shape[1]
    used = sb * tb
    split_columns(vec, split_ref)
    clear(peak_ref, sum_ref)

    def work(group):
        found = []
        for p, q, _ in group:
            if rows:
                found.append((p * tb + q, column_lse(y_ref, q, split_ref, tb, q, x_ref, p)))
            else:
                found.append((q * sb + p, column_lse(x_ref, p, split_ref, sb, p, y_ref, q)))
        for slot, pair in found:
            peak_ref[pl.ds(slot, 1), :], sum_ref[pl.ds(slot, 1), :] = pair

    count = pairs[0]
    rest = lax.rem(count, GROUP)
    large = jnp.where(rest > GROUP // 2, count, count - rest)
    middle = jnp.where(rest > GROUP // 4, count, large)
    visit_pairs(pairs, 0, large, GROUP, work)
    visit_pairs(pairs, large, middle, GROUP // 2, work)
    visit_pairs(pairs, middle, count, GROUP // 4, work)
    return merge_slots(peak_ref[:used], sum_ref[:used], sb if rows else tb)


def half_scratch(sb, tb, blk):
    return [
        pltpu.VMEM((blk, LANES), jnp.bfloat16),
        pltpu.VMEM((sb * tb, blk), jnp.float32),
        pltpu.VMEM((sb * tb, blk), jnp.float32),
    ]


def sweep_own(pairs, x_ref, y_ref, u, h, part_ref, scratch):
    sb, tb = u.shape[0], h.shape[0]
    part_ref[:sb] = half_sweep(pairs, True, x_ref, y_ref, tb, h, scratch)
    part_ref[sb:] = half_sweep(pairs, False, x_ref, y_ref, tb, u, scratch)


def sweep_shared(row_side, pairs, x_ref, y_ref, u, h, part_ref, scratch):
    sb, tb = u.shape[0], h.shape[0]
    odd = is_odd()
    summing_rows = odd if row_side else jnp.logical_not(odd)

    @pl.when(summing_rows)
    def _():
        part_ref[...] = padded(half_sweep(pairs, True, x_ref, y_ref, tb, h, scratch), part_ref)

    @pl.when(jnp.logical_not(summing_rows))
    def _():
        part_ref[...] = half_sweep(pairs, False, x_ref, y_ref, tb, u, scratch)


def project_scratch(sb, tb, blk, width):
    return [
        pltpu.VMEM((blk, LANES), jnp.bfloat16),
        pltpu.VMEM((tb, width, blk), jnp.bfloat16),
        pltpu.VMEM((sb + 1, 1, blk), jnp.float32),
        pltpu.VMEM((sb + 1, 1, blk), jnp.float32),
        pltpu.VMEM((sb + 1, width, blk), jnp.float32),
        pltpu.VMEM((sb, blk, width), jnp.float32),
    ]


def list_kernel(keep_ref, src_counts_ref, tgt_counts_ref, x_in_ref, y_in_ref, list_ref, x_ref, y_ref):
    sb, tb = keep_ref.shape
    x_ref[...] = x_in_ref[...]
    y_ref[...] = y_in_ref[...]
    counts_at = 1 + sb * tb
    n = jnp.int32(0)
    for code in range(sb * tb):
        list_ref[1 + n] = code
        n = n + (keep_ref[code // tb, code % tb] > 0).astype(jnp.int32)
    list_ref[0] = n
    for k in range(sb):
        list_ref[counts_at + k] = src_counts_ref[k]
    for k in range(tb):
        list_ref[counts_at + sb + k] = tgt_counts_ref[k]


def assemble(place, list_ref, counts_at, parts, part_refs, points_ref, vec_ref):
    n, blocks, piece, width = points_ref.shape
    blk = n * piece
    vec_ref[...] = jnp.zeros(vec_ref.shape, jnp.float32)
    for mask, first, k, count in parts:
        owner = jnp.bitwise_xor(place, mask)
        rows = min(count, blocks * piece - first)
        points_ref[owner, first // piece : (first + rows) // piece] = part_refs[k][:rows].reshape(
            rows // piece, piece, width
        )
        if rows < count:
            vecs = part_refs[k][rows:count].astype(jnp.float32)
            tile = owner * piece // LANES
            vec_ref[0, tile] += vecs[:blocks]
            vec_ref[1, tile] += vecs[blocks:]
    mass = jnp.concatenate([vec_ref[0, t] for t in range(blk // LANES)], axis=1)
    potential = jnp.concatenate([vec_ref[1, t] for t in range(blk // LANES)], axis=1) * UNIT
    block_of = lax.broadcasted_iota(jnp.int32, (blocks, blk), 0)
    slot_of = lax.broadcasted_iota(jnp.int32, (blocks, blk), 1)
    half = jnp.zeros((blocks, blk), jnp.float32)
    count = jnp.zeros((blocks, blk), jnp.int32)
    ones = jnp.ones((blocks, width), jnp.bfloat16)
    for k in range(blocks):
        wide = whole_block(points_ref, k).astype(jnp.float32)
        square = wide * wide
        high = square.astype(jnp.bfloat16)
        low = (square - high.astype(jnp.float32)).astype(jnp.bfloat16)
        norm = sum(
            lax.dot_general(ones, part, (((1,), (1,)), ((), ())), preferred_element_type=jnp.float32)
            for part in (high, low)
        )
        half = jnp.where(block_of == k, norm * (0.5 * UNIT), half)
        count = jnp.where(block_of == k, list_ref[counts_at + k], count)
    base = jnp.where(slot_of < count, jnp.log2(mass) - half, FLOOR)
    return potential, half, base


def first_kernel(x_parts, y_parts, list_ref, *refs):
    nx = 1 + max(part[2] for part in x_parts)
    ny = 1 + max(part[2] for part in y_parts)
    x_in, y_in, refs = refs[:nx], refs[nx : nx + ny], refs[nx + ny :]
    x_ref, y_ref, xfixed_ref, yfixed_ref, f_ref, part_ref, xvec_ref, yvec_ref = refs[:8]
    sb, tb = x_ref.shape[1], y_ref.shape[1]
    counts_at = 1 + sb * tb
    f, x_half, x_base = assemble(lax.axis_index("tgt"), list_ref, counts_at, x_parts, x_in, x_ref, xvec_ref)
    g, y_half, y_base = assemble(lax.axis_index("src"), list_ref, counts_at + sb, y_parts, y_in, y_ref, yvec_ref)
    f_ref[...] = f
    xfixed_ref[0], xfixed_ref[1] = x_half, x_base
    yfixed_ref[0], yfixed_ref[1], yfixed_ref[2] = y_half, y_base, g
    sweep_own(pair_list(tb, list_ref), x_ref, y_ref, f + x_base, g + y_base, part_ref, refs[8:])


def updated(old, half, lse):
    return 0.5 * (old + (half - lse))


def turned(cols):
    tb = cols.shape[0] // 2
    return jnp.concatenate([cols[tb:], cols[:tb]])


def second_kernel(list_ref, list2_ref, x_ref, y1_ref, y2_ref, xfixed_ref, yfixed1_ref, yfixed2_ref, f_in_ref, *refs):
    whole_ref, y_ref, yfixed_ref, mine_ref, part_ref = refs[:5]
    sb, tb = x_ref.shape[1], y1_ref.shape[1]
    y_ref[:, :tb] = y1_ref[...]
    y_ref[:, tb:] = y2_ref[...]
    half, base, g = [jnp.concatenate([yfixed1_ref[k], yfixed2_ref[k]]) for k in range(3)]
    yfixed_ref[0], yfixed_ref[1] = half, base
    f = updated(f_in_ref[...], xfixed_ref[0], whole_ref[:sb])
    g = updated(g, half, whole_ref[...])
    mine_ref[...] = jnp.where(is_odd(), padded(f, g), g)
    sweep_shared(
        0, pair_list(tb, list_ref, list2_ref), x_ref, y_ref, f + xfixed_ref[1], g + base, part_ref, refs[5:]
    )


def shared_kernel(row_side, list_ref, list2_ref, x_ref, y_ref, xfixed_ref, yfixed_ref, whole_ref, old_ref, *refs):
    mine_ref, part_ref = refs[:2]
    sb, tb = x_ref.shape[1], y_ref.shape[1] // 2
    f = updated(old_ref[:sb], xfixed_ref[0], whole_ref[:sb])
    g = updated(turned(old_ref[...]), yfixed_ref[0], whole_ref[...])
    mine_ref[...] = jnp.where(is_odd(), g, padded(f, g)) if row_side else jnp.where(is_odd(), padded(f, g), g)
    pairs = pair_list(tb, list_ref, list2_ref)
    sweep_shared(row_side, pairs, x_ref, y_ref, f + xfixed_ref[1], g + yfixed_ref[1], part_ref, refs[2:])


def step_kernel(list_ref, x_ref, y_ref, xfixed_ref, yfixed_in_ref, f_in_ref, whole_ref, *refs):
    yfixed_ref, f_ref, part_ref = refs[:3]
    sb, tb = x_ref.shape[1], y_ref.shape[1]
    f = updated(f_in_ref[...], xfixed_ref[0], whole_ref[:sb])
    half, base, g = [yfixed_in_ref[k] for k in range(3)]
    g = updated(g, half, whole_ref[sb:])
    f_ref[...] = f
    yfixed_ref[0], yfixed_ref[1], yfixed_ref[2] = half, base, g
    sweep_own(pair_list(tb, list_ref), x_ref, y_ref, f + xfixed_ref[1], g + base, part_ref, refs[3:])


def last_cols_kernel(row_side, list_ref, x_ref, y_ref, xfixed_ref, yfixed_in_ref, *refs):
    if row_side is None:
        f_in_ref, whole_ref, yfixed_ref, f_ref, cols_ref = refs[:5]
        scratch = refs[5:]
        sb, tb = x_ref.shape[1], cols_ref.shape[0]
        old_f, old_g = f_in_ref[...], yfixed_in_ref[2]
        rows, cols = whole_ref[:sb], whole_ref[sb:]
    else:
        whole_ref, whole2_ref, mine_ref, mine2_ref, yfixed_ref, f_ref, cols_ref = refs[:7]
        scratch = refs[7:]
        sb, tb = x_ref.shape[1], cols_ref.shape[0]
        has_rows = is_odd() if row_side else jnp.logical_not(is_odd())
        rows = jnp.where(has_rows, whole_ref[:sb], whole2_ref[:sb])
        cols = jnp.where(has_rows, whole2_ref[tb:], whole_ref[:tb])
        old_f = jnp.where(has_rows, mine2_ref[:sb], mine_ref[:sb])
        old_g = jnp.where(has_rows, mine_ref[:tb], mine2_ref[tb:])
    f = updated(old_f, xfixed_ref[0], rows)
    half, base = yfixed_in_ref[0, :tb], yfixed_in_ref[1, :tb]
    f_ref[...] = f
    yfixed_ref[0], yfixed_ref[1], yfixed_ref[2] = half, base, updated(old_g, half, cols)
    cols_ref[...] = half_sweep(pair_list(tb, list_ref), False, x_ref, y_ref, tb, f + xfixed_ref[1], scratch)


def last_rows_kernel(list_ref, x_ref, y_ref, yfixed_ref, rows_ref, *scratch):
    tb = yfixed_ref.shape[1]
    vec = yfixed_ref[2] + yfixed_ref[1]
    rows_ref[...] = half_sweep(pair_list(tb, list_ref), True, x_ref, y_ref, tb, vec, scratch)


def project_kernel(near, list_ref, x_ref, y_ref, yfixed_ref, rows_ref, *refs):
    col_refs, g_ref, out_refs = refs[:4], refs[4], refs[5 : 5 + near]
    split_ref, turned_ref, peak_ref, sum_ref, acc_ref, image_ref = refs[5 + near :]
    n, sb, piece, width = x_ref.shape
    tb = g_ref.shape[0]
    blk = n * piece
    g = updated(yfixed_ref[2], yfixed_ref[0], merge_lse([ref[...] for ref in col_refs]))
    g_ref[...] = g * (1.0 / UNIT)
    split_columns(g + yfixed_ref[1], split_ref)
    for q in range(tb):
        turned_ref[q] = whole_block(y_ref, q).T
    clear(peak_ref, sum_ref)
    acc_ref[...] = jnp.zeros(acc_ref.shape, jnp.float32)

    def move(group):
        found = []
        for p, q, real in group:
            score, peak = column_scores(y_ref, q, split_ref, tb, q, x_ref, p)
            weights = jnp.exp2((score - peak) * UNIT)
            high = weights.astype(jnp.bfloat16)
            low = (weights - high.astype(jnp.float32)).astype(jnp.bfloat16)
            ys = turned_ref[q]
            moved = jnp.dot(ys, high, preferred_element_type=jnp.float32) + jnp.dot(
                ys, low, preferred_element_type=jnp.float32
            )
            found.append((jnp.where(real, p, sb), peak * UNIT, jnp.sum(weights, axis=0, keepdims=True), moved))
        for p, peak, total, moved in found:
            old = peak_ref[p]
            new = jnp.maximum(old, peak)
            before, here = jnp.exp2(old - new), jnp.exp2(peak - new)
            peak_ref[p] = new
            sum_ref[p] = sum_ref[p] * before + total * here
            acc_ref[p] = acc_ref[p] * before + moved * here

    pairs = pair_list(tb, list_ref)
    visit_pairs(pairs, 0, pairs[0], MOVE_GROUP, move)
    rows = []
    for p in range(sb):
        total = jnp.maximum(sum_ref[p], 1.0)
        image_ref[p] = (acc_ref[p] / total).T
        rows.append(peak_ref[p] + jnp.log2(total))
    lse = jnp.concatenate(rows, axis=0)

    me = lax.rem(lax.axis_index("tgt"), near)
    for e, out_ref in enumerate(out_refs):
        for far in range(4):
            owner = far * near + jnp.bitwise_xor(me, e)
            for p in range(sb):
                out_ref[far, p * piece : (p + 1) * piece] = image_ref[p, pl.ds(pl.multiple_of(owner * piece, piece), piece)]
            tile = owner * piece // LANES
            out_ref[far, sb * piece : sb * (piece + 1)] = slots_of(tile, lse)
            out_ref[far, sb * (piece + 1) :] = slots_of(tile, rows_ref[...])


def merge_images(parts, offset, sb, piece, turn_ref):
    whole = merge_lse([lse for _, lse in parts])
    weights = []
    for k, (_, lse) in enumerate(parts):
        turn_ref[k] = jnp.exp2(lse - whole).T
        weights.append(turn_ref[k, pl.ds(offset, piece), :])
    images = []
    for p in range(sb):
        images.append(
            sum(
                image[p * piece : (p + 1) * piece] * weight[:, p : p + 1]
                for (image, _), weight in zip(parts, weights)
            )
        )
    return images, whole


def near_kernel(near, sb, piece, *refs):
    in_refs, out_refs, turn_ref = refs[:near], refs[near : near + 4], refs[near + 4]
    place = lax.axis_index("tgt")
    me, mine = lax.rem(place, near), place // near
    rows = sb * piece
    for d, out_ref in enumerate(out_refs):
        far = jnp.bitwise_xor(mine, d)
        offset = lax.rem((far * near + me) * piece, LANES)
        parts = [(ref[far, :rows], ref[far, rows : rows + sb]) for ref in in_refs]
        images, whole = merge_images(parts, pl.multiple_of(offset, piece), sb, piece, turn_ref)
        for p in range(sb):
            out_ref[p * piece : (p + 1) * piece] = images[p]
        out_ref[rows : rows + sb] = whole
        out_ref[rows + sb :] = merge_lse([ref[far, rows + sb :] for ref in in_refs])


def far_kernel(sb, piece, xfixed_ref, f_in_ref, *refs):
    in_refs, out_ref, f_ref, turn_ref = refs[:4], refs[4], refs[5], refs[6]
    rows = sb * piece
    start = lax.axis_index("tgt") * piece
    offset = lax.rem(start, LANES)
    parts = [(ref[:rows], ref[rows : rows + sb]) for ref in in_refs]
    images, _ = merge_images(parts, pl.multiple_of(offset, piece), sb, piece, turn_ref)
    for p in range(sb):
        out_ref[p] = images[p]
    tile = start // LANES
    lse = merge_lse([ref[rows + sb :] for ref in in_refs])
    f = updated(slots_of(tile, f_in_ref[...]), slots_of(tile, xfixed_ref[0]), lse)
    f_ref[...] = pltpu.roll(f * (1.0 / UNIT), lax.rem(LANES - offset, LANES), 1)[:, :piece]


def pack_kernel(*refs):
    for k, axis in enumerate(("tgt", "src")):
        points_ref, mass_ref, potential_ref = refs[3 * k : 3 * k + 3]
        out_ref = refs[6 + k]
        blocks, piece, width = points_ref.shape
        here = lax.rem(lax.axis_index(axis) * piece, LANES)
        slot = lax.broadcasted_iota(jnp.int32, (piece, LANES), 0)
        lane = lax.broadcasted_iota(jnp.int32, (piece, LANES), 1)
        put = jnp.where(lane == slot + here, 1.0, 0.0).astype(jnp.bfloat16)
        vecs = [jnp.dot(ref[...], put, preferred_element_type=jnp.float32) for ref in (mass_ref, potential_ref)]
        out_ref[: blocks * piece] = points_ref[...].reshape(blocks * piece, width)
        out_ref[blocks * piece :] = jnp.concatenate(vecs, axis=0).astype(jnp.bfloat16)


def on_device(
    src_points, tgt_points, src_mass, tgt_mass, src_potential, tgt_potential, src_counts, tgt_counts, keep
):
    ntgt, nsrc = lax.axis_size("tgt"), lax.axis_size("src")
    near = near_count("tgt")
    sb, src_piece, width = src_points.shape
    tb, tgt_piece, _ = tgt_points.shape
    blk = src_piece * ntgt
    x_rows, y_rows = sb * src_piece, tb * tgt_piece
    x_packed, y_packed = pl.pallas_call(
        pack_kernel,
        out_shape=(
            jax.ShapeDtypeStruct((x_rows + 2 * sb, width), jnp.bfloat16),
            jax.ShapeDtypeStruct((y_rows + 2 * tb, width), jnp.bfloat16),
        ),
        in_specs=[VMEM] * 6,
        out_specs=(VMEM, VMEM),
        name="pack",
    )(src_points, src_mass, src_potential, tgt_points, tgt_mass, tgt_potential)
    (x_in, x_parts), (y_in, y_parts) = gather_points(x_packed, y_packed, y_rows)
    pairs, x_own, y_own = pl.pallas_call(
        list_kernel,
        out_shape=(
            jax.ShapeDtypeStruct((1 + sb * tb + sb + tb,), jnp.int32),
            jax.ShapeDtypeStruct(x_packed.shape, x_packed.dtype),
            jax.ShapeDtypeStruct(y_packed.shape, y_packed.dtype),
        ),
        in_specs=[SMEM] * 3 + [VMEM] * 2,
        out_specs=(SMEM, VMEM, VMEM),
        compiler_params=PARAMS,
        name="kept_pairs",
    )(keep, src_counts, tgt_counts, x_packed, y_packed)
    x_in[0], y_in[0] = x_own, y_own

    def half_room(targets):
        return dict(scratch_shapes=half_scratch(sb, targets, blk), compiler_params=PARAMS)

    shared = shared_rows()
    x, y, xfixed, yfixed, f, part = pl.pallas_call(
        functools.partial(first_kernel, x_parts, y_parts),
        out_shape=(
            jax.ShapeDtypeStruct((ntgt, sb, src_piece, width), jnp.bfloat16),
            jax.ShapeDtypeStruct((nsrc, tb, tgt_piece, width), jnp.bfloat16),
            f32(2, sb, blk),
            f32(3, tb, blk),
            f32(sb, blk),
            f32(sb + tb, blk),
        ),
        in_specs=[SMEM] + [VMEM] * (len(x_in) + len(y_in)),
        out_specs=(VMEM,) * 6,
        scratch_shapes=[
            pltpu.VMEM((2, blk // LANES, sb, LANES), jnp.float32),
            pltpu.VMEM((2, blk // LANES, tb, LANES), jnp.float32),
        ]
        + half_scratch(sb, tb, blk),
        compiler_params=PARAMS,
        name="first_sweep",
    )(pairs, *x_in, *y_in)

    if shared:
        pairs_two, y_two, yfixed_two = [swap(array, "tgt", 1) for array in (pairs, y, yfixed)]
        pairs_two, part = lax.optimization_barrier((pairs_two, part))
        whole = exchange_first(part, sb)
        y, yfixed, mine, part = pl.pallas_call(
            second_kernel,
            out_shape=(
                jax.ShapeDtypeStruct((nsrc, 2 * tb, tgt_piece, width), jnp.bfloat16),
                f32(2, 2 * tb, blk),
                f32(2 * tb, blk),
                f32(2 * tb, blk),
            ),
            in_specs=[SMEM] * 2 + [VMEM] * 8,
            out_specs=(VMEM,) * 4,
            name="second_sweep",
            **half_room(2 * tb),
        )(pairs, pairs_two, x, y, y_two, xfixed, yfixed, yfixed_two, f, whole)
        for k in range(2, ITERS - 1):
            old, whole = swap(mine, "tgt", 1), exchange_shared(part, (k - 1) % 2 ^ 1)
            mine, part = pl.pallas_call(
                functools.partial(shared_kernel, k % 2 ^ 1),
                out_shape=(f32(2 * tb, blk), f32(2 * tb, blk)),
                in_specs=[SMEM] * 2 + [VMEM] * 6,
                out_specs=(VMEM, VMEM),
                name="sweep",
                **half_room(2 * tb),
            )(pairs, pairs_two, x, y, xfixed, yfixed, whole, old)
        row_side = (ITERS - 2) % 2 ^ 1
        old, whole = swap(mine, "tgt", 1), exchange_shared(part, row_side)
        last = (whole, swap(whole, "tgt", 1), mine, old)
    else:
        step = pl.pallas_call(
            step_kernel,
            out_shape=(f32(3, tb, blk), f32(sb, blk), f32(sb + tb, blk)),
            in_specs=[SMEM] + [VMEM] * 6,
            out_specs=(VMEM,) * 3,
            name="sweep",
            **half_room(tb),
        )
        for _ in range(ITERS - 2):
            yfixed, f, part = step(pairs, x, y, xfixed, yfixed, f, exchange_plain(part, sb))
        row_side, last = None, (f, exchange_plain(part, sb))

    yfixed, f, cols = pl.pallas_call(
        functools.partial(last_cols_kernel, row_side),
        out_shape=(f32(3, tb, blk), f32(sb, blk), f32(tb, blk)),
        in_specs=[SMEM] + [VMEM] * (4 + len(last)),
        out_specs=(VMEM,) * 3,
        name="last_cols",
        **half_room(tb),
    )(pairs, x, y, xfixed, yfixed, *last)
    col_parts = exchange_lse(cols, "src")
    rows = pl.pallas_call(
        last_rows_kernel,
        out_shape=f32(sb, blk),
        in_specs=[SMEM] + [VMEM] * 3,
        out_specs=VMEM,
        name="last_rows",
        **half_room(tb),
    )(pairs, x, y, yfixed)
    rows, *col_parts = lax.optimization_barrier((rows, *col_parts))
    tile = sb * (src_piece + 2)
    g, *near_parts = pl.pallas_call(
        functools.partial(project_kernel, near),
        out_shape=(f32(tb, blk),) + (f32(4, tile, width),) * near,
        in_specs=[SMEM] + [VMEM] * 8,
        out_specs=(VMEM,) * (1 + near),
        scratch_shapes=project_scratch(sb, tb, blk, width),
        compiler_params=PARAMS,
        name="project",
    )(pairs, x, y, yfixed, rows, *col_parts)
    if near > 1:
        near_parts = near_parts[:1] + [swap(near_parts[d], "tgt", d) for d in range(1, near)]
    far_parts = pl.pallas_call(
        functools.partial(near_kernel, near, sb, src_piece),
        out_shape=(f32(tile, width),) * 4,
        in_specs=[VMEM] * near,
        out_specs=(VMEM,) * 4,
        scratch_shapes=[pltpu.VMEM((near, LANES, sb), jnp.float32)],
        compiler_params=PARAMS,
        name="merge_near",
    )(*near_parts)
    far_parts = [far_parts[0]] + [swap(far_parts[k], "tgt", near * k) for k in range(1, 4)]
    images, src_final = pl.pallas_call(
        functools.partial(far_kernel, sb, src_piece),
        out_shape=(f32(sb, src_piece, width), f32(sb, src_piece)),
        in_specs=[VMEM] * 6,
        out_specs=(VMEM, VMEM),
        scratch_shapes=[pltpu.VMEM((4, LANES, sb), jnp.float32)],
        compiler_params=PARAMS,
        name="merge_far",
    )(xfixed, f, *far_parts)

    tgt_final = lax.dynamic_slice_in_dim(g, lax.axis_index("src") * tgt_piece, tgt_piece, 1)
    return images, src_final, tgt_final


def solution(mesh):
    return jax.shard_map(
        on_device,
        mesh=mesh,
        in_specs=(
            P("src", "tgt", None),
            P("tgt", "src", None),
            P("src", "tgt"),
            P("tgt", "src"),
            P("src", "tgt"),
            P("tgt", "src"),
            P("src"),
            P("tgt"),
            P("src", "tgt"),
        ),
        out_specs=(P("src", "tgt", None), P("src", "tgt"), P("tgt", "src")),
        check_vma=False,
    )
```

```python
import functools
import math

import jax
import jax.numpy as jnp
from jax import lax
from jax.experimental import pallas as pl
from jax.experimental.pallas import tpu as pltpu
from jax.sharding import PartitionSpec as P

ITERS = 4
EPSILON = 0.1
UNIT = 1.0 / (EPSILON * math.log(2.0))
FLOOR = -1e30
LANES = 128
FAR = (0, 1, 3, 2)
GROUP = 32
MOVE_GROUP = 6

SMEM = pl.BlockSpec(memory_space=pltpu.SMEM)
VMEM = pl.BlockSpec(memory_space=pltpu.VMEM)
PARAMS = pltpu.CompilerParams(vmem_limit_bytes=40 * 1024 * 1024)


def f32(*shape):
    return jax.ShapeDtypeStruct(shape, jnp.float32)


def swap(part, axis, mask):
    return lax.ppermute(part, axis, [(i, i ^ mask) for i in range(lax.axis_size(axis))])


def near_count(axis):
    return lax.axis_size(axis) // 4


def merge_lse(parts):
    top = functools.reduce(jnp.maximum, parts)
    return top + jnp.log2(sum(jnp.exp2(part - top) for part in parts))


def exchange_lse(part, axis):
    near = near_count(axis)
    if near > 1:
        part = merge_lse([part] + [swap(part, axis, d) for d in range(1, near)])
    return [part] + [swap(part, axis, near * k) for k in range(1, 4)]


def shared_rows():
    return near_count("tgt") == 2 and near_count("src") == 1


def is_odd():
    return lax.rem(lax.axis_index("tgt"), 2) == 1


def exchange_plain(part, sb):
    return jnp.concatenate([merge_lse(exchange_lse(part[:sb], "tgt")), merge_lse(exchange_lse(part[sb:], "src"))])


def exchange_first(part, sb):
    other = swap(part, "tgt", 1)
    rows = merge_lse([part[:sb], other[:sb]])
    part = jnp.where(is_odd(), padded(rows, part), jnp.concatenate([part[sb:], other[sb:]]))
    return exchange_shared(part, 1)


def padded(rows, part):
    return jnp.concatenate([rows] * (part.shape[0] // rows.shape[0]))


def exchange_shared(part, row_side):
    ntgt, nsrc = lax.axis_size("tgt"), lax.axis_size("src")

    def swap_far(k):
        pairs = [
            (s * ntgt + t, s * ntgt + (t ^ (2 * k)) if t % 2 == row_side else (s ^ FAR[k]) * ntgt + t)
            for s in range(nsrc)
            for t in range(ntgt)
        ]
        return lax.ppermute(part, ("src", "tgt"), pairs)

    return merge_lse([part] + [swap_far(k) for k in range(1, 4)])


def gather_points(x_piece, y_piece, y_rows):
    nx, ny = near_count("tgt"), near_count("src")
    y_two = swap(y_piece, "src", 2 * ny)
    y_one, y_three = swap(y_piece, "src", ny), swap(y_piece, "src", 3 * ny)
    x_far = [swap(x_piece, "tgt", nx * k) for k in range(1, 4)]
    y_one, y_three, *x_far = lax.optimization_barrier((y_one, y_three, *x_far))
    y_found = [(0, 0, y_piece), (ny, 0, y_one), (2 * ny, 0, y_two), (3 * ny, 0, y_three)]
    x_found = [(0, 0, x_piece)] + [(nx * k, 0, x_far[k - 1]) for k in range(1, 4)]
    return spread_near(x_found, "tgt"), spread_near(y_found, "src")


def spread_near(found, axis):
    near = near_count(axis)
    arrays, parts = [], []
    for d in range(near):
        for mask, first, array in found:
            parts.append((mask ^ d, first, len(arrays), array.shape[0]))
            arrays.append(swap(array, axis, d) if d else array)
    return arrays, parts


def whole_block(ref, k):
    piece = ref[:, k]
    return piece.reshape(piece.shape[0] * piece.shape[1], piece.shape[2])


def split_columns(vec, split_ref):
    blocks, slots = vec.shape
    vec = vec * (1.0 / UNIT)
    parts = []
    for _ in range(3):
        part = vec.astype(jnp.bfloat16).astype(jnp.float32)
        parts.append(part)
        vec = vec - part
    parts.append(jnp.zeros((LANES - 3 * blocks, slots), jnp.float32))
    split_ref[...] = jnp.concatenate(parts, axis=0).T.astype(jnp.bfloat16)


def column_scores(stream_ref, q, half, split_ref, blocks, k, lane_ref, p):
    if half is None:
        stream, split = whole_block(stream_ref, q), split_ref[...]
    else:
        pieces, _, piece, width = stream_ref.shape
        rows = pieces // 2 * piece
        stream = stream_ref[pl.ds(half * (pieces // 2), pieces // 2), q].reshape(rows, width)
        split = split_ref[pl.ds(pl.multiple_of(half * rows, rows), rows)]
    lane = lax.broadcasted_iota(jnp.int32, (16, LANES), 1)
    pick = jnp.where((lane < 3 * blocks) & (lax.rem(lane, blocks) == k), 1.0, 0.0).astype(jnp.bfloat16)
    pick = jnp.concatenate([pick] * (split_ref.shape[0] // 16), axis=0)
    score = lax.dot_general(
        jnp.concatenate([stream, split], axis=1),
        jnp.concatenate([whole_block(lane_ref, p), pick], axis=1),
        (((1,), (1,)), ((), ())),
        preferred_element_type=jnp.float32,
    )
    return score, jnp.max(score, axis=0, keepdims=True)


def column_lse(*operands):
    score, peak = column_scores(*operands)
    return peak * UNIT, jnp.sum(jnp.exp2((score - peak) * UNIT), axis=0, keepdims=True)


def slots_of(tile, vec):
    found = vec[:, :LANES]
    for t in range(1, vec.shape[1] // LANES):
        found = jnp.where(tile == t, vec[:, t * LANES : (t + 1) * LANES], found)
    return found


def clear(peak_ref, sum_ref):
    peak_ref[...] = jnp.full(peak_ref.shape, FLOOR, jnp.float32)
    sum_ref[...] = jnp.zeros(sum_ref.shape, jnp.float32)


def merge_slots(peak, total, count):
    shape = (count, peak.shape[0] // count, peak.shape[1])
    peak = peak.reshape(shape)
    top = jnp.max(peak, axis=1, keepdims=True)
    total = jnp.sum(total.reshape(shape) * jnp.exp2(peak - top), axis=1)
    return top[:, 0] + jnp.log2(jnp.maximum(total, 1.0))


def list_place(kind, sb, tb):
    return kind, 3 + 2 * kind * sb * tb - (sb * tb if kind == 3 else 0)


def whole_pairs(sb, tb, list_ref):
    at, start = list_place(2, sb, tb)
    count = list_ref[at]

    def pair(place):
        code = list_ref[start + jnp.minimum(place, count - 1)]
        return code // tb, lax.rem(code, tb)

    return count, pair


def pair_list(rows, sb, tb, list_ref, other_ref=None):
    at, start = list_place(0 if rows else 1, sb, tb)
    own = list_ref[at]
    count = own if other_ref is None else own + other_ref[at]

    def pair(place):
        place = jnp.minimum(place, count - 1)
        if other_ref is None:
            code, shift = list_ref[start + place], 0
        else:
            mine = place < own
            here = list_ref[start + jnp.where(mine, place, 0)]
            there = other_ref[start + jnp.where(mine, 0, place - own)]
            code, shift = jnp.where(mine, here, there), jnp.where(mine, 0, tb)
        block = code // 2
        return block // tb, lax.rem(block, tb) + shift, lax.rem(code, 2)

    return count, pair


def visit_groups(pairs, first, last, size, work):
    count, pair = pairs

    @pl.loop(0, pl.cdiv(last - first, size))
    def _(step):
        places = [first + step * size + k for k in range(size)]
        work([pair(place) + (place < count,) for place in places])


def visit_pairs(pairs, group, work):
    count = pairs[0]
    rest = lax.rem(count, group)
    large = jnp.where(rest > group // 2, count, count - rest)
    middle = jnp.where(rest > group // 4, count, large)
    visit_groups(pairs, 0, large, group, work)
    visit_groups(pairs, large, middle, group // 2, work)
    visit_groups(pairs, middle, count, group // 4, work)


def half_sweep(lists, rows, x_ref, y_ref, own, held, vec, scratch):
    split_ref, peak_ref, sum_ref = scratch
    sb = x_ref.shape[1]
    used = 2 * sb * held
    split_columns(vec, split_ref)
    clear(peak_ref, sum_ref)

    def work(group):
        found = []
        for p, q, half, _ in group:
            if rows:
                found.append(((p * held + q) * 2 + half, column_lse(y_ref, q, half, split_ref, held, q, x_ref, p)))
            else:
                found.append(((q * sb + p) * 2 + half, column_lse(x_ref, p, half, split_ref, sb, p, y_ref, q)))
        for slot, pair in found:
            peak_ref[pl.ds(slot, 1), :], sum_ref[pl.ds(slot, 1), :] = pair

    visit_pairs(pair_list(rows, sb, own, *lists), GROUP, work)
    return merge_slots(peak_ref[:used], sum_ref[:used], sb if rows else held)


def half_scratch(sb, tb, blk):
    return [
        pltpu.VMEM((blk, LANES), jnp.bfloat16),
        pltpu.VMEM((2 * sb * tb, blk), jnp.float32),
        pltpu.VMEM((2 * sb * tb, blk), jnp.float32),
    ]


def sweep_own(list_ref, x_ref, y_ref, u, h, part_ref, scratch):
    sb, tb = u.shape[0], h.shape[0]
    part_ref[:sb] = half_sweep([list_ref], True, x_ref, y_ref, tb, tb, h, scratch)
    part_ref[sb:] = half_sweep([list_ref], False, x_ref, y_ref, tb, tb, u, scratch)


def sweep_shared(row_side, lists, x_ref, y_ref, u, h, part_ref, scratch):
    sb, held = u.shape[0], h.shape[0]
    odd = is_odd()
    summing_rows = odd if row_side else jnp.logical_not(odd)

    @pl.when(summing_rows)
    def _():
        rows = half_sweep(lists, True, x_ref, y_ref, held // 2, held, h, scratch)
        part_ref[...] = padded(rows, part_ref)

    @pl.when(jnp.logical_not(summing_rows))
    def _():
        part_ref[...] = half_sweep(lists, False, x_ref, y_ref, held // 2, held, u, scratch)


def project_scratch(sb, tb, blk, width):
    return [
        pltpu.VMEM((blk, LANES), jnp.bfloat16),
        pltpu.VMEM((tb, width, blk), jnp.bfloat16),
        pltpu.VMEM((sb + 1, 1, blk), jnp.float32),
        pltpu.VMEM((sb + 1, 1, blk), jnp.float32),
        pltpu.VMEM((sb + 1, width, blk), jnp.float32),
        pltpu.VMEM((sb, blk, width), jnp.float32),
    ]


def list_kernel(blk, keep_ref, src_counts_ref, tgt_counts_ref, x_in_ref, y_in_ref, list_ref, x_ref, y_ref):
    sb, tb = keep_ref.shape
    x_ref[...] = x_in_ref[...]
    y_ref[...] = y_in_ref[...]
    half = blk // 2
    src_parts = [1 + (src_counts_ref[p] > half).astype(jnp.int32) for p in range(sb)]
    tgt_parts = [1 + (tgt_counts_ref[q] > half).astype(jnp.int32) for q in range(tb)]
    starts = [list_place(kind, sb, tb)[1] for kind in range(4)]
    counts_at = starts[3]
    found = [jnp.int32(0)] * 3
    for p in range(sb):
        for q in range(tb):
            kept = keep_ref[p, q] > 0
            code = p * tb + q
            for k, parts in enumerate((tgt_parts[q], src_parts[p])):
                list_ref[starts[k] + found[k]] = 2 * code
                list_ref[starts[k] + found[k] + 1] = 2 * code + 1
                found[k] = found[k] + jnp.where(kept, parts, 0)
            list_ref[starts[2] + found[2]] = code
            found[2] = found[2] + kept.astype(jnp.int32)
    list_ref[0], list_ref[1], list_ref[2] = found
    for k in range(sb):
        list_ref[counts_at + k] = src_counts_ref[k]
    for k in range(tb):
        list_ref[counts_at + sb + k] = tgt_counts_ref[k]


def assemble(place, list_ref, counts_at, parts, part_refs, points_ref, vec_ref):
    n, blocks, piece, width = points_ref.shape
    blk = n * piece
    vec_ref[...] = jnp.zeros(vec_ref.shape, jnp.float32)
    for mask, first, k, count in parts:
        owner = jnp.bitwise_xor(place, mask)
        rows = min(count, blocks * piece - first)
        points_ref[owner, first // piece : (first + rows) // piece] = part_refs[k][:rows].reshape(
            rows // piece, piece, width
        )
        if rows < count:
            vecs = part_refs[k][rows:count].astype(jnp.float32)
            tile = owner * piece // LANES
            vec_ref[0, tile] += vecs[:blocks]
            vec_ref[1, tile] += vecs[blocks:]
    mass = jnp.concatenate([vec_ref[0, t] for t in range(blk // LANES)], axis=1)
    potential = jnp.concatenate([vec_ref[1, t] for t in range(blk // LANES)], axis=1) * UNIT
    block_of = lax.broadcasted_iota(jnp.int32, (blocks, blk), 0)
    slot_of = lax.broadcasted_iota(jnp.int32, (blocks, blk), 1)
    half = jnp.zeros((blocks, blk), jnp.float32)
    count = jnp.zeros((blocks, blk), jnp.int32)
    ones = jnp.ones((blocks, width), jnp.bfloat16)
    for k in range(blocks):
        wide = whole_block(points_ref, k).astype(jnp.float32)
        square = wide * wide
        high = square.astype(jnp.bfloat16)
        low = (square - high.astype(jnp.float32)).astype(jnp.bfloat16)
        norm = sum(
            lax.dot_general(ones, part, (((1,), (1,)), ((), ())), preferred_element_type=jnp.float32)
            for part in (high, low)
        )
        half = jnp.where(block_of == k, norm * (0.5 * UNIT), half)
        count = jnp.where(block_of == k, list_ref[counts_at + k], count)
    base = jnp.where(slot_of < count, jnp.log2(mass) - half, FLOOR)
    return potential, half, base


def first_kernel(x_parts, y_parts, list_ref, *refs):
    nx = 1 + max(part[2] for part in x_parts)
    ny = 1 + max(part[2] for part in y_parts)
    x_in, y_in, refs = refs[:nx], refs[nx : nx + ny], refs[nx + ny :]
    x_ref, y_ref, xfixed_ref, yfixed_ref, f_ref, part_ref, xvec_ref, yvec_ref = refs[:8]
    sb, tb = x_ref.shape[1], y_ref.shape[1]
    counts_at = list_place(3, sb, tb)[1]
    f, x_half, x_base = assemble(lax.axis_index("tgt"), list_ref, counts_at, x_parts, x_in, x_ref, xvec_ref)
    g, y_half, y_base = assemble(lax.axis_index("src"), list_ref, counts_at + sb, y_parts, y_in, y_ref, yvec_ref)
    f_ref[...] = f
    xfixed_ref[0], xfixed_ref[1] = x_half, x_base
    yfixed_ref[0], yfixed_ref[1], yfixed_ref[2] = y_half, y_base, g
    sweep_own(list_ref, x_ref, y_ref, f + x_base, g + y_base, part_ref, refs[8:])


def updated(old, half, lse):
    return 0.5 * (old + (half - lse))


def turned(cols):
    tb = cols.shape[0] // 2
    return jnp.concatenate([cols[tb:], cols[:tb]])


def second_kernel(list_ref, list2_ref, x_ref, y1_ref, y2_ref, xfixed_ref, yfixed1_ref, yfixed2_ref, f_in_ref, *refs):
    whole_ref, y_ref, yfixed_ref, mine_ref, part_ref = refs[:5]
    sb, tb = x_ref.shape[1], y1_ref.shape[1]
    y_ref[:, :tb] = y1_ref[...]
    y_ref[:, tb:] = y2_ref[...]
    half, base, g = [jnp.concatenate([yfixed1_ref[k], yfixed2_ref[k]]) for k in range(3)]
    yfixed_ref[0], yfixed_ref[1] = half, base
    f = updated(f_in_ref[...], xfixed_ref[0], whole_ref[:sb])
    g = updated(g, half, whole_ref[...])
    mine_ref[...] = jnp.where(is_odd(), padded(f, g), g)
    sweep_shared(0, [list_ref, list2_ref], x_ref, y_ref, f + xfixed_ref[1], g + base, part_ref, refs[5:])


def shared_kernel(row_side, list_ref, list2_ref, x_ref, y_ref, xfixed_ref, yfixed_ref, whole_ref, old_ref, *refs):
    mine_ref, part_ref = refs[:2]
    sb = x_ref.shape[1]
    f = updated(old_ref[:sb], xfixed_ref[0], whole_ref[:sb])
    g = updated(turned(old_ref[...]), yfixed_ref[0], whole_ref[...])
    mine_ref[...] = jnp.where(is_odd(), g, padded(f, g)) if row_side else jnp.where(is_odd(), padded(f, g), g)
    lists = [list_ref, list2_ref]
    sweep_shared(row_side, lists, x_ref, y_ref, f + xfixed_ref[1], g + yfixed_ref[1], part_ref, refs[2:])


def step_kernel(list_ref, x_ref, y_ref, xfixed_ref, yfixed_in_ref, f_in_ref, whole_ref, *refs):
    yfixed_ref, f_ref, part_ref = refs[:3]
    sb = x_ref.shape[1]
    f = updated(f_in_ref[...], xfixed_ref[0], whole_ref[:sb])
    half, base, g = [yfixed_in_ref[k] for k in range(3)]
    g = updated(g, half, whole_ref[sb:])
    f_ref[...] = f
    yfixed_ref[0], yfixed_ref[1], yfixed_ref[2] = half, base, g
    sweep_own(list_ref, x_ref, y_ref, f + xfixed_ref[1], g + base, part_ref, refs[3:])


def last_cols_kernel(row_side, list_ref, x_ref, y_ref, xfixed_ref, yfixed_in_ref, *refs):
    if row_side is None:
        f_in_ref, whole_ref, yfixed_ref, f_ref, cols_ref = refs[:5]
        scratch = refs[5:]
        sb, tb = x_ref.shape[1], cols_ref.shape[0]
        old_f, old_g = f_in_ref[...], yfixed_in_ref[2]
        rows, cols = whole_ref[:sb], whole_ref[sb:]
    else:
        whole_ref, whole2_ref, mine_ref, mine2_ref, yfixed_ref, f_ref, cols_ref = refs[:7]
        scratch = refs[7:]
        sb, tb = x_ref.shape[1], cols_ref.shape[0]
        has_rows = is_odd() if row_side else jnp.logical_not(is_odd())
        rows = jnp.where(has_rows, whole_ref[:sb], whole2_ref[:sb])
        cols = jnp.where(has_rows, whole2_ref[tb:], whole_ref[:tb])
        old_f = jnp.where(has_rows, mine2_ref[:sb], mine_ref[:sb])
        old_g = jnp.where(has_rows, mine_ref[:tb], mine2_ref[tb:])
    f = updated(old_f, xfixed_ref[0], rows)
    half, base = yfixed_in_ref[0, :tb], yfixed_in_ref[1, :tb]
    f_ref[...] = f
    yfixed_ref[0], yfixed_ref[1], yfixed_ref[2] = half, base, updated(old_g, half, cols)
    cols_ref[...] = half_sweep([list_ref], False, x_ref, y_ref, tb, tb, f + xfixed_ref[1], scratch)


def last_rows_kernel(list_ref, x_ref, y_ref, yfixed_ref, rows_ref, split_ref, peak_ref, sum_ref):
    sb, tb = x_ref.shape[1], yfixed_ref.shape[1]
    split_columns(yfixed_ref[2] + yfixed_ref[1], split_ref)
    clear(peak_ref, sum_ref)

    def work(group):
        found = [(p * tb + q, column_lse(y_ref, q, None, split_ref, tb, q, x_ref, p)) for p, q, _ in group]
        for slot, pair in found:
            peak_ref[pl.ds(slot, 1), :], sum_ref[pl.ds(slot, 1), :] = pair

    visit_pairs(whole_pairs(sb, tb, list_ref), GROUP // 2, work)
    rows_ref[...] = merge_slots(peak_ref[: sb * tb], sum_ref[: sb * tb], sb)


def project_kernel(near, list_ref, x_ref, y_ref, yfixed_ref, rows_ref, *refs):
    col_refs, g_ref, out_refs = refs[:4], refs[4], refs[5 : 5 + near]
    split_ref, turned_ref, peak_ref, sum_ref, acc_ref, image_ref = refs[5 + near :]
    n, sb, piece, width = x_ref.shape
    tb = g_ref.shape[0]
    blk = n * piece
    g = updated(yfixed_ref[2], yfixed_ref[0], merge_lse([ref[...] for ref in col_refs]))
    g_ref[...] = g * (1.0 / UNIT)
    split_columns(g + yfixed_ref[1], split_ref)
    for q in range(tb):
        turned_ref[q] = whole_block(y_ref, q).T
    clear(peak_ref, sum_ref)
    acc_ref[...] = jnp.zeros(acc_ref.shape, jnp.float32)

    def move(group):
        found = []
        for p, q, real in group:
            score, peak = column_scores(y_ref, q, None, split_ref, tb, q, x_ref, p)
            weights = jnp.exp2((score - peak) * UNIT)
            high = weights.astype(jnp.bfloat16)
            low = (weights - high.astype(jnp.float32)).astype(jnp.bfloat16)
            ys = turned_ref[q]
            moved = jnp.dot(ys, high, preferred_element_type=jnp.float32) + jnp.dot(
                ys, low, preferred_element_type=jnp.float32
            )
            found.append((jnp.where(real, p, sb), peak * UNIT, jnp.sum(weights, axis=0, keepdims=True), moved))
        for p, peak, total, moved in found:
            old = peak_ref[p]
            new = jnp.maximum(old, peak)
            before, here = jnp.exp2(old - new), jnp.exp2(peak - new)
            peak_ref[p] = new
            sum_ref[p] = sum_ref[p] * before + total * here
            acc_ref[p] = acc_ref[p] * before + moved * here

    pairs = whole_pairs(sb, tb, list_ref)
    rest = lax.rem(pairs[0], MOVE_GROUP)
    large = jnp.where(rest > MOVE_GROUP // 2, pairs[0], pairs[0] - rest)
    visit_groups(pairs, 0, large, MOVE_GROUP, move)
    visit_groups(pairs, large, pairs[0], MOVE_GROUP // 2, move)
    rows = []
    for p in range(sb):
        total = jnp.maximum(sum_ref[p], 1.0)
        image_ref[p] = (acc_ref[p] / total).T
        rows.append(peak_ref[p] + jnp.log2(total))
    lse = jnp.concatenate(rows, axis=0)

    me = lax.rem(lax.axis_index("tgt"), near)
    for e, out_ref in enumerate(out_refs):
        for far in range(4):
            owner = far * near + jnp.bitwise_xor(me, e)
            for p in range(sb):
                out_ref[far, p * piece : (p + 1) * piece] = image_ref[p, pl.ds(pl.multiple_of(owner * piece, piece), piece)]
            tile = owner * piece // LANES
            out_ref[far, sb * piece : sb * (piece + 1)] = slots_of(tile, lse)
            out_ref[far, sb * (piece + 1) :] = slots_of(tile, rows_ref[...])


def merge_images(parts, offset, sb, piece, turn_ref):
    whole = merge_lse([lse for _, lse in parts])
    weights = []
    for k, (_, lse) in enumerate(parts):
        turn_ref[k] = jnp.exp2(lse - whole).T
        weights.append(turn_ref[k, pl.ds(offset, piece), :])
    images = []
    for p in range(sb):
        images.append(
            sum(
                image[p * piece : (p + 1) * piece] * weight[:, p : p + 1]
                for (image, _), weight in zip(parts, weights)
            )
        )
    return images, whole


def near_kernel(near, sb, piece, *refs):
    in_refs, out_refs, turn_ref = refs[:near], refs[near : near + 4], refs[near + 4]
    place = lax.axis_index("tgt")
    me, mine = lax.rem(place, near), place // near
    rows = sb * piece
    for d, out_ref in enumerate(out_refs):
        far = jnp.bitwise_xor(mine, d)
        offset = lax.rem((far * near + me) * piece, LANES)
        parts = [(ref[far, :rows], ref[far, rows : rows + sb]) for ref in in_refs]
        images, whole = merge_images(parts, pl.multiple_of(offset, piece), sb, piece, turn_ref)
        for p in range(sb):
            out_ref[p * piece : (p + 1) * piece] = images[p]
        out_ref[rows : rows + sb] = whole
        out_ref[rows + sb :] = merge_lse([ref[far, rows + sb :] for ref in in_refs])


def far_kernel(sb, piece, xfixed_ref, f_in_ref, *refs):
    in_refs, out_ref, f_ref, turn_ref = refs[:4], refs[4], refs[5], refs[6]
    rows = sb * piece
    start = lax.axis_index("tgt") * piece
    offset = lax.rem(start, LANES)
    parts = [(ref[:rows], ref[rows : rows + sb]) for ref in in_refs]
    images, _ = merge_images(parts, pl.multiple_of(offset, piece), sb, piece, turn_ref)
    for p in range(sb):
        out_ref[p] = images[p]
    tile = start // LANES
    lse = merge_lse([ref[rows + sb :] for ref in in_refs])
    f = updated(slots_of(tile, f_in_ref[...]), slots_of(tile, xfixed_ref[0]), lse)
    f_ref[...] = pltpu.roll(f * (1.0 / UNIT), lax.rem(LANES - offset, LANES), 1)[:, :piece]


def pack_kernel(*refs):
    for k, axis in enumerate(("tgt", "src")):
        points_ref, mass_ref, potential_ref = refs[3 * k : 3 * k + 3]
        out_ref = refs[6 + k]
        blocks, piece, width = points_ref.shape
        here = lax.rem(lax.axis_index(axis) * piece, LANES)
        slot = lax.broadcasted_iota(jnp.int32, (piece, LANES), 0)
        lane = lax.broadcasted_iota(jnp.int32, (piece, LANES), 1)
        put = jnp.where(lane == slot + here, 1.0, 0.0).astype(jnp.bfloat16)
        vecs = [jnp.dot(ref[...], put, preferred_element_type=jnp.float32) for ref in (mass_ref, potential_ref)]
        out_ref[: blocks * piece] = points_ref[...].reshape(blocks * piece, width)
        out_ref[blocks * piece :] = jnp.concatenate(vecs, axis=0).astype(jnp.bfloat16)


def on_device(
    src_points, tgt_points, src_mass, tgt_mass, src_potential, tgt_potential, src_counts, tgt_counts, keep
):
    ntgt, nsrc = lax.axis_size("tgt"), lax.axis_size("src")
    near = near_count("tgt")
    sb, src_piece, width = src_points.shape
    tb, tgt_piece, _ = tgt_points.shape
    blk = src_piece * ntgt
    x_rows, y_rows = sb * src_piece, tb * tgt_piece
    x_packed, y_packed = pl.pallas_call(
        pack_kernel,
        out_shape=(
            jax.ShapeDtypeStruct((x_rows + 2 * sb, width), jnp.bfloat16),
            jax.ShapeDtypeStruct((y_rows + 2 * tb, width), jnp.bfloat16),
        ),
        in_specs=[VMEM] * 6,
        out_specs=(VMEM, VMEM),
        name="pack",
    )(src_points, src_mass, src_potential, tgt_points, tgt_mass, tgt_potential)
    (x_in, x_parts), (y_in, y_parts) = gather_points(x_packed, y_packed, y_rows)
    pairs, x_own, y_own = pl.pallas_call(
        functools.partial(list_kernel, blk),
        out_shape=(
            jax.ShapeDtypeStruct((list_place(3, sb, tb)[1] + sb + tb,), jnp.int32),
            jax.ShapeDtypeStruct(x_packed.shape, x_packed.dtype),
            jax.ShapeDtypeStruct(y_packed.shape, y_packed.dtype),
        ),
        in_specs=[SMEM] * 3 + [VMEM] * 2,
        out_specs=(SMEM, VMEM, VMEM),
        compiler_params=PARAMS,
        name="kept_pairs",
    )(keep, src_counts, tgt_counts, x_packed, y_packed)
    x_in[0], y_in[0] = x_own, y_own

    def half_room(targets):
        return dict(scratch_shapes=half_scratch(sb, targets, blk), compiler_params=PARAMS)

    shared = shared_rows()
    x, y, xfixed, yfixed, f, part = pl.pallas_call(
        functools.partial(first_kernel, x_parts, y_parts),
        out_shape=(
            jax.ShapeDtypeStruct((ntgt, sb, src_piece, width), jnp.bfloat16),
            jax.ShapeDtypeStruct((nsrc, tb, tgt_piece, width), jnp.bfloat16),
            f32(2, sb, blk),
            f32(3, tb, blk),
            f32(sb, blk),
            f32(sb + tb, blk),
        ),
        in_specs=[SMEM] + [VMEM] * (len(x_in) + len(y_in)),
        out_specs=(VMEM,) * 6,
        scratch_shapes=[
            pltpu.VMEM((2, blk // LANES, sb, LANES), jnp.float32),
            pltpu.VMEM((2, blk // LANES, tb, LANES), jnp.float32),
        ]
        + half_scratch(sb, tb, blk),
        compiler_params=PARAMS,
        name="first_sweep",
    )(pairs, *x_in, *y_in)

    if shared:
        pairs_two, y_two, yfixed_two = [swap(array, "tgt", 1) for array in (pairs, y, yfixed)]
        pairs_two, part = lax.optimization_barrier((pairs_two, part))
        whole = exchange_first(part, sb)
        y, yfixed, mine, part = pl.pallas_call(
            second_kernel,
            out_shape=(
                jax.ShapeDtypeStruct((nsrc, 2 * tb, tgt_piece, width), jnp.bfloat16),
                f32(2, 2 * tb, blk),
                f32(2 * tb, blk),
                f32(2 * tb, blk),
            ),
            in_specs=[SMEM] * 2 + [VMEM] * 8,
            out_specs=(VMEM,) * 4,
            name="second_sweep",
            **half_room(2 * tb),
        )(pairs, pairs_two, x, y, y_two, xfixed, yfixed, yfixed_two, f, whole)
        for k in range(2, ITERS - 1):
            old, whole = swap(mine, "tgt", 1), exchange_shared(part, (k - 1) % 2 ^ 1)
            mine, part = pl.pallas_call(
                functools.partial(shared_kernel, k % 2 ^ 1),
                out_shape=(f32(2 * tb, blk), f32(2 * tb, blk)),
                in_specs=[SMEM] * 2 + [VMEM] * 6,
                out_specs=(VMEM, VMEM),
                name="sweep",
                **half_room(2 * tb),
            )(pairs, pairs_two, x, y, xfixed, yfixed, whole, old)
        row_side = (ITERS - 2) % 2 ^ 1
        old, whole = swap(mine, "tgt", 1), exchange_shared(part, row_side)
        last = (whole, swap(whole, "tgt", 1), mine, old)
    else:
        step = pl.pallas_call(
            step_kernel,
            out_shape=(f32(3, tb, blk), f32(sb, blk), f32(sb + tb, blk)),
            in_specs=[SMEM] + [VMEM] * 6,
            out_specs=(VMEM,) * 3,
            name="sweep",
            **half_room(tb),
        )
        for _ in range(ITERS - 2):
            yfixed, f, part = step(pairs, x, y, xfixed, yfixed, f, exchange_plain(part, sb))
        row_side, last = None, (f, exchange_plain(part, sb))

    yfixed, f, cols = pl.pallas_call(
        functools.partial(last_cols_kernel, row_side),
        out_shape=(f32(3, tb, blk), f32(sb, blk), f32(tb, blk)),
        in_specs=[SMEM] + [VMEM] * (4 + len(last)),
        out_specs=(VMEM,) * 3,
        name="last_cols",
        **half_room(tb),
    )(pairs, x, y, xfixed, yfixed, *last)
    col_parts = exchange_lse(cols, "src")
    rows = pl.pallas_call(
        last_rows_kernel,
        out_shape=f32(sb, blk),
        in_specs=[SMEM] + [VMEM] * 3,
        out_specs=VMEM,
        name="last_rows",
        **half_room(tb),
    )(pairs, x, y, yfixed)
    rows, *col_parts = lax.optimization_barrier((rows, *col_parts))
    tile = sb * (src_piece + 2)
    g, *near_parts = pl.pallas_call(
        functools.partial(project_kernel, near),
        out_shape=(f32(tb, blk),) + (f32(4, tile, width),) * near,
        in_specs=[SMEM] + [VMEM] * 8,
        out_specs=(VMEM,) * (1 + near),
        scratch_shapes=project_scratch(sb, tb, blk, width),
        compiler_params=PARAMS,
        name="project",
    )(pairs, x, y, yfixed, rows, *col_parts)
    if near > 1:
        near_parts = near_parts[:1] + [swap(near_parts[d], "tgt", d) for d in range(1, near)]
    far_parts = pl.pallas_call(
        functools.partial(near_kernel, near, sb, src_piece),
        out_shape=(f32(tile, width),) * 4,
        in_specs=[VMEM] * near,
        out_specs=(VMEM,) * 4,
        scratch_shapes=[pltpu.VMEM((near, LANES, sb), jnp.float32)],
        compiler_params=PARAMS,
        name="merge_near",
    )(*near_parts)
    far_parts = [far_parts[0]] + [swap(far_parts[k], "tgt", near * k) for k in range(1, 4)]
    images, src_final = pl.pallas_call(
        functools.partial(far_kernel, sb, src_piece),
        out_shape=(f32(sb, src_piece, width), f32(sb, src_piece)),
        in_specs=[VMEM] * 6,
        out_specs=(VMEM, VMEM),
        scratch_shapes=[pltpu.VMEM((4, LANES, sb), jnp.float32)],
        compiler_params=PARAMS,
        name="merge_far",
    )(xfixed, f, *far_parts)

    tgt_final = lax.dynamic_slice_in_dim(g, lax.axis_index("src") * tgt_piece, tgt_piece, 1)
    return images, src_final, tgt_final


def solution(mesh):
    return jax.shard_map(
        on_device,
        mesh=mesh,
        in_specs=(
            P("src", "tgt", None),
            P("tgt", "src", None),
            P("src", "tgt"),
            P("tgt", "src"),
            P("src", "tgt"),
            P("tgt", "src"),
            P("src"),
            P("tgt"),
            P("src", "tgt"),
        ),
        out_specs=(P("src", "tgt", None), P("src", "tgt"), P("tgt", "src")),
        check_vma=False,
    )
```

```python
import functools
import math

import jax
import jax.numpy as jnp
from jax import lax
from jax.experimental import pallas as pl
from jax.experimental.pallas import tpu as pltpu
from jax.sharding import PartitionSpec as P

ITERS = 4
EPSILON = 0.1
UNIT = 1.0 / (EPSILON * math.log(2.0))
FLOOR = -1e30
LANES = 128
FAR = (0, 1, 3, 2)
GROUP = 16
MOVE_GROUP = 6

SMEM = pl.BlockSpec(memory_space=pltpu.SMEM)
VMEM = pl.BlockSpec(memory_space=pltpu.VMEM)
PARAMS = pltpu.CompilerParams(vmem_limit_bytes=40 * 1024 * 1024)


def f32(*shape):
    return jax.ShapeDtypeStruct(shape, jnp.float32)


def swap(part, axis, mask):
    return lax.ppermute(part, axis, [(i, i ^ mask) for i in range(lax.axis_size(axis))])


def near_count(axis):
    return lax.axis_size(axis) // 4


def merge_lse(parts):
    top = functools.reduce(jnp.maximum, parts)
    return top + jnp.log2(sum(jnp.exp2(part - top) for part in parts))


def exchange_lse(part, axis):
    near = near_count(axis)
    if near > 1:
        part = merge_lse([part] + [swap(part, axis, d) for d in range(1, near)])
    return [part] + [swap(part, axis, near * k) for k in range(1, 4)]


def shared_rows():
    return near_count("tgt") == 2 and near_count("src") == 1


def is_odd():
    return lax.rem(lax.axis_index("tgt"), 2) == 1


def exchange_plain(part, sb):
    return jnp.concatenate([merge_lse(exchange_lse(part[:sb], "tgt")), merge_lse(exchange_lse(part[sb:], "src"))])


def exchange_first(part, sb):
    other = swap(part, "tgt", 1)
    rows = merge_lse([part[:sb], other[:sb]])
    part = jnp.where(is_odd(), padded(rows, part), jnp.concatenate([part[sb:], other[sb:]]))
    return exchange_shared(part, 1)


def padded(rows, part):
    return jnp.concatenate([rows] * (part.shape[0] // rows.shape[0]))


def exchange_shared(part, row_side):
    ntgt, nsrc = lax.axis_size("tgt"), lax.axis_size("src")

    def swap_far(k):
        pairs = [
            (s * ntgt + t, s * ntgt + (t ^ (2 * k)) if t % 2 == row_side else (s ^ FAR[k]) * ntgt + t)
            for s in range(nsrc)
            for t in range(ntgt)
        ]
        return lax.ppermute(part, ("src", "tgt"), pairs)

    return merge_lse([part] + [swap_far(k) for k in range(1, 4)])


def gather_points(x_piece, y_piece, y_rows):
    nx, ny = near_count("tgt"), near_count("src")
    y_two = swap(y_piece, "src", 2 * ny)
    y_one, y_three = swap(y_piece, "src", ny), swap(y_piece, "src", 3 * ny)
    x_far = [swap(x_piece, "tgt", nx * k) for k in range(1, 4)]
    y_one, y_three, *x_far = lax.optimization_barrier((y_one, y_three, *x_far))
    y_found = [(0, 0, y_piece), (ny, 0, y_one), (2 * ny, 0, y_two), (3 * ny, 0, y_three)]
    x_found = [(0, 0, x_piece)] + [(nx * k, 0, x_far[k - 1]) for k in range(1, 4)]
    return spread_near(x_found, "tgt"), spread_near(y_found, "src")


def spread_near(found, axis):
    near = near_count(axis)
    arrays, parts = [], []
    for d in range(near):
        for mask, first, array in found:
            parts.append((mask ^ d, first, len(arrays), array.shape[0]))
            arrays.append(swap(array, axis, d) if d else array)
    return arrays, parts


def whole_block(ref, k):
    piece = ref[:, k]
    return piece.reshape(piece.shape[0] * piece.shape[1], piece.shape[2])


def split_columns(vec, split_ref):
    blocks, slots = vec.shape
    vec = vec * (1.0 / UNIT)
    parts = []
    for _ in range(3):
        part = vec.astype(jnp.bfloat16).astype(jnp.float32)
        parts.append(part)
        vec = vec - part
    parts.append(jnp.zeros((LANES - 3 * blocks, slots), jnp.float32))
    split_ref[...] = jnp.concatenate(parts, axis=0).T.astype(jnp.bfloat16)


def column_scores(stream_ref, q, split_ref, blocks, k, lane_ref, p):
    lane = lax.broadcasted_iota(jnp.int32, (16, LANES), 1)
    pick = jnp.where((lane < 3 * blocks) & (lax.rem(lane, blocks) == k), 1.0, 0.0).astype(jnp.bfloat16)
    pick = jnp.concatenate([pick] * (split_ref.shape[0] // 16), axis=0)
    score = lax.dot_general(
        jnp.concatenate([whole_block(stream_ref, q), split_ref[...]], axis=1),
        jnp.concatenate([whole_block(lane_ref, p), pick], axis=1),
        (((1,), (1,)), ((), ())),
        preferred_element_type=jnp.float32,
    )
    return score, jnp.max(score, axis=0, keepdims=True)


def column_lse(*operands):
    score, peak = column_scores(*operands)
    return peak * UNIT, jnp.sum(jnp.exp2((score - peak) * UNIT), axis=0, keepdims=True)


def slots_of(tile, vec):
    found = vec[:, :LANES]
    for t in range(1, vec.shape[1] // LANES):
        found = jnp.where(tile == t, vec[:, t * LANES : (t + 1) * LANES], found)
    return found


def clear(peak_ref, sum_ref):
    peak_ref[...] = jnp.full(peak_ref.shape, FLOOR, jnp.float32)
    sum_ref[...] = jnp.zeros(sum_ref.shape, jnp.float32)


def merge_slots(peak, total, count):
    shape = (count, peak.shape[0] // count, peak.shape[1])
    peak = peak.reshape(shape)
    top = jnp.max(peak, axis=1, keepdims=True)
    total = jnp.sum(total.reshape(shape) * jnp.exp2(peak - top), axis=1)
    return top[:, 0] + jnp.log2(jnp.maximum(total, 1.0))


def pair_list(tb, list_ref, other_ref=None):
    own = list_ref[0]
    count = own if other_ref is None else own + other_ref[0]

    def pair(place):
        place = jnp.minimum(place, count - 1)
        if other_ref is None:
            code, shift = list_ref[1 + place], 0
        else:
            mine = place < own
            here, there = list_ref[1 + jnp.where(mine, place, 0)], other_ref[1 + jnp.where(mine, 0, place - own)]
            code = jnp.where(mine, here, there)
            shift = jnp.where(mine, 0, tb)
        return code // tb, lax.rem(code, tb) + shift

    return count, pair


def visit_pairs(pairs, first, last, group, work):
    count, pair = pairs

    @pl.loop(0, pl.cdiv(last - first, group))
    def _(step):
        places = [first + step * group + k for k in range(group)]
        work([pair(place) + (place < count,) for place in places])


def half_sweep(pairs, rows, x_ref, y_ref, tb, vec, scratch):
    split_ref, peak_ref, sum_ref = scratch
    sb = x_ref.shape[1]
    used = sb * tb
    split_columns(vec, split_ref)
    clear(peak_ref, sum_ref)

    def work(group):
        found = []
        for p, q, _ in group:
            if rows:
                found.append((p * tb + q, column_lse(y_ref, q, split_ref, tb, q, x_ref, p)))
            else:
                found.append((q * sb + p, column_lse(x_ref, p, split_ref, sb, p, y_ref, q)))
        for slot, pair in found:
            peak_ref[pl.ds(slot, 1), :], sum_ref[pl.ds(slot, 1), :] = pair

    count = pairs[0]
    rest = lax.rem(count, GROUP)
    large = jnp.where(rest > GROUP // 2, count, count - rest)
    middle = jnp.where(rest > GROUP // 4, count, large)
    visit_pairs(pairs, 0, large, GROUP, work)
    visit_pairs(pairs, large, middle, GROUP // 2, work)
    visit_pairs(pairs, middle, count, GROUP // 4, work)
    return merge_slots(peak_ref[:used], sum_ref[:used], sb if rows else tb)


def half_scratch(sb, tb, blk):
    return [
        pltpu.VMEM((blk, LANES), jnp.bfloat16),
        pltpu.VMEM((sb * tb, blk), jnp.float32),
        pltpu.VMEM((sb * tb, blk), jnp.float32),
    ]


def sweep_own(pairs, x_ref, y_ref, u, h, part_ref, scratch):
    sb, tb = u.shape[0], h.shape[0]
    part_ref[:sb] = half_sweep(pairs, True, x_ref, y_ref, tb, h, scratch)
    part_ref[sb:] = half_sweep(pairs, False, x_ref, y_ref, tb, u, scratch)


def sweep_shared(row_side, pairs, x_ref, y_ref, u, h, part_ref, scratch):
    sb, tb = u.shape[0], h.shape[0]
    odd = is_odd()
    summing_rows = odd if row_side else jnp.logical_not(odd)

    @pl.when(summing_rows)
    def _():
        part_ref[...] = padded(half_sweep(pairs, True, x_ref, y_ref, tb, h, scratch), part_ref)

    @pl.when(jnp.logical_not(summing_rows))
    def _():
        part_ref[...] = half_sweep(pairs, False, x_ref, y_ref, tb, u, scratch)


def project_scratch(sb, tb, blk, width):
    return [
        pltpu.VMEM((blk, LANES), jnp.bfloat16),
        pltpu.VMEM((tb, width, blk), jnp.bfloat16),
        pltpu.VMEM((sb + 1, 1, blk), jnp.float32),
        pltpu.VMEM((sb + 1, 1, blk), jnp.float32),
        pltpu.VMEM((sb + 1, width, blk), jnp.float32),
        pltpu.VMEM((sb, blk, width), jnp.float32),
    ]


def list_kernel(keep_ref, src_counts_ref, tgt_counts_ref, x_in_ref, y_in_ref, list_ref, x_ref, y_ref):
    sb, tb = keep_ref.shape
    x_ref[...] = x_in_ref[...]
    y_ref[...] = y_in_ref[...]
    counts_at = 1 + sb * tb
    n = jnp.int32(0)
    for code in range(sb * tb):
        list_ref[1 + n] = code
        n = n + (keep_ref[code // tb, code % tb] > 0).astype(jnp.int32)
    list_ref[0] = n
    for k in range(sb):
        list_ref[counts_at + k] = src_counts_ref[k]
    for k in range(tb):
        list_ref[counts_at + sb + k] = tgt_counts_ref[k]


def assemble(place, list_ref, counts_at, parts, part_refs, points_ref, vec_ref):
    n, blocks, piece, width = points_ref.shape
    blk = n * piece
    vec_ref[...] = jnp.zeros(vec_ref.shape, jnp.float32)
    for mask, first, k, count in parts:
        owner = jnp.bitwise_xor(place, mask)
        rows = min(count, blocks * piece - first)
        points_ref[owner, first // piece : (first + rows) // piece] = part_refs[k][:rows].reshape(
            rows // piece, piece, width
        )
        if rows < count:
            vecs = part_refs[k][rows:count].astype(jnp.float32)
            tile = owner * piece // LANES
            vec_ref[0, tile] += vecs[:blocks]
            vec_ref[1, tile] += vecs[blocks:]
    mass = jnp.concatenate([vec_ref[0, t] for t in range(blk // LANES)], axis=1)
    potential = jnp.concatenate([vec_ref[1, t] for t in range(blk // LANES)], axis=1) * UNIT
    block_of = lax.broadcasted_iota(jnp.int32, (blocks, blk), 0)
    slot_of = lax.broadcasted_iota(jnp.int32, (blocks, blk), 1)
    half = jnp.zeros((blocks, blk), jnp.float32)
    count = jnp.zeros((blocks, blk), jnp.int32)
    ones = jnp.ones((blocks, width), jnp.bfloat16)
    for k in range(blocks):
        wide = whole_block(points_ref, k).astype(jnp.float32)
        square = wide * wide
        high = square.astype(jnp.bfloat16)
        low = (square - high.astype(jnp.float32)).astype(jnp.bfloat16)
        norm = sum(
            lax.dot_general(ones, part, (((1,), (1,)), ((), ())), preferred_element_type=jnp.float32)
            for part in (high, low)
        )
        half = jnp.where(block_of == k, norm * (0.5 * UNIT), half)
        count = jnp.where(block_of == k, list_ref[counts_at + k], count)
    base = jnp.where(slot_of < count, jnp.log2(mass) - half, FLOOR)
    return potential, half, base


def first_kernel(x_parts, y_parts, list_ref, *refs):
    nx = 1 + max(part[2] for part in x_parts)
    ny = 1 + max(part[2] for part in y_parts)
    x_in, y_in, refs = refs[:nx], refs[nx : nx + ny], refs[nx + ny :]
    x_ref, y_ref, xfixed_ref, yfixed_ref, f_ref, part_ref, xvec_ref, yvec_ref = refs[:8]
    sb, tb = x_ref.shape[1], y_ref.shape[1]
    counts_at = 1 + sb * tb
    f, x_half, x_base = assemble(lax.axis_index("tgt"), list_ref, counts_at, x_parts, x_in, x_ref, xvec_ref)
    g, y_half, y_base = assemble(lax.axis_index("src"), list_ref, counts_at + sb, y_parts, y_in, y_ref, yvec_ref)
    f_ref[...] = f
    xfixed_ref[0], xfixed_ref[1] = x_half, x_base
    yfixed_ref[0], yfixed_ref[1], yfixed_ref[2] = y_half, y_base, g
    sweep_own(pair_list(tb, list_ref), x_ref, y_ref, f + x_base, g + y_base, part_ref, refs[8:])


def updated(old, half, lse):
    return 0.5 * (old + (half - lse))


def turned(cols):
    tb = cols.shape[0] // 2
    return jnp.concatenate([cols[tb:], cols[:tb]])


def second_kernel(list_ref, list2_ref, x_ref, y1_ref, y2_ref, xfixed_ref, yfixed1_ref, yfixed2_ref, f_in_ref, *refs):
    whole_ref, y_ref, yfixed_ref, mine_ref, part_ref = refs[:5]
    sb, tb = x_ref.shape[1], y1_ref.shape[1]
    y_ref[:, :tb] = y1_ref[...]
    y_ref[:, tb:] = y2_ref[...]
    half, base, g = [jnp.concatenate([yfixed1_ref[k], yfixed2_ref[k]]) for k in range(3)]
    yfixed_ref[0], yfixed_ref[1] = half, base
    f = updated(f_in_ref[...], xfixed_ref[0], whole_ref[:sb])
    g = updated(g, half, whole_ref[...])
    mine_ref[...] = jnp.where(is_odd(), padded(f, g), g)
    sweep_shared(
        0, pair_list(tb, list_ref, list2_ref), x_ref, y_ref, f + xfixed_ref[1], g + base, part_ref, refs[5:]
    )


def shared_kernel(row_side, list_ref, list2_ref, x_ref, y_ref, xfixed_ref, yfixed_ref, whole_ref, old_ref, *refs):
    mine_ref, part_ref = refs[:2]
    sb, tb = x_ref.shape[1], y_ref.shape[1] // 2
    f = updated(old_ref[:sb], xfixed_ref[0], whole_ref[:sb])
    g = updated(turned(old_ref[...]), yfixed_ref[0], whole_ref[...])
    mine_ref[...] = jnp.where(is_odd(), g, padded(f, g)) if row_side else jnp.where(is_odd(), padded(f, g), g)
    pairs = pair_list(tb, list_ref, list2_ref)
    sweep_shared(row_side, pairs, x_ref, y_ref, f + xfixed_ref[1], g + yfixed_ref[1], part_ref, refs[2:])


def step_kernel(list_ref, x_ref, y_ref, xfixed_ref, yfixed_in_ref, f_in_ref, whole_ref, *refs):
    yfixed_ref, f_ref, part_ref = refs[:3]
    sb, tb = x_ref.shape[1], y_ref.shape[1]
    f = updated(f_in_ref[...], xfixed_ref[0], whole_ref[:sb])
    half, base, g = [yfixed_in_ref[k] for k in range(3)]
    g = updated(g, half, whole_ref[sb:])
    f_ref[...] = f
    yfixed_ref[0], yfixed_ref[1], yfixed_ref[2] = half, base, g
    sweep_own(pair_list(tb, list_ref), x_ref, y_ref, f + xfixed_ref[1], g + base, part_ref, refs[3:])


def last_cols_kernel(row_side, list_ref, x_ref, y_ref, xfixed_ref, yfixed_in_ref, *refs):
    if row_side is None:
        f_in_ref, whole_ref, yfixed_ref, f_ref, cols_ref = refs[:5]
        scratch = refs[5:]
        sb, tb = x_ref.shape[1], cols_ref.shape[0]
        old_f, old_g = f_in_ref[...], yfixed_in_ref[2]
        rows, cols = whole_ref[:sb], whole_ref[sb:]
    else:
        whole_ref, whole2_ref, mine_ref, mine2_ref, yfixed_ref, f_ref, cols_ref = refs[:7]
        scratch = refs[7:]
        sb, tb = x_ref.shape[1], cols_ref.shape[0]
        has_rows = is_odd() if row_side else jnp.logical_not(is_odd())
        rows = jnp.where(has_rows, whole_ref[:sb], whole2_ref[:sb])
        cols = jnp.where(has_rows, whole2_ref[tb:], whole_ref[:tb])
        old_f = jnp.where(has_rows, mine2_ref[:sb], mine_ref[:sb])
        old_g = jnp.where(has_rows, mine_ref[:tb], mine2_ref[tb:])
    f = updated(old_f, xfixed_ref[0], rows)
    half, base = yfixed_in_ref[0, :tb], yfixed_in_ref[1, :tb]
    f_ref[...] = f
    yfixed_ref[0], yfixed_ref[1], yfixed_ref[2] = half, base, updated(old_g, half, cols)
    cols_ref[...] = half_sweep(pair_list(tb, list_ref), False, x_ref, y_ref, tb, f + xfixed_ref[1], scratch)


def last_rows_kernel(list_ref, x_ref, y_ref, yfixed_ref, rows_ref, *scratch):
    tb = yfixed_ref.shape[1]
    vec = yfixed_ref[2] + yfixed_ref[1]
    rows_ref[...] = half_sweep(pair_list(tb, list_ref), True, x_ref, y_ref, tb, vec, scratch)


def project_kernel(near, list_ref, x_ref, y_ref, yfixed_ref, rows_ref, *refs):
    col_refs, g_ref, out_refs = refs[:4], refs[4], refs[5 : 5 + near]
    split_ref, turned_ref, peak_ref, sum_ref, acc_ref, image_ref = refs[5 + near :]
    n, sb, piece, width = x_ref.shape
    tb = g_ref.shape[0]
    blk = n * piece
    g = updated(yfixed_ref[2], yfixed_ref[0], merge_lse([ref[...] for ref in col_refs]))
    g_ref[...] = g * (1.0 / UNIT)
    split_columns(g + yfixed_ref[1], split_ref)
    for q in range(tb):
        turned_ref[q] = whole_block(y_ref, q).T
    clear(peak_ref, sum_ref)
    acc_ref[...] = jnp.zeros(acc_ref.shape, jnp.float32)

    def move(group):
        found = []
        for p, q, real in group:
            score, peak = column_scores(y_ref, q, split_ref, tb, q, x_ref, p)
            weights = jnp.exp2((score - peak) * UNIT)
            high = weights.astype(jnp.bfloat16)
            low = (weights - high.astype(jnp.float32)).astype(jnp.bfloat16)
            ys = turned_ref[q]
            moved = jnp.dot(ys, high, preferred_element_type=jnp.float32) + jnp.dot(
                ys, low, preferred_element_type=jnp.float32
            )
            found.append((jnp.where(real, p, sb), peak * UNIT, jnp.sum(weights, axis=0, keepdims=True), moved))
        for p, peak, total, moved in found:
            old = peak_ref[p]
            new = jnp.maximum(old, peak)
            before, here = jnp.exp2(old - new), jnp.exp2(peak - new)
            peak_ref[p] = new
            sum_ref[p] = sum_ref[p] * before + total * here
            acc_ref[p] = acc_ref[p] * before + moved * here

    pairs = pair_list(tb, list_ref)
    rest = lax.rem(pairs[0], MOVE_GROUP)
    large = jnp.where(rest > MOVE_GROUP // 2, pairs[0], pairs[0] - rest)
    visit_pairs(pairs, 0, large, MOVE_GROUP, move)
    visit_pairs(pairs, large, pairs[0], MOVE_GROUP // 2, move)
    rows = []
    for p in range(sb):
        total = jnp.maximum(sum_ref[p], 1.0)
        image_ref[p] = (acc_ref[p] / total).T
        rows.append(peak_ref[p] + jnp.log2(total))
    lse = jnp.concatenate(rows, axis=0)

    me = lax.rem(lax.axis_index("tgt"), near)
    for e, out_ref in enumerate(out_refs):
        for far in range(4):
            owner = far * near + jnp.bitwise_xor(me, e)
            for p in range(sb):
                out_ref[far, p * piece : (p + 1) * piece] = image_ref[p, pl.ds(pl.multiple_of(owner * piece, piece), piece)]
            tile = owner * piece // LANES
            out_ref[far, sb * piece : sb * (piece + 1)] = slots_of(tile, lse)
            out_ref[far, sb * (piece + 1) :] = slots_of(tile, rows_ref[...])


def merge_images(parts, offset, sb, piece, turn_ref):
    whole = merge_lse([lse for _, lse in parts])
    weights = []
    for k, (_, lse) in enumerate(parts):
        turn_ref[k] = jnp.exp2(lse - whole).T
        weights.append(turn_ref[k, pl.ds(offset, piece), :])
    images = []
    for p in range(sb):
        images.append(
            sum(
                image[p * piece : (p + 1) * piece] * weight[:, p : p + 1]
                for (image, _), weight in zip(parts, weights)
            )
        )
    return images, whole


def near_kernel(near, sb, piece, *refs):
    in_refs, out_refs, turn_ref = refs[:near], refs[near : near + 4], refs[near + 4]
    place = lax.axis_index("tgt")
    me, mine = lax.rem(place, near), place // near
    rows = sb * piece
    for d, out_ref in enumerate(out_refs):
        far = jnp.bitwise_xor(mine, d)
        offset = lax.rem((far * near + me) * piece, LANES)
        parts = [(ref[far, :rows], ref[far, rows : rows + sb]) for ref in in_refs]
        images, whole = merge_images(parts, pl.multiple_of(offset, piece), sb, piece, turn_ref)
        for p in range(sb):
            out_ref[p * piece : (p + 1) * piece] = images[p]
        out_ref[rows : rows + sb] = whole
        out_ref[rows + sb :] = merge_lse([ref[far, rows + sb :] for ref in in_refs])


def far_kernel(sb, piece, xfixed_ref, f_in_ref, *refs):
    in_refs, out_ref, f_ref, turn_ref = refs[:4], refs[4], refs[5], refs[6]
    rows = sb * piece
    start = lax.axis_index("tgt") * piece
    offset = lax.rem(start, LANES)
    parts = [(ref[:rows], ref[rows : rows + sb]) for ref in in_refs]
    images, _ = merge_images(parts, pl.multiple_of(offset, piece), sb, piece, turn_ref)
    for p in range(sb):
        out_ref[p] = images[p]
    tile = start // LANES
    lse = merge_lse([ref[rows + sb :] for ref in in_refs])
    f = updated(slots_of(tile, f_in_ref[...]), slots_of(tile, xfixed_ref[0]), lse)
    f_ref[...] = pltpu.roll(f * (1.0 / UNIT), lax.rem(LANES - offset, LANES), 1)[:, :piece]


def pack_kernel(*refs):
    for k, axis in enumerate(("tgt", "src")):
        points_ref, mass_ref, potential_ref = refs[3 * k : 3 * k + 3]
        out_ref = refs[6 + k]
        blocks, piece, width = points_ref.shape
        here = lax.rem(lax.axis_index(axis) * piece, LANES)
        slot = lax.broadcasted_iota(jnp.int32, (piece, LANES), 0)
        lane = lax.broadcasted_iota(jnp.int32, (piece, LANES), 1)
        put = jnp.where(lane == slot + here, 1.0, 0.0).astype(jnp.bfloat16)
        vecs = [jnp.dot(ref[...], put, preferred_element_type=jnp.float32) for ref in (mass_ref, potential_ref)]
        out_ref[: blocks * piece] = points_ref[...].reshape(blocks * piece, width)
        out_ref[blocks * piece :] = jnp.concatenate(vecs, axis=0).astype(jnp.bfloat16)


def on_device(
    src_points, tgt_points, src_mass, tgt_mass, src_potential, tgt_potential, src_counts, tgt_counts, keep
):
    ntgt, nsrc = lax.axis_size("tgt"), lax.axis_size("src")
    near = near_count("tgt")
    sb, src_piece, width = src_points.shape
    tb, tgt_piece, _ = tgt_points.shape
    blk = src_piece * ntgt
    x_rows, y_rows = sb * src_piece, tb * tgt_piece
    x_packed, y_packed = pl.pallas_call(
        pack_kernel,
        out_shape=(
            jax.ShapeDtypeStruct((x_rows + 2 * sb, width), jnp.bfloat16),
            jax.ShapeDtypeStruct((y_rows + 2 * tb, width), jnp.bfloat16),
        ),
        in_specs=[VMEM] * 6,
        out_specs=(VMEM, VMEM),
        name="pack",
    )(src_points, src_mass, src_potential, tgt_points, tgt_mass, tgt_potential)
    (x_in, x_parts), (y_in, y_parts) = gather_points(x_packed, y_packed, y_rows)
    pairs, x_own, y_own = pl.pallas_call(
        list_kernel,
        out_shape=(
            jax.ShapeDtypeStruct((1 + sb * tb + sb + tb,), jnp.int32),
            jax.ShapeDtypeStruct(x_packed.shape, x_packed.dtype),
            jax.ShapeDtypeStruct(y_packed.shape, y_packed.dtype),
        ),
        in_specs=[SMEM] * 3 + [VMEM] * 2,
        out_specs=(SMEM, VMEM, VMEM),
        compiler_params=PARAMS,
        name="kept_pairs",
    )(keep, src_counts, tgt_counts, x_packed, y_packed)
    x_in[0], y_in[0] = x_own, y_own

    def half_room(targets):
        return dict(scratch_shapes=half_scratch(sb, targets, blk), compiler_params=PARAMS)

    shared = shared_rows()
    x, y, xfixed, yfixed, f, part = pl.pallas_call(
        functools.partial(first_kernel, x_parts, y_parts),
        out_shape=(
            jax.ShapeDtypeStruct((ntgt, sb, src_piece, width), jnp.bfloat16),
            jax.ShapeDtypeStruct((nsrc, tb, tgt_piece, width), jnp.bfloat16),
            f32(2, sb, blk),
            f32(3, tb, blk),
            f32(sb, blk),
            f32(sb + tb, blk),
        ),
        in_specs=[SMEM] + [VMEM] * (len(x_in) + len(y_in)),
        out_specs=(VMEM,) * 6,
        scratch_shapes=[
            pltpu.VMEM((2, blk // LANES, sb, LANES), jnp.float32),
            pltpu.VMEM((2, blk // LANES, tb, LANES), jnp.float32),
        ]
        + half_scratch(sb, tb, blk),
        compiler_params=PARAMS,
        name="first_sweep",
    )(pairs, *x_in, *y_in)

    if shared:
        pairs_two, y_two, yfixed_two = [swap(array, "tgt", 1) for array in (pairs, y, yfixed)]
        pairs_two, part = lax.optimization_barrier((pairs_two, part))
        whole = exchange_first(part, sb)
        y, yfixed, mine, part = pl.pallas_call(
            second_kernel,
            out_shape=(
                jax.ShapeDtypeStruct((nsrc, 2 * tb, tgt_piece, width), jnp.bfloat16),
                f32(2, 2 * tb, blk),
                f32(2 * tb, blk),
                f32(2 * tb, blk),
            ),
            in_specs=[SMEM] * 2 + [VMEM] * 8,
            out_specs=(VMEM,) * 4,
            name="second_sweep",
            **half_room(2 * tb),
        )(pairs, pairs_two, x, y, y_two, xfixed, yfixed, yfixed_two, f, whole)
        for k in range(2, ITERS - 1):
            old, whole = swap(mine, "tgt", 1), exchange_shared(part, (k - 1) % 2 ^ 1)
            mine, part = pl.pallas_call(
                functools.partial(shared_kernel, k % 2 ^ 1),
                out_shape=(f32(2 * tb, blk), f32(2 * tb, blk)),
                in_specs=[SMEM] * 2 + [VMEM] * 6,
                out_specs=(VMEM, VMEM),
                name="sweep",
                **half_room(2 * tb),
            )(pairs, pairs_two, x, y, xfixed, yfixed, whole, old)
        row_side = (ITERS - 2) % 2 ^ 1
        old, whole = swap(mine, "tgt", 1), exchange_shared(part, row_side)
        last = (whole, swap(whole, "tgt", 1), mine, old)
    else:
        step = pl.pallas_call(
            step_kernel,
            out_shape=(f32(3, tb, blk), f32(sb, blk), f32(sb + tb, blk)),
            in_specs=[SMEM] + [VMEM] * 6,
            out_specs=(VMEM,) * 3,
            name="sweep",
            **half_room(tb),
        )
        for _ in range(ITERS - 2):
            yfixed, f, part = step(pairs, x, y, xfixed, yfixed, f, exchange_plain(part, sb))
        row_side, last = None, (f, exchange_plain(part, sb))

    yfixed, f, cols = pl.pallas_call(
        functools.partial(last_cols_kernel, row_side),
        out_shape=(f32(3, tb, blk), f32(sb, blk), f32(tb, blk)),
        in_specs=[SMEM] + [VMEM] * (4 + len(last)),
        out_specs=(VMEM,) * 3,
        name="last_cols",
        **half_room(tb),
    )(pairs, x, y, xfixed, yfixed, *last)
    col_parts = exchange_lse(cols, "src")
    rows = pl.pallas_call(
        last_rows_kernel,
        out_shape=f32(sb, blk),
        in_specs=[SMEM] + [VMEM] * 3,
        out_specs=VMEM,
        name="last_rows",
        **half_room(tb),
    )(pairs, x, y, yfixed)
    rows, *col_parts = lax.optimization_barrier((rows, *col_parts))
    tile = sb * (src_piece + 2)
    g, *near_parts = pl.pallas_call(
        functools.partial(project_kernel, near),
        out_shape=(f32(tb, blk),) + (f32(4, tile, width),) * near,
        in_specs=[SMEM] + [VMEM] * 8,
        out_specs=(VMEM,) * (1 + near),
        scratch_shapes=project_scratch(sb, tb, blk, width),
        compiler_params=PARAMS,
        name="project",
    )(pairs, x, y, yfixed, rows, *col_parts)
    if near > 1:
        near_parts = near_parts[:1] + [swap(near_parts[d], "tgt", d) for d in range(1, near)]
    far_parts = pl.pallas_call(
        functools.partial(near_kernel, near, sb, src_piece),
        out_shape=(f32(tile, width),) * 4,
        in_specs=[VMEM] * near,
        out_specs=(VMEM,) * 4,
        scratch_shapes=[pltpu.VMEM((near, LANES, sb), jnp.float32)],
        compiler_params=PARAMS,
        name="merge_near",
    )(*near_parts)
    far_parts = [far_parts[0]] + [swap(far_parts[k], "tgt", near * k) for k in range(1, 4)]
    images, src_final = pl.pallas_call(
        functools.partial(far_kernel, sb, src_piece),
        out_shape=(f32(sb, src_piece, width), f32(sb, src_piece)),
        in_specs=[VMEM] * 6,
        out_specs=(VMEM, VMEM),
        scratch_shapes=[pltpu.VMEM((4, LANES, sb), jnp.float32)],
        compiler_params=PARAMS,
        name="merge_far",
    )(xfixed, f, *far_parts)

    tgt_final = lax.dynamic_slice_in_dim(g, lax.axis_index("src") * tgt_piece, tgt_piece, 1)
    return images, src_final, tgt_final


def solution(mesh):
    return jax.shard_map(
        on_device,
        mesh=mesh,
        in_specs=(
            P("src", "tgt", None),
            P("tgt", "src", None),
            P("src", "tgt"),
            P("tgt", "src"),
            P("src", "tgt"),
            P("tgt", "src"),
            P("src"),
            P("tgt"),
            P("src", "tgt"),
        ),
        out_specs=(P("src", "tgt", None), P("src", "tgt"), P("tgt", "src")),
        check_vma=False,
    )
```

```python
import functools
import math

import jax
import jax.numpy as jnp
from jax import lax
from jax.experimental import pallas as pl
from jax.experimental.pallas import tpu as pltpu
from jax.sharding import PartitionSpec as P

ITERS = 4
EPSILON = 0.1
UNIT = 1.0 / (EPSILON * math.log(2.0))
FLOOR = -1e30
LANES = 128
FAR = (0, 1, 3, 2)
GROUP = 16
MOVE_GROUP = 8

SMEM = pl.BlockSpec(memory_space=pltpu.SMEM)
VMEM = pl.BlockSpec(memory_space=pltpu.VMEM)
PARAMS = pltpu.CompilerParams(vmem_limit_bytes=40 * 1024 * 1024)


def f32(*shape):
    return jax.ShapeDtypeStruct(shape, jnp.float32)


def swap(part, axis, mask):
    return lax.ppermute(part, axis, [(i, i ^ mask) for i in range(lax.axis_size(axis))])


def near_count(axis):
    return lax.axis_size(axis) // 4


def merge_lse(parts):
    top = functools.reduce(jnp.maximum, parts)
    return top + jnp.log2(sum(jnp.exp2(part - top) for part in parts))


def exchange_lse(part, axis):
    near = near_count(axis)
    if near > 1:
        part = merge_lse([part] + [swap(part, axis, d) for d in range(1, near)])
    return [part] + [swap(part, axis, near * k) for k in range(1, 4)]


def shared_rows():
    return near_count("tgt") == 2 and near_count("src") == 1


def is_odd():
    return lax.rem(lax.axis_index("tgt"), 2) == 1


def exchange_plain(part, sb):
    return jnp.concatenate([merge_lse(exchange_lse(part[:sb], "tgt")), merge_lse(exchange_lse(part[sb:], "src"))])


def exchange_first(part, sb):
    other = swap(part, "tgt", 1)
    rows = merge_lse([part[:sb], other[:sb]])
    part = jnp.where(is_odd(), padded(rows, part), jnp.concatenate([part[sb:], other[sb:]]))
    return exchange_shared(part, 1)


def padded(rows, part):
    return jnp.concatenate([rows] * (part.shape[0] // rows.shape[0]))


def exchange_shared(part, row_side):
    ntgt, nsrc = lax.axis_size("tgt"), lax.axis_size("src")

    def swap_far(k):
        pairs = [
            (s * ntgt + t, s * ntgt + (t ^ (2 * k)) if t % 2 == row_side else (s ^ FAR[k]) * ntgt + t)
            for s in range(nsrc)
            for t in range(ntgt)
        ]
        return lax.ppermute(part, ("src", "tgt"), pairs)

    return merge_lse([part] + [swap_far(k) for k in range(1, 4)])


def gather_points(x_piece, y_piece, y_rows):
    nx, ny = near_count("tgt"), near_count("src")
    y_two = swap(y_piece, "src", 2 * ny)
    y_one, y_three = swap(y_piece, "src", ny), swap(y_piece, "src", 3 * ny)
    x_far = [swap(x_piece, "tgt", nx * k) for k in range(1, 4)]
    y_one, y_three, *x_far = lax.optimization_barrier((y_one, y_three, *x_far))
    y_found = [(0, 0, y_piece), (ny, 0, y_one), (2 * ny, 0, y_two), (3 * ny, 0, y_three)]
    x_found = [(0, 0, x_piece)] + [(nx * k, 0, x_far[k - 1]) for k in range(1, 4)]
    return spread_near(x_found, "tgt"), spread_near(y_found, "src")


def spread_near(found, axis):
    near = near_count(axis)
    arrays, parts = [], []
    for d in range(near):
        for mask, first, array in found:
            parts.append((mask ^ d, first, len(arrays), array.shape[0]))
            arrays.append(swap(array, axis, d) if d else array)
    return arrays, parts


def whole_block(ref, k):
    piece = ref[:, k]
    return piece.reshape(piece.shape[0] * piece.shape[1], piece.shape[2])


def split_columns(vec, split_ref):
    blocks, slots = vec.shape
    vec = vec * (1.0 / UNIT)
    parts = []
    for _ in range(3):
        part = vec.astype(jnp.bfloat16).astype(jnp.float32)
        parts.append(part)
        vec = vec - part
    parts.append(jnp.zeros((LANES - 3 * blocks, slots), jnp.float32))
    split_ref[...] = jnp.concatenate(parts, axis=0).T.astype(jnp.bfloat16)


def column_scores(stream_ref, q, split_ref, blocks, k, lane_ref, p):
    lane = lax.broadcasted_iota(jnp.int32, (16, LANES), 1)
    pick = jnp.where((lane < 3 * blocks) & (lax.rem(lane, blocks) == k), 1.0, 0.0).astype(jnp.bfloat16)
    pick = jnp.concatenate([pick] * (split_ref.shape[0] // 16), axis=0)
    score = lax.dot_general(
        jnp.concatenate([whole_block(stream_ref, q), split_ref[...]], axis=1),
        jnp.concatenate([whole_block(lane_ref, p), pick], axis=1),
        (((1,), (1,)), ((), ())),
        preferred_element_type=jnp.float32,
    )
    return score, jnp.max(score, axis=0, keepdims=True)


def column_lse(*operands):
    score, peak = column_scores(*operands)
    return peak * UNIT, jnp.sum(jnp.exp2((score - peak) * UNIT), axis=0, keepdims=True)


def slots_of(tile, vec):
    found = vec[:, :LANES]
    for t in range(1, vec.shape[1] // LANES):
        found = jnp.where(tile == t, vec[:, t * LANES : (t + 1) * LANES], found)
    return found


def clear(peak_ref, sum_ref):
    peak_ref[...] = jnp.full(peak_ref.shape, FLOOR, jnp.float32)
    sum_ref[...] = jnp.zeros(sum_ref.shape, jnp.float32)


def merge_slots(peak, total, count):
    shape = (count, peak.shape[0] // count, peak.shape[1])
    peak = peak.reshape(shape)
    top = jnp.max(peak, axis=1, keepdims=True)
    total = jnp.sum(total.reshape(shape) * jnp.exp2(peak - top), axis=1)
    return top[:, 0] + jnp.log2(jnp.maximum(total, 1.0))


def pair_list(tb, list_ref, other_ref=None):
    own = list_ref[0]
    count = own if other_ref is None else own + other_ref[0]

    def pair(place):
        place = jnp.minimum(place, count - 1)
        if other_ref is None:
            code, shift = list_ref[1 + place], 0
        else:
            mine = place < own
            here, there = list_ref[1 + jnp.where(mine, place, 0)], other_ref[1 + jnp.where(mine, 0, place - own)]
            code = jnp.where(mine, here, there)
            shift = jnp.where(mine, 0, tb)
        return code // tb, lax.rem(code, tb) + shift

    return count, pair


def visit_pairs(pairs, first, last, group, work):
    count, pair = pairs

    @pl.loop(0, pl.cdiv(last - first, group))
    def _(step):
        places = [first + step * group + k for k in range(group)]
        work([pair(place) + (place < count,) for place in places])


def half_sweep(pairs, rows, x_ref, y_ref, tb, vec, scratch):
    split_ref, peak_ref, sum_ref = scratch
    sb = x_ref.shape[1]
    used = sb * tb
    split_columns(vec, split_ref)
    clear(peak_ref, sum_ref)

    def work(group):
        found = []
        for p, q, _ in group:
            if rows:
                found.append((p * tb + q, column_lse(y_ref, q, split_ref, tb, q, x_ref, p)))
            else:
                found.append((q * sb + p, column_lse(x_ref, p, split_ref, sb, p, y_ref, q)))
        for slot, pair in found:
            peak_ref[pl.ds(slot, 1), :], sum_ref[pl.ds(slot, 1), :] = pair

    count = pairs[0]
    rest = lax.rem(count, GROUP)
    large = jnp.where(rest > GROUP // 2, count, count - rest)
    middle = jnp.where(rest > GROUP // 4, count, large)
    visit_pairs(pairs, 0, large, GROUP, work)
    visit_pairs(pairs, large, middle, GROUP // 2, work)
    visit_pairs(pairs, middle, count, GROUP // 4, work)
    return merge_slots(peak_ref[:used], sum_ref[:used], sb if rows else tb)


def half_scratch(sb, tb, blk):
    return [
        pltpu.VMEM((blk, LANES), jnp.bfloat16),
        pltpu.VMEM((sb * tb, blk), jnp.float32),
        pltpu.VMEM((sb * tb, blk), jnp.float32),
    ]


def sweep_own(pairs, x_ref, y_ref, u, h, part_ref, scratch):
    sb, tb = u.shape[0], h.shape[0]
    part_ref[:sb] = half_sweep(pairs, True, x_ref, y_ref, tb, h, scratch)
    part_ref[sb:] = half_sweep(pairs, False, x_ref, y_ref, tb, u, scratch)


def sweep_shared(row_side, pairs, x_ref, y_ref, u, h, part_ref, scratch):
    sb, tb = u.shape[0], h.shape[0]
    odd = is_odd()
    summing_rows = odd if row_side else jnp.logical_not(odd)

    @pl.when(summing_rows)
    def _():
        part_ref[...] = padded(half_sweep(pairs, True, x_ref, y_ref, tb, h, scratch), part_ref)

    @pl.when(jnp.logical_not(summing_rows))
    def _():
        part_ref[...] = half_sweep(pairs, False, x_ref, y_ref, tb, u, scratch)


def project_scratch(sb, tb, blk, width):
    return [
        pltpu.VMEM((blk, LANES), jnp.bfloat16),
        pltpu.VMEM((tb, width, blk), jnp.bfloat16),
        pltpu.VMEM((sb + 1, 1, blk), jnp.float32),
        pltpu.VMEM((sb + 1, 1, blk), jnp.float32),
        pltpu.VMEM((sb + 1, width, blk), jnp.float32),
        pltpu.VMEM((sb, blk, width), jnp.float32),
    ]


def list_kernel(keep_ref, src_counts_ref, tgt_counts_ref, x_in_ref, y_in_ref, list_ref, x_ref, y_ref):
    sb, tb = keep_ref.shape
    x_ref[...] = x_in_ref[...]
    y_ref[...] = y_in_ref[...]
    counts_at = 1 + sb * tb
    n = jnp.int32(0)
    for code in range(sb * tb):
        list_ref[1 + n] = code
        n = n + (keep_ref[code // tb, code % tb] > 0).astype(jnp.int32)
    list_ref[0] = n
    for k in range(sb):
        list_ref[counts_at + k] = src_counts_ref[k]
    for k in range(tb):
        list_ref[counts_at + sb + k] = tgt_counts_ref[k]


def assemble(place, list_ref, counts_at, parts, part_refs, points_ref, vec_ref):
    n, blocks, piece, width = points_ref.shape
    blk = n * piece
    vec_ref[...] = jnp.zeros(vec_ref.shape, jnp.float32)
    for mask, first, k, count in parts:
        owner = jnp.bitwise_xor(place, mask)
        rows = min(count, blocks * piece - first)
        points_ref[owner, first // piece : (first + rows) // piece] = part_refs[k][:rows].reshape(
            rows // piece, piece, width
        )
        if rows < count:
            vecs = part_refs[k][rows:count].astype(jnp.float32)
            tile = owner * piece // LANES
            vec_ref[0, tile] += vecs[:blocks]
            vec_ref[1, tile] += vecs[blocks:]
    mass = jnp.concatenate([vec_ref[0, t] for t in range(blk // LANES)], axis=1)
    potential = jnp.concatenate([vec_ref[1, t] for t in range(blk // LANES)], axis=1) * UNIT
    block_of = lax.broadcasted_iota(jnp.int32, (blocks, blk), 0)
    slot_of = lax.broadcasted_iota(jnp.int32, (blocks, blk), 1)
    half = jnp.zeros((blocks, blk), jnp.float32)
    count = jnp.zeros((blocks, blk), jnp.int32)
    ones = jnp.ones((blocks, width), jnp.bfloat16)
    for k in range(blocks):
        wide = whole_block(points_ref, k).astype(jnp.float32)
        square = wide * wide
        high = square.astype(jnp.bfloat16)
        low = (square - high.astype(jnp.float32)).astype(jnp.bfloat16)
        norm = sum(
            lax.dot_general(ones, part, (((1,), (1,)), ((), ())), preferred_element_type=jnp.float32)
            for part in (high, low)
        )
        half = jnp.where(block_of == k, norm * (0.5 * UNIT), half)
        count = jnp.where(block_of == k, list_ref[counts_at + k], count)
    base = jnp.where(slot_of < count, jnp.log2(mass) - half, FLOOR)
    return potential, half, base


def first_kernel(x_parts, y_parts, list_ref, *refs):
    nx = 1 + max(part[2] for part in x_parts)
    ny = 1 + max(part[2] for part in y_parts)
    x_in, y_in, refs = refs[:nx], refs[nx : nx + ny], refs[nx + ny :]
    x_ref, y_ref, xfixed_ref, yfixed_ref, f_ref, part_ref, xvec_ref, yvec_ref = refs[:8]
    sb, tb = x_ref.shape[1], y_ref.shape[1]
    counts_at = 1 + sb * tb
    f, x_half, x_base = assemble(lax.axis_index("tgt"), list_ref, counts_at, x_parts, x_in, x_ref, xvec_ref)
    g, y_half, y_base = assemble(lax.axis_index("src"), list_ref, counts_at + sb, y_parts, y_in, y_ref, yvec_ref)
    f_ref[...] = f
    xfixed_ref[0], xfixed_ref[1] = x_half, x_base
    yfixed_ref[0], yfixed_ref[1], yfixed_ref[2] = y_half, y_base, g
    sweep_own(pair_list(tb, list_ref), x_ref, y_ref, f + x_base, g + y_base, part_ref, refs[8:])


def updated(old, half, lse):
    return 0.5 * (old + (half - lse))


def turned(cols):
    tb = cols.shape[0] // 2
    return jnp.concatenate([cols[tb:], cols[:tb]])


def second_kernel(list_ref, list2_ref, x_ref, y1_ref, y2_ref, xfixed_ref, yfixed1_ref, yfixed2_ref, f_in_ref, *refs):
    whole_ref, y_ref, yfixed_ref, mine_ref, part_ref = refs[:5]
    sb, tb = x_ref.shape[1], y1_ref.shape[1]
    y_ref[:, :tb] = y1_ref[...]
    y_ref[:, tb:] = y2_ref[...]
    half, base, g = [jnp.concatenate([yfixed1_ref[k], yfixed2_ref[k]]) for k in range(3)]
    yfixed_ref[0], yfixed_ref[1] = half, base
    f = updated(f_in_ref[...], xfixed_ref[0], whole_ref[:sb])
    g = updated(g, half, whole_ref[...])
    mine_ref[...] = jnp.where(is_odd(), padded(f, g), g)
    sweep_shared(
        0, pair_list(tb, list_ref, list2_ref), x_ref, y_ref, f + xfixed_ref[1], g + base, part_ref, refs[5:]
    )


def shared_kernel(row_side, list_ref, list2_ref, x_ref, y_ref, xfixed_ref, yfixed_ref, whole_ref, old_ref, *refs):
    mine_ref, part_ref = refs[:2]
    sb, tb = x_ref.shape[1], y_ref.shape[1] // 2
    f = updated(old_ref[:sb], xfixed_ref[0], whole_ref[:sb])
    g = updated(turned(old_ref[...]), yfixed_ref[0], whole_ref[...])
    mine_ref[...] = jnp.where(is_odd(), g, padded(f, g)) if row_side else jnp.where(is_odd(), padded(f, g), g)
    pairs = pair_list(tb, list_ref, list2_ref)
    sweep_shared(row_side, pairs, x_ref, y_ref, f + xfixed_ref[1], g + yfixed_ref[1], part_ref, refs[2:])


def step_kernel(list_ref, x_ref, y_ref, xfixed_ref, yfixed_in_ref, f_in_ref, whole_ref, *refs):
    yfixed_ref, f_ref, part_ref = refs[:3]
    sb, tb = x_ref.shape[1], y_ref.shape[1]
    f = updated(f_in_ref[...], xfixed_ref[0], whole_ref[:sb])
    half, base, g = [yfixed_in_ref[k] for k in range(3)]
    g = updated(g, half, whole_ref[sb:])
    f_ref[...] = f
    yfixed_ref[0], yfixed_ref[1], yfixed_ref[2] = half, base, g
    sweep_own(pair_list(tb, list_ref), x_ref, y_ref, f + xfixed_ref[1], g + base, part_ref, refs[3:])


def last_cols_kernel(row_side, list_ref, x_ref, y_ref, xfixed_ref, yfixed_in_ref, *refs):
    if row_side is None:
        f_in_ref, whole_ref, yfixed_ref, f_ref, cols_ref = refs[:5]
        scratch = refs[5:]
        sb, tb = x_ref.shape[1], cols_ref.shape[0]
        old_f, old_g = f_in_ref[...], yfixed_in_ref[2]
        rows, cols = whole_ref[:sb], whole_ref[sb:]
    else:
        whole_ref, whole2_ref, mine_ref, mine2_ref, yfixed_ref, f_ref, cols_ref = refs[:7]
        scratch = refs[7:]
        sb, tb = x_ref.shape[1], cols_ref.shape[0]
        has_rows = is_odd() if row_side else jnp.logical_not(is_odd())
        rows = jnp.where(has_rows, whole_ref[:sb], whole2_ref[:sb])
        cols = jnp.where(has_rows, whole2_ref[tb:], whole_ref[:tb])
        old_f = jnp.where(has_rows, mine2_ref[:sb], mine_ref[:sb])
        old_g = jnp.where(has_rows, mine_ref[:tb], mine2_ref[tb:])
    f = updated(old_f, xfixed_ref[0], rows)
    half, base = yfixed_in_ref[0, :tb], yfixed_in_ref[1, :tb]
    f_ref[...] = f
    yfixed_ref[0], yfixed_ref[1], yfixed_ref[2] = half, base, updated(old_g, half, cols)
    cols_ref[...] = half_sweep(pair_list(tb, list_ref), False, x_ref, y_ref, tb, f + xfixed_ref[1], scratch)


def last_rows_kernel(list_ref, x_ref, y_ref, yfixed_ref, rows_ref, *scratch):
    tb = yfixed_ref.shape[1]
    vec = yfixed_ref[2] + yfixed_ref[1]
    rows_ref[...] = half_sweep(pair_list(tb, list_ref), True, x_ref, y_ref, tb, vec, scratch)


def project_kernel(near, list_ref, x_ref, y_ref, yfixed_ref, rows_ref, *refs):
    col_refs, g_ref, out_refs = refs[:4], refs[4], refs[5 : 5 + near]
    split_ref, turned_ref, peak_ref, sum_ref, acc_ref, image_ref = refs[5 + near :]
    n, sb, piece, width = x_ref.shape
    tb = g_ref.shape[0]
    blk = n * piece
    g = updated(yfixed_ref[2], yfixed_ref[0], merge_lse([ref[...] for ref in col_refs]))
    g_ref[...] = g * (1.0 / UNIT)
    split_columns(g + yfixed_ref[1], split_ref)
    for q in range(tb):
        turned_ref[q] = whole_block(y_ref, q).T
    clear(peak_ref, sum_ref)
    acc_ref[...] = jnp.zeros(acc_ref.shape, jnp.float32)

    def move(group):
        found = []
        for p, q, real in group:
            score, peak = column_scores(y_ref, q, split_ref, tb, q, x_ref, p)
            weights = jnp.exp2((score - peak) * UNIT)
            high = weights.astype(jnp.bfloat16)
            low = (weights - high.astype(jnp.float32)).astype(jnp.bfloat16)
            ys = turned_ref[q]
            moved = jnp.dot(ys, high, preferred_element_type=jnp.float32) + jnp.dot(
                ys, low, preferred_element_type=jnp.float32
            )
            found.append((jnp.where(real, p, sb), peak * UNIT, jnp.sum(weights, axis=0, keepdims=True), moved))
        for p, peak, total, moved in found:
            old = peak_ref[p]
            new = jnp.maximum(old, peak)
            before, here = jnp.exp2(old - new), jnp.exp2(peak - new)
            peak_ref[p] = new
            sum_ref[p] = sum_ref[p] * before + total * here
            acc_ref[p] = acc_ref[p] * before + moved * here

    pairs = pair_list(tb, list_ref)
    rest = lax.rem(pairs[0], MOVE_GROUP)
    large = jnp.where(rest > MOVE_GROUP // 2, pairs[0], pairs[0] - rest)
    visit_pairs(pairs, 0, large, MOVE_GROUP, move)
    visit_pairs(pairs, large, pairs[0], MOVE_GROUP // 2, move)
    rows = []
    for p in range(sb):
        total = jnp.maximum(sum_ref[p], 1.0)
        image_ref[p] = (acc_ref[p] / total).T
        rows.append(peak_ref[p] + jnp.log2(total))
    lse = jnp.concatenate(rows, axis=0)

    me = lax.rem(lax.axis_index("tgt"), near)
    for e, out_ref in enumerate(out_refs):
        for far in range(4):
            owner = far * near + jnp.bitwise_xor(me, e)
            for p in range(sb):
                out_ref[far, p * piece : (p + 1) * piece] = image_ref[p, pl.ds(pl.multiple_of(owner * piece, piece), piece)]
            tile = owner * piece // LANES
            out_ref[far, sb * piece : sb * (piece + 1)] = slots_of(tile, lse)
            out_ref[far, sb * (piece + 1) :] = slots_of(tile, rows_ref[...])


def merge_images(parts, offset, sb, piece, turn_ref):
    whole = merge_lse([lse for _, lse in parts])
    weights = []
    for k, (_, lse) in enumerate(parts):
        turn_ref[k] = jnp.exp2(lse - whole).T
        weights.append(turn_ref[k, pl.ds(offset, piece), :])
    images = []
    for p in range(sb):
        images.append(
            sum(
                image[p * piece : (p + 1) * piece] * weight[:, p : p + 1]
                for (image, _), weight in zip(parts, weights)
            )
        )
    return images, whole


def near_kernel(near, sb, piece, *refs):
    in_refs, out_refs, turn_ref = refs[:near], refs[near : near + 4], refs[near + 4]
    place = lax.axis_index("tgt")
    me, mine = lax.rem(place, near), place // near
    rows = sb * piece
    for d, out_ref in enumerate(out_refs):
        far = jnp.bitwise_xor(mine, d)
        offset = lax.rem((far * near + me) * piece, LANES)
        parts = [(ref[far, :rows], ref[far, rows : rows + sb]) for ref in in_refs]
        images, whole = merge_images(parts, pl.multiple_of(offset, piece), sb, piece, turn_ref)
        for p in range(sb):
            out_ref[p * piece : (p + 1) * piece] = images[p]
        out_ref[rows : rows + sb] = whole
        out_ref[rows + sb :] = merge_lse([ref[far, rows + sb :] for ref in in_refs])


def far_kernel(sb, piece, xfixed_ref, f_in_ref, *refs):
    in_refs, out_ref, f_ref, turn_ref = refs[:4], refs[4], refs[5], refs[6]
    rows = sb * piece
    start = lax.axis_index("tgt") * piece
    offset = lax.rem(start, LANES)
    parts = [(ref[:rows], ref[rows : rows + sb]) for ref in in_refs]
    images, _ = merge_images(parts, pl.multiple_of(offset, piece), sb, piece, turn_ref)
    for p in range(sb):
        out_ref[p] = images[p]
    tile = start // LANES
    lse = merge_lse([ref[rows + sb :] for ref in in_refs])
    f = updated(slots_of(tile, f_in_ref[...]), slots_of(tile, xfixed_ref[0]), lse)
    f_ref[...] = pltpu.roll(f * (1.0 / UNIT), lax.rem(LANES - offset, LANES), 1)[:, :piece]


def pack_kernel(*refs):
    for k, axis in enumerate(("tgt", "src")):
        points_ref, mass_ref, potential_ref = refs[3 * k : 3 * k + 3]
        out_ref = refs[6 + k]
        blocks, piece, width = points_ref.shape
        here = lax.rem(lax.axis_index(axis) * piece, LANES)
        slot = lax.broadcasted_iota(jnp.int32, (piece, LANES), 0)
        lane = lax.broadcasted_iota(jnp.int32, (piece, LANES), 1)
        put = jnp.where(lane == slot + here, 1.0, 0.0).astype(jnp.bfloat16)
        vecs = [jnp.dot(ref[...], put, preferred_element_type=jnp.float32) for ref in (mass_ref, potential_ref)]
        out_ref[: blocks * piece] = points_ref[...].reshape(blocks * piece, width)
        out_ref[blocks * piece :] = jnp.concatenate(vecs, axis=0).astype(jnp.bfloat16)


def on_device(
    src_points, tgt_points, src_mass, tgt_mass, src_potential, tgt_potential, src_counts, tgt_counts, keep
):
    ntgt, nsrc = lax.axis_size("tgt"), lax.axis_size("src")
    near = near_count("tgt")
    sb, src_piece, width = src_points.shape
    tb, tgt_piece, _ = tgt_points.shape
    blk = src_piece * ntgt
    x_rows, y_rows = sb * src_piece, tb * tgt_piece
    x_packed, y_packed = pl.pallas_call(
        pack_kernel,
        out_shape=(
            jax.ShapeDtypeStruct((x_rows + 2 * sb, width), jnp.bfloat16),
            jax.ShapeDtypeStruct((y_rows + 2 * tb, width), jnp.bfloat16),
        ),
        in_specs=[VMEM] * 6,
        out_specs=(VMEM, VMEM),
        name="pack",
    )(src_points, src_mass, src_potential, tgt_points, tgt_mass, tgt_potential)
    (x_in, x_parts), (y_in, y_parts) = gather_points(x_packed, y_packed, y_rows)
    pairs, x_own, y_own = pl.pallas_call(
        list_kernel,
        out_shape=(
            jax.ShapeDtypeStruct((1 + sb * tb + sb + tb,), jnp.int32),
            jax.ShapeDtypeStruct(x_packed.shape, x_packed.dtype),
            jax.ShapeDtypeStruct(y_packed.shape, y_packed.dtype),
        ),
        in_specs=[SMEM] * 3 + [VMEM] * 2,
        out_specs=(SMEM, VMEM, VMEM),
        compiler_params=PARAMS,
        name="kept_pairs",
    )(keep, src_counts, tgt_counts, x_packed, y_packed)
    x_in[0], y_in[0] = x_own, y_own

    def half_room(targets):
        return dict(scratch_shapes=half_scratch(sb, targets, blk), compiler_params=PARAMS)

    shared = shared_rows()
    x, y, xfixed, yfixed, f, part = pl.pallas_call(
        functools.partial(first_kernel, x_parts, y_parts),
        out_shape=(
            jax.ShapeDtypeStruct((ntgt, sb, src_piece, width), jnp.bfloat16),
            jax.ShapeDtypeStruct((nsrc, tb, tgt_piece, width), jnp.bfloat16),
            f32(2, sb, blk),
            f32(3, tb, blk),
            f32(sb, blk),
            f32(sb + tb, blk),
        ),
        in_specs=[SMEM] + [VMEM] * (len(x_in) + len(y_in)),
        out_specs=(VMEM,) * 6,
        scratch_shapes=[
            pltpu.VMEM((2, blk // LANES, sb, LANES), jnp.float32),
            pltpu.VMEM((2, blk // LANES, tb, LANES), jnp.float32),
        ]
        + half_scratch(sb, tb, blk),
        compiler_params=PARAMS,
        name="first_sweep",
    )(pairs, *x_in, *y_in)

    if shared:
        pairs_two, y_two, yfixed_two = [swap(array, "tgt", 1) for array in (pairs, y, yfixed)]
        pairs_two, part = lax.optimization_barrier((pairs_two, part))
        whole = exchange_first(part, sb)
        y, yfixed, mine, part = pl.pallas_call(
            second_kernel,
            out_shape=(
                jax.ShapeDtypeStruct((nsrc, 2 * tb, tgt_piece, width), jnp.bfloat16),
                f32(2, 2 * tb, blk),
                f32(2 * tb, blk),
                f32(2 * tb, blk),
            ),
            in_specs=[SMEM] * 2 + [VMEM] * 8,
            out_specs=(VMEM,) * 4,
            name="second_sweep",
            **half_room(2 * tb),
        )(pairs, pairs_two, x, y, y_two, xfixed, yfixed, yfixed_two, f, whole)
        for k in range(2, ITERS - 1):
            old, whole = swap(mine, "tgt", 1), exchange_shared(part, (k - 1) % 2 ^ 1)
            mine, part = pl.pallas_call(
                functools.partial(shared_kernel, k % 2 ^ 1),
                out_shape=(f32(2 * tb, blk), f32(2 * tb, blk)),
                in_specs=[SMEM] * 2 + [VMEM] * 6,
                out_specs=(VMEM, VMEM),
                name="sweep",
                **half_room(2 * tb),
            )(pairs, pairs_two, x, y, xfixed, yfixed, whole, old)
        row_side = (ITERS - 2) % 2 ^ 1
        old, whole = swap(mine, "tgt", 1), exchange_shared(part, row_side)
        last = (whole, swap(whole, "tgt", 1), mine, old)
    else:
        step = pl.pallas_call(
            step_kernel,
            out_shape=(f32(3, tb, blk), f32(sb, blk), f32(sb + tb, blk)),
            in_specs=[SMEM] + [VMEM] * 6,
            out_specs=(VMEM,) * 3,
            name="sweep",
            **half_room(tb),
        )
        for _ in range(ITERS - 2):
            yfixed, f, part = step(pairs, x, y, xfixed, yfixed, f, exchange_plain(part, sb))
        row_side, last = None, (f, exchange_plain(part, sb))

    yfixed, f, cols = pl.pallas_call(
        functools.partial(last_cols_kernel, row_side),
        out_shape=(f32(3, tb, blk), f32(sb, blk), f32(tb, blk)),
        in_specs=[SMEM] + [VMEM] * (4 + len(last)),
        out_specs=(VMEM,) * 3,
        name="last_cols",
        **half_room(tb),
    )(pairs, x, y, xfixed, yfixed, *last)
    col_parts = exchange_lse(cols, "src")
    rows = pl.pallas_call(
        last_rows_kernel,
        out_shape=f32(sb, blk),
        in_specs=[SMEM] + [VMEM] * 3,
        out_specs=VMEM,
        name="last_rows",
        **half_room(tb),
    )(pairs, x, y, yfixed)
    rows, *col_parts = lax.optimization_barrier((rows, *col_parts))
    tile = sb * (src_piece + 2)
    g, *near_parts = pl.pallas_call(
        functools.partial(project_kernel, near),
        out_shape=(f32(tb, blk),) + (f32(4, tile, width),) * near,
        in_specs=[SMEM] + [VMEM] * 8,
        out_specs=(VMEM,) * (1 + near),
        scratch_shapes=project_scratch(sb, tb, blk, width),
        compiler_params=PARAMS,
        name="project",
    )(pairs, x, y, yfixed, rows, *col_parts)
    if near > 1:
        near_parts = near_parts[:1] + [swap(near_parts[d], "tgt", d) for d in range(1, near)]
    far_parts = pl.pallas_call(
        functools.partial(near_kernel, near, sb, src_piece),
        out_shape=(f32(tile, width),) * 4,
        in_specs=[VMEM] * near,
        out_specs=(VMEM,) * 4,
        scratch_shapes=[pltpu.VMEM((near, LANES, sb), jnp.float32)],
        compiler_params=PARAMS,
        name="merge_near",
    )(*near_parts)
    far_parts = [far_parts[0]] + [swap(far_parts[k], "tgt", near * k) for k in range(1, 4)]
    images, src_final = pl.pallas_call(
        functools.partial(far_kernel, sb, src_piece),
        out_shape=(f32(sb, src_piece, width), f32(sb, src_piece)),
        in_specs=[VMEM] * 6,
        out_specs=(VMEM, VMEM),
        scratch_shapes=[pltpu.VMEM((4, LANES, sb), jnp.float32)],
        compiler_params=PARAMS,
        name="merge_far",
    )(xfixed, f, *far_parts)

    tgt_final = lax.dynamic_slice_in_dim(g, lax.axis_index("src") * tgt_piece, tgt_piece, 1)
    return images, src_final, tgt_final


def solution(mesh):
    return jax.shard_map(
        on_device,
        mesh=mesh,
        in_specs=(
            P("src", "tgt", None),
            P("tgt", "src", None),
            P("src", "tgt"),
            P("tgt", "src"),
            P("src", "tgt"),
            P("tgt", "src"),
            P("src"),
            P("tgt"),
            P("src", "tgt"),
        ),
        out_specs=(P("src", "tgt", None), P("src", "tgt"), P("tgt", "src")),
        check_vma=False,
    )
```
